256 devices in a mesh: gx: 8 (over z_lo, x), gy: 4 (over z_hi), gz: 8 (over y, core).
Axes of the slice: x: 4, y: 4, z: 8 (z_hi: 4, z_lo: 2; z = z_hi * 2 + z_lo), core: 2. Of those that a mesh axis runs over, the one named last changes fastest.
Arguments:
- volume: bfloat16 [4, 32, 32, 1024], P(None, 'gx', 'gy', 'gz'), may hold values from -6 to 6
- cotangent: bfloat16 [64, 32, 32, 1024], P(None, 'gx', 'gy', 'gz'), may hold values from -0.015625 to 0.015625
- w1_master: float32 [3456], replicated, may hold values from -0.625 to 0.625
- w1_first: float32 [3456], replicated, may hold values from -6 to 6
- w1_second: float32 [3456], replicated, may hold values from 0.1 to 4
- w2_master: float32 [55296], P(('gx', 'gy', 'gz')), may hold values from -0.21875 to 0.21875
- w2_first: float32 [55296], P(('gx', 'gy', 'gz')), may hold values from -6 to 6
- w2_second: float32 [55296], P(('gx', 'gy', 'gz')), may hold values from 0.1 to 4
Outputs:
- w1_new: float32 [3456], replicated
- w1_first_new: float32 [3456], replicated
- w1_second_new: float32 [3456], replicated
- w2_new: float32 [55296], P(('gx', 'gy', 'gz'))
- w2_first_new: float32 [55296], P(('gx', 'gy', 'gz'))
- w2_second_new: float32 [55296], P(('gx', 'gy', 'gz'))
The draws below stay inside these ranges and needn't reach their ends.
All inputs are finite; a program needn't handle non-finite values.
Results may differ from the reference program's by a relative error of at most 0.00055.
Values may be sent and summed in bfloat16 or wider, within the bound.
No kernel may reach another device: no remote copies, remote signals or barrier semaphores. Data moves between devices by JAX's collectives and lax.ppermute only.
A program may use at most 128 MiB of HBM per device.

```python
import math
import jax
import jax.numpy as jnp
from jax import lax

CI = 4
C1 = 32
C2 = 64
NX = 32
NY = 32
NZ = 1024
WIDE = 55296
NARROW = 3456


def level_of(key, dims, pieces, smallest, high):
    def one(axis_at, shards_of):
        draws = jax.random.uniform(jax.random.fold_in(jax.random.fold_in(key, 6), axis_at), (shards_of,), jnp.float32, smallest / len(pieces), high / len(pieces))
        return jnp.repeat(jnp.exp(draws), dims[axis_at] // shards_of).reshape((-1,) + (1,) * (len(dims) - axis_at - 1))

    loudness = one(*pieces[0])
    for cut in pieces[1:]:
        loudness = loudness * one(*cut)
    return loudness


def bell_draw(own_key, shape, width, most, shards=(), dtype=jnp.bfloat16):
    entries = jax.random.normal(own_key, shape, jnp.float32) * width
    if len(shards) > 0:
        entries = level_of(own_key, shape, shards, -0.22, 0.18) * entries
    return jnp.clip(entries, min=-most, max=most).astype(dtype)


def setup_inputs(seed: int = 0) -> dict:
    splits = jax.random.split(jax.random.key(seed), 9)
    return {
        "volume": bell_draw(splits[0], (CI, NX, NY, NZ), 1.0, 6.0, ((1, 8), (2, 4), (3, 8))),
        "cotangent": bell_draw(splits[1], (C2, NX, NY, NZ), (1.0 / (NX * NY * NZ) ** 0.5), 0.015625, ((1, 8), (2, 4), (3, 8))),
        "w1_master": bell_draw(splits[2], (NARROW,), (27 * CI) ** -0.5, 0.625, (), jnp.float32),
        "w1_first": bell_draw(splits[3], (NARROW,), 1.0, 6.0, (), jnp.float32),
        "w1_second": jnp.clip(jnp.exp(jax.random.uniform(splits[4], (NARROW,), jnp.float32, math.log(0.1), math.log(4.0))), 0.1, 4.0),
        "w2_master": bell_draw(splits[5], (WIDE,), (27 * C1) ** -0.5, 0.21875, ((0, 256),), jnp.float32),
        "w2_first": bell_draw(splits[6], (WIDE,), 1.0, 6.0, ((0, 256),), jnp.float32),
        "w2_second": jnp.clip(jnp.exp(math.log(4.0) - 3.6888794 * jax.random.uniform(splits[7], (WIDE,), jnp.float32) ** level_of(splits[7], (WIDE,), ((0, 256),), -0.2, 0.2)), 0.1, 4.0),
    }


OFFSETS = [(a, b, c) for a in range(3) for b in range(3) for c in range(3)]

def pad_cells(field):
    return jnp.pad(field, ((0, 0), (1, 1), (1, 1), (1, 1)))

def window(padded, a, b, c):
    return padded[:, a:a + NX, b:b + NY, c:c + NZ]

def lamb_bank(master, first, second, grad, blocks):
    first_new = 0.9 * first + 0.1 * grad
    second_new = 0.999 * second + 0.001 * grad * grad
    direction = first_new / (1.0 - 0.9 ** 10) / (jnp.sqrt(second_new / (1.0 - 0.999 ** 10)) + 1e-06) + 0.01 * master
    weight_sq = lax.optimization_barrier(jnp.sum((master * master).reshape(blocks, -1), axis=1))
    update_sq = lax.optimization_barrier(jnp.sum((direction * direction).reshape(blocks, -1), axis=1))
    ratio = jnp.sqrt(weight_sq) / (jnp.sqrt(update_sq) + 1e-06)
    scaled = (ratio[:, None] * direction.reshape(blocks, -1)).reshape(-1)
    return (master - 0.01 * scaled, first_new, second_new)

def reference(volume, cotangent, w1_master, w1_first, w1_second, w2_master, w2_first, w2_second):
    narrow_half = w1_master.astype(jnp.bfloat16).reshape(C1, 27, CI).astype(jnp.float32)
    wide_half = w2_master.astype(jnp.bfloat16).reshape(C2, 27, C1).astype(jnp.float32)
    field_pad = pad_cells(volume.astype(jnp.float32))
    pre_first = jnp.zeros((C1, NX, NY, NZ), jnp.float32)
    for index, (a, b, c) in enumerate(OFFSETS):
        pre_first = pre_first + jnp.einsum('ci,ixyz->cxyz', narrow_half[:, index, :], window(field_pad, a, b, c))
    act_first = jax.nn.silu(pre_first).astype(jnp.bfloat16)
    act_pad = pad_cells(act_first.astype(jnp.float32))
    cot_full = cotangent.astype(jnp.float32)
    cot_pad = pad_cells(cot_full)
    wide_terms = []
    grad_act = jnp.zeros((C1, NX, NY, NZ), jnp.float32)
    for index, (a, b, c) in enumerate(OFFSETS):
        wide_terms.append(jnp.einsum('dxyz,cxyz->dc', cot_full, window(act_pad, a, b, c)))
        grad_act = grad_act + jnp.einsum('dc,dxyz->cxyz', wide_half[:, index, :], window(cot_pad, 2 - a, 2 - b, 2 - c))
    grad_wide = jnp.stack(wide_terms, axis=1).reshape(-1)
    sig = jax.nn.sigmoid(pre_first)
    grad_pre = (grad_act * sig * (1.0 + pre_first * (1.0 - sig))).astype(jnp.bfloat16).astype(jnp.float32)
    narrow_terms = []
    for index, (a, b, c) in enumerate(OFFSETS):
        narrow_terms.append(jnp.einsum('cxyz,ixyz->ci', grad_pre, window(field_pad, a, b, c)))
    grad_narrow = jnp.stack(narrow_terms, axis=1).reshape(-1)
    w1_new, w1_first_new, w1_second_new = lamb_bank(w1_master, w1_first, w1_second, grad_narrow, C1)
    w2_new, w2_first_new, w2_second_new = lamb_bank(w2_master, w2_first, w2_second, grad_wide, C2)
    return (w1_new, w1_first_new, w1_second_new, w2_new, w2_first_new, w2_second_new)
```

```python
import jax
import jax.numpy as jnp
from jax import lax
from jax.experimental import pallas as pl
from jax.experimental.pallas import tpu as pltpu
from jax.sharding import Mesh, PartitionSpec as P

CI = 4
C1 = 32
C2 = 64
F32 = jnp.float32
BF16 = jnp.bfloat16
GX = ("zl", "x")
GY = ("zh",)
GZ = ("y", "core")
VMEM = pl.BlockSpec(memory_space=pltpu.VMEM)
PARAMS = pltpu.CompilerParams(vmem_limit_bytes=32 * 1024 * 1024)


def dot(a, b):
    return lax.dot_general(a, b, (((1,), (0,)), ((), ())), preferred_element_type=F32)


def dot_nt(a, b):
    return lax.dot_general(a, b, (((1,), (1,)), ((), ())), preferred_element_type=F32)


def dot_tn(a, b):
    return lax.dot_general(a, b, (((0,), (0,)), ((), ())), preferred_element_type=F32)


def call(kernel, out_shapes, *args, flops=0):
    return pl.pallas_call(
        kernel,
        out_shape=out_shapes,
        in_specs=[VMEM] * len(args),
        out_specs=jax.tree.map(lambda _: VMEM, out_shapes),
        compiler_params=PARAMS,
    )(*args)


def shape(dims, dtype):
    return jax.ShapeDtypeStruct(dims, dtype)


def y_messages(c_ref, l_ref, r_ref, up_ref, dn_ref):
    slabs = [l_ref] + [c_ref.at[x] for x in range(4)] + [r_ref]
    first, last = [], []
    for xe, slab in enumerate(slabs):
        up_ref[xe * 64 : xe * 64 + 64, :] = slab[448:512, :]
        dn_ref[xe * 64 : xe * 64 + 64, :] = slab[0:64, :]
        vol = slab[512:544, :].astype(F32)
        first.append(vol[0:4])
        last.append(vol[28:32])
    fill = jnp.zeros((8, 128), F32)
    up_ref[384:416, :] = jnp.concatenate(last + [fill], axis=0).astype(BF16)
    dn_ref[384:416, :] = jnp.concatenate(first + [fill], axis=0).astype(BF16)


def assemble(c_ref, l_ref, r_ref, yp_ref, yn_ref, e_ref, ve_ref, up_ref, dn_ref):
    slabs = [l_ref] + [c_ref.at[x] for x in range(4)] + [r_ref]
    before = yp_ref[384:416, :].astype(F32)
    after = yn_ref[384:416, :].astype(F32)
    for xe, slab in enumerate(slabs):
        e_ref[xe, 0:64, :] = yp_ref[xe * 64 : xe * 64 + 64, :]
        e_ref[xe, 64:576, :] = slab[0:512, :]
        e_ref[xe, 576:640, :] = yn_ref[xe * 64 : xe * 64 + 64, :]
        vol = slab[512:544, :].astype(F32)
        ve_ref[xe] = jnp.concatenate(
            [before[xe * 4 : xe * 4 + 4], vol, after[xe * 4 : xe * 4 + 4], jnp.zeros((8, 128), F32)], axis=0
        ).astype(BF16)
    row = lax.broadcasted_iota(jnp.int32, (32, 768), 0)
    lane = lax.broadcasted_iota(jnp.int32, (32, 768), 1)
    pick = (row < 6) & (lane == row * 128 + 127)
    pick = pick | ((row >= 16) & (row < 22) & (lane == (row - 16) * 128))
    pick = pick.astype(F32).astype(BF16)
    cot = jnp.concatenate([e_ref[xe] for xe in range(6)], axis=1)
    vol = jnp.concatenate([ve_ref[xe] for xe in range(6)], axis=1)
    vol = jnp.concatenate([vol, jnp.zeros((80, 768), BF16)], axis=0)
    edge = jnp.concatenate([dot_nt(pick, cot), dot_nt(pick, vol)], axis=1).astype(BF16)
    up_ref[...] = edge[0:16]
    dn_ref[...] = edge[16:32]


def roll(v, by):
    return pltpu.roll(v, by % v.shape[1], 1)


def gradients(e_ref, ve_ref, ml_ref, mr_ref, wt_ref, wb_ref, out_ref, ga_ref):
    lane = lax.broadcasted_iota(jnp.int32, (1, 128), 1)
    low, high = lane == 0, lane == 127
    eye = (
        lax.broadcasted_iota(jnp.int32, (48, 128), 0) == lax.broadcasted_iota(jnp.int32, (48, 128), 1)
    ).astype(F32).astype(BF16)
    left = dot_nt(eye, ml_ref[:, 640:768])
    right = dot_nt(eye, mr_ref[:, 640:768])
    shifted = []
    for xe in range(6):
        v = ve_ref[xe].astype(F32)
        shifted.append(
            (
                jnp.where(low, left[:, xe : xe + 1], roll(v, 1)).astype(BF16),
                ve_ref[xe],
                jnp.where(high, right[:, xe : xe + 1], roll(v, -1)).astype(BF16),
            )
        )
    rest = jnp.zeros((80, 128), BF16)
    patches = jnp.concatenate(
        [
            jnp.concatenate([shifted[x + a][c] for a in range(3) for c in range(3)] + [rest], axis=0)
            for x in range(4)
        ],
        axis=1,
    )
    pre = dot(wb_ref[...], patches)
    sig = 1.0 / (1.0 + jnp.exp(-pre))
    act = (pre * sig).astype(BF16)
    slope = sig * (1.0 + pre * (1.0 - sig))
    halos = []
    for ref in (ml_ref, mr_ref):
        m = ref[:, 0:640].astype(F32)
        halos.append(
            jnp.concatenate(
                [
                    jnp.concatenate([m[a : a + 4, 128 * k : 128 * k + 256] for a in range(3)], axis=1)
                    for k in range(4)
                ],
                axis=0,
            ).astype(BF16)
        )
    none = jnp.zeros((32, 64), BF16)
    blocks = []
    for c in range(3):
        for yl in range(2):
            cells = []
            for a in range(3):
                for yp in range(4):
                    b = yp - yl
                    if 0 <= b <= 2:
                        tap = (2 - a) * 9 + (2 - b) * 3 + (2 - c)
                        cells.append(wt_ref[tap * 32 : tap * 32 + 32, :])
                    else:
                        cells.append(none)
            blocks.append(jnp.concatenate(cells, axis=1))
    bank = jnp.concatenate(blocks, axis=0)
    from_left = dot_nt(bank[0:64], halos[0])
    from_right = dot_nt(bank[128:192], halos[1])
    for k in range(4):
        for xp in range(2):
            cells = jnp.concatenate(
                [
                    jnp.concatenate(
                        [e_ref[2 * xp + j + a, 128 * k : 128 * k + 256, :] for j in range(2)], axis=1
                    )
                    for a in range(3)
                ],
                axis=0,
            )
            v = dot(bank, cells)
            for j in range(2):
                x = 2 * xp + j
                at = slice(128 * j, 128 * j + 128)
                col = 4 * k + x
                ga_ref[64 * k : 64 * k + 64, 128 * x : 128 * x + 128] = (
                    v[64:128, at]
                    + jnp.where(low, from_left[:, col : col + 1], roll(v[0:64, at], 1))
                    + jnp.where(high, from_right[:, col : col + 1], roll(v[128:192, at], -1))
                )
    grad_pre = (ga_ref[...] * slope).astype(BF16)
    product = dot_nt(grad_pre, patches)
    total = product[0:32]
    for y in range(1, 8):
        total = total + roll(product[32 * y : 32 * y + 32], -4 * y)
    row = lax.broadcasted_iota(jnp.int32, (512, 128), 0)
    col = lax.broadcasted_iota(jnp.int32, (512, 128), 1)
    group, inner = row // 48, row % 48
    a, c = group // 3, group % 3
    b, i = inner // 4, inner % 4
    chosen = (b < 3) & (group < 9) & (col == (9 * a + 3 * b + c) * 4 + i)
    narrow = lax.dot_general(
        total,
        chosen.astype(F32),
        (((1,), (0,)), ((), ())),
        precision=lax.Precision.HIGHEST,
        preferred_element_type=F32,
    )
    act32 = act.astype(F32)
    before, after = [], []
    for x in range(4):
        part = act32[:, 128 * x : 128 * x + 128]
        before.append(jnp.where(low, 0.0, roll(part, 1)).astype(BF16))
        after.append(jnp.where(high, 0.0, roll(part, -1)).astype(BF16))
    before = jnp.concatenate(before, axis=1)
    after = jnp.concatenate(after, axis=1)
    empty = jnp.zeros((32, 512), BF16)
    rows = []
    for k in range(4):
        parts = []
        for yl in range(2):
            at = slice(64 * k + 32 * yl, 64 * k + 32 * yl + 32)
            parts += [before[at], act[at], after[at], empty]
        rows.append(jnp.concatenate(parts, axis=0))
    acts = jnp.concatenate(rows, axis=1)
    cots = jnp.concatenate(
        [
            jnp.concatenate(
                [e_ref[x + a, 128 * k : 128 * k + 256, :] for k in range(4) for x in range(4)], axis=1
            )
            for a in range(3)
        ],
        axis=0,
    )
    wide = dot_nt(cots, acts)
    row = lax.broadcasted_iota(jnp.int32, (16, 512), 0)
    lanes = lax.broadcasted_iota(jnp.int32, (16, 512), 1)
    pick = ((row < 4) & (lanes == row * 128)) | ((row >= 4) & (row < 8) & (lanes == (row - 4) * 128 + 127))
    edges = dot_nt(pick.astype(F32).astype(BF16), act)
    gap = jnp.zeros((4, 64), F32)
    one = jnp.zeros((4, 32), F32)
    table = []
    for k in range(4):
        e0 = edges[0:4, 64 * k : 64 * k + 32]
        e1 = edges[0:4, 64 * k + 32 : 64 * k + 64]
        table.append(jnp.concatenate([gap, e0, one, gap, e1, one], axis=1))
    for k in range(4):
        e0 = edges[4:8, 64 * k : 64 * k + 32]
        e1 = edges[4:8, 64 * k + 32 : 64 * k + 64]
        table.append(jnp.concatenate([e0, one, gap, e1, one, gap], axis=1))
    table = jnp.concatenate(table, axis=0).astype(BF16)
    wide = wide + dot_tn(jnp.concatenate(halos, axis=0), table)
    taps = []
    for a in range(3):
        for b in range(3):
            at = (2 - a) * 256 + (2 - b) * 64
            taps.append((wide[at : at + 64, 0:128] + wide[at + 64 : at + 128, 128:256])[:, 0:96])
    wide = jnp.concatenate(taps + [jnp.zeros((64, 32), F32)], axis=1)
    for p in range(8):
        out_ref[p, :, 0:896] = wide[8 * p : 8 * p + 8]
        for j in range(4):
            out_ref[p, :, 896 + 128 * j : 1024 + 128 * j] = narrow[8 * j : 8 * j + 8]


def second_stage(in_ref, out_ref):
    total = in_ref[0]
    for p in range(1, 8):
        total = total + in_ref[p]
    narrow = total[:, 896:1408]
    for owner in range(8):
        x, yh = owner // 2, owner % 2
        block = jnp.concatenate(
            [total[owner : owner + 1, 128 * j : 128 * j + 128] for j in range(7)] + [jnp.zeros((1, 128), F32)],
            axis=0,
        )
        both = jnp.concatenate([narrow, block], axis=1)
        for q in range(4):
            out_ref[x * 8 + yh * 4 + q] = both


def moments(master, first, second, grad):
    first_new = 0.9 * first + 0.1 * grad
    second_new = 0.999 * second + 0.001 * grad * grad
    direction = (
        first_new / (1.0 - 0.9**10) / (jnp.sqrt(second_new / (1.0 - 0.999**10)) + 1e-06)
        + 0.01 * master
    )
    return (first_new, second_new, direction)


def update(in_ref, wide_ref, narrow_ref, wide_out, narrow_out):
    total = in_ref[0]
    for p in range(1, 32):
        total = total + in_ref[p]
    inside = (
        lax.broadcasted_iota(jnp.int32, (8, 128), 0) * 128 + lax.broadcasted_iota(jnp.int32, (8, 128), 1)
    ) < 864
    master, first, second = wide_ref[0], wide_ref[1], wide_ref[2]
    first_new, second_new, direction = moments(master, first, second, total[:, 512:640])
    direction = jnp.where(inside, direction, 0.0)
    ratio = jnp.sqrt(jnp.sum(master * master, keepdims=True)) / (
        jnp.sqrt(jnp.sum(direction * direction, keepdims=True)) + 1e-06
    )
    wide_out[0] = master - 0.01 * (ratio * direction)
    wide_out[1] = first_new
    wide_out[2] = second_new
    grad = jnp.concatenate([total[:, 128 * j : 128 * j + 128] for j in range(4)], axis=0)
    master, first, second = narrow_ref[0], narrow_ref[1], narrow_ref[2]
    first_new, second_new, direction = moments(master, first, second, grad)
    direction = jnp.where(lax.broadcasted_iota(jnp.int32, (32, 128), 1) < 108, direction, 0.0)
    ratio = jnp.sqrt(jnp.sum(master * master, axis=1, keepdims=True)) / (
        jnp.sqrt(jnp.sum(direction * direction, axis=1, keepdims=True)) + 1e-06
    )
    narrow_out[0] = master - 0.01 * (ratio * direction)
    narrow_out[1] = first_new
    narrow_out[2] = second_new


def exchange(up, down, axes):
    size = lax.axis_size(axes)
    pairs = [(i, i + 1) for i in range(size - 1)]
    before = lax.ppermute(up, axes, pairs)
    after = lax.ppermute(down, axes, [(j, i) for i, j in pairs])
    return before, after


def spread(value, axes):
    size = lax.axis_size(axes)
    return lax.all_to_all(
        jnp.broadcast_to(value[None], (size,) + value.shape), axes, 0, 0, tiled=True
    )


def local(volume, cotangent, w1_master, w1_first, w1_second, w2_master, w2_first, w2_second):
    cot = cotangent.reshape(2, 4, 4, 2, 4, 8, 128).transpose(4, 5, 0, 2, 1, 3, 6).reshape(4, 512, 128)
    vol = volume.transpose(1, 2, 0, 3).reshape(4, 32, 128)
    slabs = jnp.concatenate([cot, vol], axis=1)
    before_x, after_x = exchange(slabs[3], slabs[0], GX)
    owned = jnp.stack([w2_master, w2_first, w2_second])
    near = spread(owned, GZ)
    bank = spread(near[:, 0].astype(BF16), GX + GY).reshape(2, 4, 4, 2, 864)
    bank = bank.transpose(4, 0, 2, 1, 3).reshape(864, 64)
    half = lax.axis_index("y") // 2
    block = lax.dynamic_slice_in_dim(near, half * 4, 4, axis=0).transpose(1, 0, 2).reshape(3, 864)
    block = jnp.pad(block, ((0, 0), (0, 160))).reshape(3, 8, 128)
    narrow_half = w1_master.astype(BF16).reshape(C1, 3, 3, 3, CI)
    band = (
        jnp.arange(12)[None, None, :] == jnp.arange(8)[:, None, None] + jnp.arange(3)[None, :, None]
    ).astype(BF16)
    narrow_band = jnp.einsum("cabsi,ybe->ycasei", narrow_half, band).reshape(256, 432)
    narrow_band = jnp.pad(narrow_band, ((0, 0), (0, 80)))
    narrow = jnp.pad(
        jnp.stack([w1_master, w1_first, w1_second]).reshape(3, C1, 108), ((0, 0), (0, 0), (0, 20))
    )
    up, down = call(
        y_messages, (shape((416, 128), BF16), shape((416, 128), BF16)), slabs, before_x, after_x
    )
    before_y, after_y = exchange(up, down, GY)
    cells, fields, up, down = call(
        assemble,
        (
            shape((6, 640, 128), BF16),
            shape((6, 48, 128), BF16),
            shape((16, 768), BF16),
            shape((16, 768), BF16),
        ),
        slabs,
        before_x,
        after_x,
        before_y,
        after_y,
    )
    before_z, after_z = exchange(up, down, GZ)
    sums = pl.pallas_call(
        gradients,
        out_shape=shape((8, 8, 1408), F32),
        in_specs=[VMEM] * 6,
        out_specs=VMEM,
        scratch_shapes=[pltpu.VMEM((256, 512), F32)],
        compiler_params=PARAMS,
    )(cells, fields, before_z, after_z, bank, narrow_band)
    sums = lax.all_to_all(sums, ("zl", "zh"), 0, 0, tiled=True)
    sums = call(second_stage, shape((32, 8, 640), F32), sums)
    sums = lax.all_to_all(sums, ("x", "y", "core"), 0, 0, tiled=True)
    wide_new, narrow_new = call(
        update, (shape((3, 8, 128), F32), shape((3, 32, 128), F32)), sums, block, narrow
    )
    quarter = (lax.axis_index("y") % 2) * 2 + lax.axis_index("core")
    wide_new = lax.dynamic_slice_in_dim(wide_new.reshape(3, 1024), quarter * 216, 216, axis=1)
    narrow_new = narrow_new[:, :, :108].reshape(3, 3456)
    return (
        narrow_new[0],
        narrow_new[1],
        narrow_new[2],
        wide_new[0],
        wide_new[1],
        wide_new[2],
    )


def solution(mesh):
    parts = Mesh(mesh.devices.reshape(2, 4, 4, 4, 2), GX + GY + GZ)
    field = P(None, GX, GY, GZ)
    owned = P(GX + GY + GZ)
    return jax.shard_map(
        local,
        mesh=parts,
        in_specs=(field, field, P(), P(), P(), owned, owned, owned),
        out_specs=(P(), P(), P(), owned, owned, owned),
        check_vma=False,
    )
```

```python
import jax
import jax.numpy as jnp
from jax import lax
from jax.experimental import pallas as pl
from jax.experimental.pallas import tpu as pltpu
from jax.sharding import Mesh, PartitionSpec as P

CI = 4
C1 = 32
C2 = 64
F32 = jnp.float32
BF16 = jnp.bfloat16
GX = ("zl", "x")
GY = ("zh",)
GZ = ("y", "core")
VMEM = pl.BlockSpec(memory_space=pltpu.VMEM)
PARAMS = pltpu.CompilerParams(vmem_limit_bytes=32 * 1024 * 1024)


def dot(a, b):
    return lax.dot_general(a, b, (((1,), (0,)), ((), ())), preferred_element_type=F32)


def dot_nt(a, b):
    return lax.dot_general(a, b, (((1,), (1,)), ((), ())), preferred_element_type=F32)


def dot_tn(a, b):
    return lax.dot_general(a, b, (((0,), (0,)), ((), ())), preferred_element_type=F32)


def call(kernel, out_shapes, *args, scratch=(), space=VMEM):
    return pl.pallas_call(
        kernel,
        out_shape=out_shapes,
        in_specs=[space] * len(args),
        out_specs=jax.tree.map(lambda _: VMEM, out_shapes),
        scratch_shapes=scratch,
        compiler_params=PARAMS,
    )(*args)


def shape(dims, dtype):
    return jax.ShapeDtypeStruct(dims, dtype)


def roll(v, by):
    return pltpu.roll(v, by % v.shape[1], 1)


def lanes():
    return lax.broadcasted_iota(jnp.int32, (1, 128), 1)


def within(v, low, high):
    return jnp.where((lanes() >= low) & (lanes() < high), v, 0.0)


def two_rows(v):
    return [v[:, 0:128], jnp.concatenate([v[:, 128:216], jnp.zeros((1, 40), F32)], axis=1)]


def place(two, q):
    lane = lax.broadcasted_iota(jnp.int32, (1, 128), 1)
    row, at = divmod(216 * q, 128)
    one, last = roll(two[0:1], at), roll(jnp.where(lane < 88, two[1:2], 0.0), at)
    gap = jnp.zeros((1, 128), F32)
    pieces = [gap] * row + [
        jnp.where(lane >= at, one, 0.0),
        jnp.where(lane < at, one, 0.0) + jnp.where(lane >= at, last, 0.0),
        jnp.where(lane < at, last, 0.0),
    ]
    return jnp.concatenate((pieces + [gap] * 8)[:8], axis=0)


def take(block, q):
    lane = lax.broadcasted_iota(jnp.int32, (1, 128), 1)
    row, at = divmod(216 * q, 128)
    moved = [roll(block[r : r + 1], -at) for r in range(row, min(row + 3, 8))]
    one = jnp.where(lane < 128 - at, moved[0], moved[1])
    two = jnp.where(lane < 128 - at, moved[1], moved[2]) if len(moved) > 2 else moved[1]
    return jnp.concatenate([one, two], axis=0)


def along_gz():
    return lax.axis_index("y") * 2 + lax.axis_index("core")


def pack(
    cot_hbm, vol_hbm, w2_hbm, f2_hbm, s2_hbm, slab_ref, up_ref, dn_ref, out_ref, own_ref,
    cot_ref, vol_ref, w2_ref, f2_ref, s2_ref, cot32, vol32, sems,
):
    copies = [
        pltpu.make_async_copy(source, target, sems.at[i])
        for i, (source, target) in enumerate(
            ((cot_hbm, cot_ref), (vol_hbm, vol_ref), (w2_hbm, w2_ref), (f2_hbm, f2_ref), (s2_hbm, s2_ref))
        )
    ]
    for copy in copies:
        copy.start()
    for copy in copies:
        copy.wait()
    cot32[...] = cot_ref[...].astype(F32)
    vol32[...] = vol_ref[...].astype(F32)
    for x in range(4):
        for y in range(8):
            slab_ref[x, 64 * y : 64 * y + 64, :] = cot32[pl.ds(8 * x + y, 64, stride=32), :].astype(BF16)
        slab_ref[x, 512:544, :] = jnp.concatenate(
            [vol32[pl.ds(8 * x + y, 4, stride=32), :] for y in range(8)], axis=0
        ).astype(BF16)
    up_ref[...] = slab_ref[3]
    dn_ref[...] = slab_ref[0]
    row = lax.broadcasted_iota(jnp.int32, (16, 512), 0)
    lane = lax.broadcasted_iota(jnp.int32, (16, 512), 1)
    pick = ((row < 4) & (lane == row * 128)) | ((row >= 4) & (row < 8) & (lane == row * 128 - 385))
    cells = jnp.concatenate([slab_ref[x] for x in range(4)], axis=1)
    cells = jnp.concatenate([cells, jnp.zeros((96, 512), BF16)], axis=0)
    edge = dot_nt(pick.astype(F32).astype(BF16), cells)
    own = [row for ref in (w2_ref, f2_ref, s2_ref) for row in two_rows(ref[...])]
    own_ref[...] = jnp.concatenate(own + [jnp.zeros((2, 128), F32)], axis=0)
    ends = []
    for side in range(2):
        at = slice(4 * side, 4 * side + 4)
        tail = edge[at, 512:640]
        tail = [sum(roll(tail[x : x + 1], 32 * x) for x in range(4))] + own[0:2] + [jnp.zeros((5, 128), F32)]
        ends.append(jnp.concatenate([edge[at, 128 * j : 128 * j + 128] for j in range(4)] + tail, axis=0))
    me = along_gz()
    for p in range(8):
        message = jnp.where(me < p, ends[1], ends[0]).astype(BF16)
        for x in range(8):
            out_ref[8 * x + p] = message


def y_messages(slab_ref, l_ref, r_ref, in_ref, up_ref, dn_ref, bank_ref, beyond_ref):
    slabs = [l_ref] + [slab_ref.at[x] for x in range(4)] + [r_ref]
    first, last = [], []
    for xe, slab in enumerate(slabs):
        up_ref[xe * 64 : xe * 64 + 64, :] = slab[448:512, :]
        dn_ref[xe * 64 : xe * 64 + 64, :] = slab[0:64, :]
        vol = slab[512:544, :].astype(F32)
        first.append(vol[0:4])
        last.append(vol[28:32])
    fill = [jnp.zeros((8, 128), F32)]
    four = [jnp.zeros((4, 128), F32)]
    across, along = lax.axis_index("zl") * 4 + lax.axis_index("x"), along_gz()
    rows_up, rows_dn = [], []
    for side in range(2):
        other = along + 2 * side - 1
        inside = (other >= 0) & (other <= 7)
        other = jnp.clip(other, 0, 7)
        mid = jnp.where(inside, in_ref[8 * across + other].astype(F32), 0.0)
        before = in_ref[8 * jnp.maximum(across - 1, 0) + other].astype(F32)
        before = jnp.where(inside & (across > 0), before, 0.0)
        after = in_ref[8 * jnp.minimum(across + 1, 7) + other].astype(F32)
        after = jnp.where(inside & (across < 7), after, 0.0)
        parts = [
            jnp.concatenate(
                [before[4 * j + 3 : 4 * j + 4], mid[4 * j : 4 * j + 4], after[4 * j : 4 * j + 1]], axis=0
            )
            for j in range(4)
        ]
        tail = [before[16:17]] + [mid[16:17]] * 4 + [after[16:17]]
        tail = [roll(row, -32 * x) for row, x in zip(tail, (3, 0, 1, 2, 3, 0), strict=True)]
        parts.append(within(jnp.concatenate(tail, axis=0), 0, 32))
        for j in range(5):
            beyond_ref[8 * side : 8 * side + 8, 128 * j : 128 * j + 128] = jnp.concatenate(
                [parts[j], jnp.zeros((2, 128), F32)], axis=0
            )
        rows_up.append(within(roll(parts[3], -64), 0, 64) + within(roll(parts[4], 36), 64, 68))
        rows_dn.append(within(parts[0], 0, 64) + within(roll(parts[4], 64), 64, 68))
    up_ref[384:432, :] = jnp.concatenate(last + fill + rows_up + four, axis=0).astype(BF16)
    dn_ref[384:432, :] = jnp.concatenate(first + fill + rows_dn + four, axis=0).astype(BF16)
    bank = jnp.concatenate([in_ref[p, 16:24, :].astype(F32)[1:3] for p in range(64)], axis=0).astype(BF16)
    up_ref[432:560, :] = bank
    dn_ref[432:560, :] = bank
    bank_ref[...] = bank


def assemble(slab_ref, l_ref, r_ref, beyond_ref, yp_ref, yn_ref, e_ref, ve_ref):
    slabs = [l_ref] + [slab_ref.at[x] for x in range(4)] + [r_ref]
    along_y = lax.axis_index("zh")
    some, more = along_y > 0, along_y < 3
    before = jnp.where(some, yp_ref[384:432, :].astype(F32), 0.0)
    after = jnp.where(more, yn_ref[384:432, :].astype(F32), 0.0)
    for xe, slab in enumerate(slabs):
        e_ref[xe, 0:64, :] = jnp.where(some, yp_ref[xe * 64 : xe * 64 + 64, :].astype(F32), 0.0).astype(BF16)
        e_ref[xe, 64:576, :] = slab[0:512, :]
        e_ref[xe, 576:640, :] = jnp.where(more, yn_ref[xe * 64 : xe * 64 + 64, :].astype(F32), 0.0).astype(BF16)
        vol = slab[512:544, :].astype(F32)
        ve_ref[xe] = jnp.concatenate(
            [before[xe * 4 : xe * 4 + 4], vol, after[xe * 4 : xe * 4 + 4], jnp.zeros((8, 128), F32)], axis=0
        ).astype(BF16)
    ends = []
    for side in range(2):
        parts = [roll(beyond_ref[8 * side : 8 * side + 6, 128 * j : 128 * j + 128], 64) for j in range(5)]
        prev = before[32 + 6 * side : 38 + 6 * side]
        nxt = after[32 + 6 * side : 38 + 6 * side]
        tiles = [within(prev, 0, 64) + within(parts[0], 64, 128)]
        for k in range(1, 4):
            tiles.append(jnp.where(lanes() < 64, parts[k - 1], parts[k]))
        tiles.append(within(parts[3], 0, 64) + within(roll(nxt, 64), 64, 128))
        tiles.append(
            within(roll(prev, -64), 0, 4) + within(roll(parts[4], -60), 4, 36) + within(roll(nxt, -28), 36, 40)
        )
        ends.append(
            jnp.concatenate([jnp.concatenate(tiles, axis=1), jnp.zeros((10, 768), F32)], axis=0).astype(BF16)
        )
    return ends


def flatten(narrow):
    lane = lax.broadcasted_iota(jnp.int32, (1, 128), 1)
    rows = [jnp.zeros((1, 128), F32) for _ in range(33)]
    for c in range(32):
        row, at = divmod(108 * c, 128)
        moved = roll(jnp.where(lane < 108, narrow[c : c + 1], 0.0), at)
        if at + 108 <= 128:
            rows[row] = rows[row] + moved
        else:
            rows[row] = rows[row] + jnp.where(lane >= at, moved, 0.0)
            rows[row + 1] = rows[row + 1] + jnp.where(lane < at, moved, 0.0)
    return jnp.concatenate(rows[:32], axis=0)


def turned(yp_ref, yn_ref, own_ref, far_ref, rows_ref):
    me = lax.axis_index("zh")
    for by, ref, first in ((0, own_ref, 0), (3, yp_ref, 432), (1, yn_ref, 432), (2, far_ref, 0)):
        zh = (me + by) % 4
        for across in range(8):
            at = pl.multiple_of(64 * across + 16 * zh, 16)
            rows_ref[pl.ds(at, 16), :] = ref[first + 16 * across : first + 16 * across + 16, :].astype(F32)
    parts = []
    for q in range(4):
        parts.append(rows_ref[pl.ds(2 * q, 64, stride=8), :].T)
        parts.append(rows_ref[pl.ds(2 * q + 1, 64, stride=8), :].T[0:88])
    return jnp.concatenate(parts, axis=0).astype(BF16)


def narrow_lanes():
    row = lax.broadcasted_iota(jnp.int32, (512, 128), 0)
    col = lax.broadcasted_iota(jnp.int32, (512, 128), 1)
    group, inner = row // 48, row % 48
    a, c = group // 3, group % 3
    b, i = inner // 4, inner % 4
    return ((b < 3) & (group < 9) & (col == (9 * a + 3 * b + c) * 4 + i)).astype(F32)


def narrow_rows(w1_ref, out_ref):
    lane = lax.broadcasted_iota(jnp.int32, (1, 128), 1)
    rows = []
    for c in range(32):
        row, at = divmod(108 * c, 128)
        piece = roll(w1_ref[row : row + 1, :], -at)
        if at > 20:
            piece = jnp.where(lane < 128 - at, piece, roll(w1_ref[row + 1 : row + 2, :], -at))
        rows.append(jnp.where(lane < 108, piece, 0.0))
    bank = jnp.concatenate(rows, axis=0).astype(BF16)
    first = dot_nt(bank, narrow_lanes().astype(BF16))
    for y in range(8):
        out_ref[32 * y : 32 * y + 32, :] = roll(first, 4 * y).astype(BF16)


def gradients(
    slab_ref, l_ref, r_ref, beyond_ref, yp_ref, yn_ref, bank_ref, far_ref, wb_ref, out_ref, e_ref, ve_ref, ga_ref, rows_ref
):
    ends = assemble(slab_ref, l_ref, r_ref, beyond_ref, yp_ref, yn_ref, e_ref, ve_ref)
    lane = lax.broadcasted_iota(jnp.int32, (1, 128), 1)
    low, high = lane == 0, lane == 127
    eye = (
        lax.broadcasted_iota(jnp.int32, (48, 128), 0) == lax.broadcasted_iota(jnp.int32, (48, 128), 1)
    ).astype(F32).astype(BF16)
    left = dot_nt(eye, ends[0][:, 640:768])
    right = dot_nt(eye, ends[1][:, 640:768])
    shifted = []
    for xe in range(6):
        v = ve_ref[xe].astype(F32)
        shifted.append(
            (
                jnp.where(low, left[:, xe : xe + 1], roll(v, 1)).astype(BF16),
                ve_ref[xe],
                jnp.where(high, right[:, xe : xe + 1], roll(v, -1)).astype(BF16),
            )
        )
    rest = jnp.zeros((80, 128), BF16)
    patches = jnp.concatenate(
        [
            jnp.concatenate([shifted[x + a][c] for a in range(3) for c in range(3)] + [rest], axis=0)
            for x in range(4)
        ],
        axis=1,
    )
    pre = dot(wb_ref[...], patches)
    sig = 1.0 / (1.0 + jnp.exp(-pre))
    act = (pre * sig).astype(BF16)
    slope = sig * (1.0 + pre * (1.0 - sig))
    halos = []
    for end in ends:
        m = end[:, 0:640].astype(F32)
        halos.append(
            jnp.concatenate(
                [
                    jnp.concatenate([m[a : a + 4, 128 * k : 128 * k + 256] for a in range(3)], axis=1)
                    for k in range(4)
                ],
                axis=0,
            ).astype(BF16)
        )
    none = jnp.zeros((32, 64), BF16)
    weights = turned(yp_ref, yn_ref, bank_ref, far_ref, rows_ref)
    blocks = []
    for c in range(3):
        for yl in range(2):
            cells = []
            for a in range(3):
                for yp in range(4):
                    b = yp - yl
                    if 0 <= b <= 2:
                        tap = (2 - a) * 9 + (2 - b) * 3 + (2 - c)
                        cells.append(weights[tap * 32 : tap * 32 + 32])
                    else:
                        cells.append(none)
            blocks.append(jnp.concatenate(cells, axis=1))
    bank = jnp.concatenate(blocks, axis=0)
    from_left = dot_nt(bank[0:64], halos[0])
    from_right = dot_nt(bank[128:192], halos[1])
    for k in range(4):
        for xp in range(2):
            cells = jnp.concatenate(
                [
                    jnp.concatenate(
                        [e_ref[2 * xp + j + a, 128 * k : 128 * k + 256, :] for j in range(2)], axis=1
                    )
                    for a in range(3)
                ],
                axis=0,
            )
            v = dot(bank, cells)
            for j in range(2):
                x = 2 * xp + j
                at = slice(128 * j, 128 * j + 128)
                col = 4 * k + x
                ga_ref[64 * k : 64 * k + 64, 128 * x : 128 * x + 128] = (
                    v[64:128, at]
                    + jnp.where(low, from_left[:, col : col + 1], roll(v[0:64, at], 1))
                    + jnp.where(high, from_right[:, col : col + 1], roll(v[128:192, at], -1))
                )
    grad_pre = (ga_ref[...] * slope).astype(BF16)
    product = dot_nt(grad_pre, patches)
    total = product[0:32]
    for y in range(1, 8):
        total = total + roll(product[32 * y : 32 * y + 32], -4 * y)
    chosen = narrow_lanes()
    narrow = lax.dot_general(
        total,
        chosen,
        (((1,), (0,)), ((), ())),
        precision=lax.Precision.HIGHEST,
        preferred_element_type=F32,
    )
    act32 = act.astype(F32)
    before, after = [], []
    for x in range(4):
        part = act32[:, 128 * x : 128 * x + 128]
        before.append(jnp.where(low, 0.0, roll(part, 1)).astype(BF16))
        after.append(jnp.where(high, 0.0, roll(part, -1)).astype(BF16))
    before = jnp.concatenate(before, axis=1)
    after = jnp.concatenate(after, axis=1)
    empty = jnp.zeros((32, 512), BF16)
    rows = []
    for k in range(4):
        parts = []
        for yl in range(2):
            at = slice(64 * k + 32 * yl, 64 * k + 32 * yl + 32)
            parts += [before[at], act[at], after[at], empty]
        rows.append(jnp.concatenate(parts, axis=0))
    acts = jnp.concatenate(rows, axis=1)
    cots = jnp.concatenate(
        [
            jnp.concatenate(
                [e_ref[x + a, 128 * k : 128 * k + 256, :] for k in range(4) for x in range(4)], axis=1
            )
            for a in range(3)
        ],
        axis=0,
    )
    wide = dot_nt(cots, acts)
    row = lax.broadcasted_iota(jnp.int32, (16, 512), 0)
    lanes = lax.broadcasted_iota(jnp.int32, (16, 512), 1)
    pick = ((row < 4) & (lanes == row * 128)) | ((row >= 4) & (row < 8) & (lanes == (row - 4) * 128 + 127))
    edges = dot_nt(pick.astype(F32).astype(BF16), act)
    gap = jnp.zeros((4, 64), F32)
    one = jnp.zeros((4, 32), F32)
    table = []
    for k in range(4):
        e0 = edges[0:4, 64 * k : 64 * k + 32]
        e1 = edges[0:4, 64 * k + 32 : 64 * k + 64]
        table.append(jnp.concatenate([gap, e0, one, gap, e1, one], axis=1))
    for k in range(4):
        e0 = edges[4:8, 64 * k : 64 * k + 32]
        e1 = edges[4:8, 64 * k + 32 : 64 * k + 64]
        table.append(jnp.concatenate([e0, one, gap, e1, one, gap], axis=1))
    table = jnp.concatenate(table, axis=0).astype(BF16)
    wide = wide + dot_tn(jnp.concatenate(halos, axis=0), table)
    taps = []
    for a in range(3):
        for b in range(3):
            at = (2 - a) * 256 + (2 - b) * 64
            taps.append((wide[at : at + 64, 0:128] + wide[at + 64 : at + 128, 128:256])[:, 0:96])
    wide = jnp.concatenate(taps + [jnp.zeros((64, 32), F32)], axis=1)
    flat = flatten(narrow)
    for p in range(8):
        out_ref[p, :, 0:896] = wide[8 * p : 8 * p + 8]
        for j in range(4):
            out_ref[p, :, 896 + 128 * j : 1024 + 128 * j] = flat[8 * j : 8 * j + 8]


def second_stage(in_ref, out_ref):
    total = in_ref[0]
    for p in range(1, 8):
        total = total + in_ref[p]
    gap = jnp.zeros((1, 128), F32)
    for zh in range(4):
        out_ref[zh, :, 0:512] = total[:, 896:1408]
        for yh in range(2):
            row = 2 * zh + yh
            pieces = [total[row : row + 1, 128 * j : 128 * j + 128] for j in range(7)]
            out_ref[zh, :, 512 + 128 * yh : 640 + 128 * yh] = jnp.concatenate(pieces + [gap], axis=0)


def third_stage(in_ref, own_ref, out_ref):
    total = in_ref[0]
    for p in range(1, 4):
        total = total + in_ref[p]
    for p in range(8):
        yh = p // 4
        out_ref[p, :, 0:512] = total[:, 0:512]
        out_ref[p, :, 512:640] = total[:, 512 + 128 * yh : 640 + 128 * yh]
        out_ref[p, :, 640:768] = own_ref[...]


def moments(master, first, second, grad):
    first_new = 0.9 * first + 0.1 * grad
    second_new = 0.999 * second + 0.001 * grad * grad
    direction = (
        first_new / (1.0 - 0.9**10) / (jnp.sqrt(second_new / (1.0 - 0.999**10)) + 1e-06)
        + 0.01 * master
    )
    return (first_new, second_new, direction)


def runs():
    row = lax.broadcasted_iota(jnp.int32, (27, 128), 0)
    lane = lax.broadcasted_iota(jnp.int32, (27, 128), 1)
    start = (row * 128) // 108
    run = (row * 128 + lane) // 108
    return [(run == start + p, lane == start + p) for p in range(3)]


def run_sums(value):
    total = jnp.zeros((27, 128), F32)
    for inside, column in runs():
        part = jnp.sum(jnp.where(inside, value, 0.0), axis=1, keepdims=True)
        total = total + jnp.where(column, part, 0.0)
    return jnp.sum(total, axis=0, keepdims=True)


def run_spread(value):
    total = jnp.zeros((27, 128), F32)
    for inside, column in runs():
        part = jnp.sum(jnp.where(column, value, 0.0), axis=1, keepdims=True)
        total = total + jnp.where(inside, part, 0.0)
    return total


def update(in_ref, own_ref, m_ref, f_ref, s_ref, w2_ref, f2_ref, s2_ref, w1_ref, f1_ref, s1_ref):
    y = lax.axis_index("y")
    quarter = y % 2 * 2 + lax.axis_index("core")
    total = in_ref[0, :, 0:640]
    for p in range(1, 8):
        total = total + in_ref[p, :, 0:640]
    grad = total[:, 512:640]
    inside = (
        lax.broadcasted_iota(jnp.int32, (8, 128), 0) * 128 + lax.broadcasted_iota(jnp.int32, (8, 128), 1)
    ) < 864
    group = in_ref[pl.ds(y // 2 * 4, 4), :, 640:768]
    block = []
    for j in range(3):
        block.append(sum(place(group[q, 2 * j : 2 * j + 2], q) for q in range(4)))
    _, _, direction = moments(block[0], block[1], block[2], grad)
    direction = jnp.where(inside, direction, 0.0)
    ratio = jnp.sqrt(jnp.sum(block[0] * block[0], keepdims=True)) / (
        jnp.sqrt(jnp.sum(direction * direction, keepdims=True)) + 1e-06
    )
    mine = take(grad, 0)
    for q in range(1, 4):
        mine = jnp.where(quarter == q, take(grad, q), mine)
    master, first, second = (own_ref[2 * j : 2 * j + 2] for j in range(3))
    first_new, second_new, direction = moments(master, first, second, mine)
    for ref, value in (
        (w2_ref, master - 0.01 * (ratio * direction)),
        (f2_ref, first_new),
        (s2_ref, second_new),
    ):
        ref[...] = jnp.concatenate([value[0:1], value[1:2, 0:88]], axis=1)
    tiles = [total[:, 128 * j : 128 * j + 128] for j in range(4)]
    grad = jnp.concatenate(tiles, axis=0)[0:27]
    master = m_ref[...]
    first_new, second_new, direction = moments(master, f_ref[...], s_ref[...], grad)
    ratio = jnp.sqrt(run_sums(master * master)) / (jnp.sqrt(run_sums(direction * direction)) + 1e-06)
    w1_ref[...] = master - 0.01 * (run_spread(ratio) * direction)
    f1_ref[...] = first_new
    s1_ref[...] = second_new


def exchange(up, down, axes):
    size = lax.axis_size(axes)
    pairs = [(i, i + 1) for i in range(size - 1)]
    before = lax.ppermute(up, axes, pairs)
    after = lax.ppermute(down, axes, [(j, i) for i, j in pairs])
    return before, after


def local(volume, cotangent, w1_master, w1_first, w1_second, w2_master, w2_first, w2_second):
    wide = [w.reshape(1, 216) for w in (w2_master, w2_first, w2_second)]
    narrow = [w.reshape(27, 128) for w in (w1_master, w1_first, w1_second)]
    narrow_band = call(narrow_rows, shape((256, 512), BF16), narrow[0])
    face, along_y = shape((544, 128), BF16), shape((560, 128), BF16)
    slabs, up, down, message, own = call(
        pack,
        (shape((4, 544, 128), BF16), face, face, shape((64, 24, 128), BF16), shape((8, 128), F32)),
        cotangent.reshape(2048, 128),
        volume.reshape(128, 128),
        *wide,
        scratch=(
            pltpu.VMEM((2048, 128), BF16),
            pltpu.VMEM((128, 128), BF16),
            pltpu.VMEM((1, 216), F32),
            pltpu.VMEM((1, 216), F32),
            pltpu.VMEM((1, 216), F32),
            pltpu.VMEM((2048, 128), F32),
            pltpu.VMEM((128, 128), F32),
            pltpu.SemaphoreType.DMA((5,)),
        ),
        space=pl.BlockSpec(memory_space=pltpu.HBM),
    )
    before_x, after_x = exchange(up, down, GX)
    message = lax.all_to_all(message, GX + GZ, 0, 0, tiled=True)
    up, down, bank, beyond = call(
        y_messages,
        (along_y, along_y, shape((128, 128), BF16), shape((16, 640), F32)),
        slabs,
        before_x,
        after_x,
        message,
    )
    before_y, after_y, far = (
        lax.ppermute(part, GY, [(i, (i + by) % 4) for i in range(4)])
        for part, by in ((up, 1), (down, 3), (bank, 2))
    )
    sums = call(
        gradients,
        shape((8, 8, 1408), F32),
        slabs,
        before_x,
        after_x,
        beyond,
        before_y,
        after_y,
        bank,
        far,
        narrow_band,
        scratch=(
            pltpu.VMEM((6, 640, 128), BF16),
            pltpu.VMEM((6, 48, 128), BF16),
            pltpu.VMEM((256, 512), F32),
            pltpu.VMEM((512, 128), F32),
        ),
    )
    sums = lax.all_to_all(sums, GX, 0, 0, tiled=True)
    sums = call(second_stage, shape((4, 8, 768), F32), sums)
    sums = lax.all_to_all(sums, GY, 0, 0, tiled=True)
    sums = call(third_stage, shape((8, 8, 768), F32), sums, own)
    sums = lax.all_to_all(sums, GZ, 0, 0, tiled=True)
    one, rows = shape((1, 216), F32), shape((27, 128), F32)
    new = call(update, (one, one, one, rows, rows, rows), sums, own, *narrow)
    return tuple(w.reshape(-1) for w in new[3:] + new[:3])


def solution(mesh):
    parts = Mesh(mesh.devices.reshape(2, 4, 4, 4, 2), GX + GY + GZ)
    field = P(None, GX, GY, GZ)
    owned = P(GX + GY + GZ)
    return jax.shard_map(
        local,
        mesh=parts,
        in_specs=(field, field, P(), P(), P(), owned, owned, owned),
        out_specs=(P(), P(), P(), owned, owned, owned),
        check_vma=False,
    )
```

```python
import jax
import jax.numpy as jnp
from jax import lax
from jax.experimental import pallas as pl
from jax.experimental.pallas import tpu as pltpu
from jax.sharding import Mesh, PartitionSpec as P

CI = 4
C1 = 32
C2 = 64
F32 = jnp.float32
BF16 = jnp.bfloat16
GX = ("zl", "x")
GY = ("zh",)
GZ = ("y", "core")
VMEM = pl.BlockSpec(memory_space=pltpu.VMEM)
PARAMS = pltpu.CompilerParams(vmem_limit_bytes=32 * 1024 * 1024)


def dot(a, b):
    return lax.dot_general(a, b, (((1,), (0,)), ((), ())), preferred_element_type=F32)


def dot_nt(a, b):
    return lax.dot_general(a, b, (((1,), (1,)), ((), ())), preferred_element_type=F32)


def dot_tn(a, b):
    return lax.dot_general(a, b, (((0,), (0,)), ((), ())), preferred_element_type=F32)


def call(kernel, out_shapes, *args, scratch=(), space=VMEM, params=PARAMS):
    return pl.pallas_call(
        kernel,
        out_shape=out_shapes,
        in_specs=[space] * len(args),
        out_specs=jax.tree.map(lambda _: VMEM, out_shapes),
        scratch_shapes=scratch,
        compiler_params=params,
    )(*args)


def shape(dims, dtype):
    return jax.ShapeDtypeStruct(dims, dtype)


def roll(v, by):
    return pltpu.roll(v, by % v.shape[1], 1)


def lanes():
    return lax.broadcasted_iota(jnp.int32, (1, 128), 1)


def within(v, low, high):
    return jnp.where((lanes() >= low) & (lanes() < high), v, 0.0)


def two_rows(v):
    return [v[:, 0:128], jnp.concatenate([v[:, 128:216], jnp.zeros((1, 40), F32)], axis=1)]


def place(two, q):
    lane = lax.broadcasted_iota(jnp.int32, (1, 128), 1)
    row, at = divmod(216 * q, 128)
    one, last = roll(two[0:1], at), roll(jnp.where(lane < 88, two[1:2], 0.0), at)
    gap = jnp.zeros((1, 128), F32)
    pieces = [gap] * row + [
        jnp.where(lane >= at, one, 0.0),
        jnp.where(lane < at, one, 0.0) + jnp.where(lane >= at, last, 0.0),
        jnp.where(lane < at, last, 0.0),
    ]
    return jnp.concatenate((pieces + [gap] * 8)[:8], axis=0)


def take(block, q):
    lane = lax.broadcasted_iota(jnp.int32, (1, 128), 1)
    row, at = divmod(216 * q, 128)
    moved = [roll(block[r : r + 1], -at) for r in range(row, min(row + 3, 8))]
    one = jnp.where(lane < 128 - at, moved[0], moved[1])
    two = jnp.where(lane < 128 - at, moved[1], moved[2]) if len(moved) > 2 else moved[1]
    return jnp.concatenate([one, two], axis=0)


def along_gz():
    return lax.axis_index("y") * 2 + lax.axis_index("core")


def pack(
    cot_hbm, vol_hbm, w2_hbm, f2_hbm, s2_hbm, slab_ref, up_ref, dn_ref, out_ref, own_ref,
    cot_ref, vol_ref, w2_ref, f2_ref, s2_ref, cot32, vol32, sems,
):
    copies = [
        pltpu.make_async_copy(source, target, sems.at[i])
        for i, (source, target) in enumerate(
            ((cot_hbm, cot_ref), (vol_hbm, vol_ref), (w2_hbm, w2_ref), (f2_hbm, f2_ref), (s2_hbm, s2_ref))
        )
    ]
    for copy in copies:
        copy.start()
    for copy in copies:
        copy.wait()
    cot32[...] = cot_ref[...].astype(F32)
    vol32[...] = vol_ref[...].astype(F32)
    for x in range(4):
        for y in range(8):
            slab_ref[x, 64 * y : 64 * y + 64, :] = cot32[pl.ds(8 * x + y, 64, stride=32), :].astype(BF16)
        slab_ref[x, 512:544, :] = jnp.concatenate(
            [vol32[pl.ds(8 * x + y, 4, stride=32), :] for y in range(8)], axis=0
        ).astype(BF16)
    up_ref[...] = slab_ref[3]
    dn_ref[...] = slab_ref[0]
    row = lax.broadcasted_iota(jnp.int32, (16, 512), 0)
    lane = lax.broadcasted_iota(jnp.int32, (16, 512), 1)
    pick = ((row < 4) & (lane == row * 128)) | ((row >= 4) & (row < 8) & (lane == row * 128 - 385))
    cells = jnp.concatenate([slab_ref[x] for x in range(4)], axis=1)
    cells = jnp.concatenate([cells, jnp.zeros((96, 512), BF16)], axis=0)
    edge = dot_nt(pick.astype(F32).astype(BF16), cells)
    own = [row for ref in (w2_ref, f2_ref, s2_ref) for row in two_rows(ref[...])]
    own_ref[...] = jnp.concatenate(own + [jnp.zeros((2, 128), F32)], axis=0)
    ends = []
    for side in range(2):
        at = slice(4 * side, 4 * side + 4)
        tail = edge[at, 512:640]
        tail = [sum(roll(tail[x : x + 1], 32 * x) for x in range(4))] + own[0:2] + [jnp.zeros((5, 128), F32)]
        ends.append(jnp.concatenate([edge[at, 128 * j : 128 * j + 128] for j in range(4)] + tail, axis=0))
    me = along_gz()
    for p in range(8):
        message = jnp.where(me < p, ends[1], ends[0]).astype(BF16)
        for x in range(8):
            out_ref[8 * x + p] = message


def bank_rows(in_ref, out_ref):
    rows = [in_ref[p, 16:24, :].astype(F32)[1:3] for p in range(64)]
    out_ref[...] = jnp.concatenate(rows, axis=0).astype(BF16)


def y_messages(slab_ref, l_ref, r_ref, in_ref, bank_ref, up_ref, dn_ref, beyond_ref):
    slabs = [l_ref] + [slab_ref.at[x] for x in range(4)] + [r_ref]
    first, last = [], []
    for xe, slab in enumerate(slabs):
        up_ref[xe * 64 : xe * 64 + 64, :] = slab[448:512, :]
        dn_ref[xe * 64 : xe * 64 + 64, :] = slab[0:64, :]
        vol = slab[512:544, :].astype(F32)
        first.append(vol[0:4])
        last.append(vol[28:32])
    fill = [jnp.zeros((8, 128), F32)]
    four = [jnp.zeros((4, 128), F32)]
    across, along = lax.axis_index("zl") * 4 + lax.axis_index("x"), along_gz()
    rows_up, rows_dn = [], []
    for side in range(2):
        other = along + 2 * side - 1
        inside = (other >= 0) & (other <= 7)
        other = jnp.clip(other, 0, 7)
        mid = jnp.where(inside, in_ref[8 * across + other].astype(F32), 0.0)
        before = in_ref[8 * jnp.maximum(across - 1, 0) + other].astype(F32)
        before = jnp.where(inside & (across > 0), before, 0.0)
        after = in_ref[8 * jnp.minimum(across + 1, 7) + other].astype(F32)
        after = jnp.where(inside & (across < 7), after, 0.0)
        parts = [
            jnp.concatenate(
                [before[4 * j + 3 : 4 * j + 4], mid[4 * j : 4 * j + 4], after[4 * j : 4 * j + 1]], axis=0
            )
            for j in range(4)
        ]
        tail = [before[16:17]] + [mid[16:17]] * 4 + [after[16:17]]
        tail = [roll(row, -32 * x) for row, x in zip(tail, (3, 0, 1, 2, 3, 0), strict=True)]
        parts.append(within(jnp.concatenate(tail, axis=0), 0, 32))
        for j in range(5):
            beyond_ref[8 * side : 8 * side + 8, 128 * j : 128 * j + 128] = jnp.concatenate(
                [parts[j], jnp.zeros((2, 128), F32)], axis=0
            )
        rows_up.append(within(roll(parts[3], -64), 0, 64) + within(roll(parts[4], 36), 64, 68))
        rows_dn.append(within(parts[0], 0, 64) + within(roll(parts[4], 64), 64, 68))
    up_ref[384:432, :] = jnp.concatenate(last + fill + rows_up + four, axis=0).astype(BF16)
    dn_ref[384:432, :] = jnp.concatenate(first + fill + rows_dn + four, axis=0).astype(BF16)
    up_ref[432:560, :] = bank_ref[...]
    dn_ref[432:560, :] = bank_ref[...]


def assemble(slab_ref, l_ref, r_ref, beyond_ref, yp_ref, yn_ref, e_ref, ve_ref):
    slabs = [l_ref] + [slab_ref.at[x] for x in range(4)] + [r_ref]
    along_y = lax.axis_index("zh")
    some, more = along_y > 0, along_y < 3
    before = jnp.where(some, yp_ref[384:432, :].astype(F32), 0.0)
    after = jnp.where(more, yn_ref[384:432, :].astype(F32), 0.0)
    for xe, slab in enumerate(slabs):
        e_ref[xe, 0:64, :] = jnp.where(some, yp_ref[xe * 64 : xe * 64 + 64, :].astype(F32), 0.0).astype(BF16)
        e_ref[xe, 64:576, :] = slab[0:512, :]
        e_ref[xe, 576:640, :] = jnp.where(more, yn_ref[xe * 64 : xe * 64 + 64, :].astype(F32), 0.0).astype(BF16)
        vol = slab[512:544, :].astype(F32)
        ve_ref[xe] = jnp.concatenate(
            [before[xe * 4 : xe * 4 + 4], vol, after[xe * 4 : xe * 4 + 4], jnp.zeros((8, 128), F32)], axis=0
        ).astype(BF16)
    ends = []
    for side in range(2):
        parts = [roll(beyond_ref[8 * side : 8 * side + 6, 128 * j : 128 * j + 128], 64) for j in range(5)]
        prev = before[32 + 6 * side : 38 + 6 * side]
        nxt = after[32 + 6 * side : 38 + 6 * side]
        tiles = [within(prev, 0, 64) + within(parts[0], 64, 128)]
        for k in range(1, 4):
            tiles.append(jnp.where(lanes() < 64, parts[k - 1], parts[k]))
        tiles.append(within(parts[3], 0, 64) + within(roll(nxt, 64), 64, 128))
        tiles.append(
            within(roll(prev, -64), 0, 4) + within(roll(parts[4], -60), 4, 36) + within(roll(nxt, -28), 36, 40)
        )
        ends.append(
            jnp.concatenate([jnp.concatenate(tiles, axis=1), jnp.zeros((10, 768), F32)], axis=0).astype(BF16)
        )
    return ends


def flatten(narrow):
    lane = lax.broadcasted_iota(jnp.int32, (1, 128), 1)
    rows = [jnp.zeros((1, 128), F32) for _ in range(33)]
    for c in range(32):
        row, at = divmod(108 * c, 128)
        moved = roll(jnp.where(lane < 108, narrow[c : c + 1], 0.0), at)
        if at + 108 <= 128:
            rows[row] = rows[row] + moved
        else:
            rows[row] = rows[row] + jnp.where(lane >= at, moved, 0.0)
            rows[row + 1] = rows[row + 1] + jnp.where(lane < at, moved, 0.0)
    return jnp.concatenate(rows[:32], axis=0)


def turned(yp_ref, yn_ref, own_ref, far_ref, rows_ref):
    me = lax.axis_index("zh")
    for by, ref, first in ((0, own_ref, 0), (3, yp_ref, 432), (1, yn_ref, 432), (2, far_ref, 0)):
        zh = (me + by) % 4
        for across in range(8):
            at = pl.multiple_of(64 * across + 16 * zh, 16)
            rows_ref[pl.ds(at, 16), :] = ref[first + 16 * across : first + 16 * across + 16, :].astype(F32)
    parts = []
    for q in range(4):
        parts.append(rows_ref[pl.ds(2 * q, 64, stride=8), :].T)
        parts.append(rows_ref[pl.ds(2 * q + 1, 64, stride=8), :].T[0:88])
    return jnp.concatenate(parts, axis=0).astype(BF16)


def narrow_lanes():
    row = lax.broadcasted_iota(jnp.int32, (512, 128), 0)
    col = lax.broadcasted_iota(jnp.int32, (512, 128), 1)
    group, inner = row // 48, row % 48
    a, c = group // 3, group % 3
    b, i = inner // 4, inner % 4
    return ((b < 3) & (group < 9) & (col == (9 * a + 3 * b + c) * 4 + i)).astype(F32)


def narrow_rows(w1_ref, out_ref, pick_ref):
    lane = lax.broadcasted_iota(jnp.int32, (1, 128), 1)
    rows = []
    for c in range(32):
        row, at = divmod(108 * c, 128)
        piece = roll(w1_ref[row : row + 1, :], -at)
        if at > 20:
            piece = jnp.where(lane < 128 - at, piece, roll(w1_ref[row + 1 : row + 2, :], -at))
        rows.append(jnp.where(lane < 108, piece, 0.0))
    bank = jnp.concatenate(rows, axis=0).astype(BF16)
    pick = narrow_lanes().astype(BF16)
    pick_ref[...] = pick
    first = dot_nt(bank, pick)
    for y in range(8):
        out_ref[32 * y : 32 * y + 32, :] = roll(first, 4 * y).astype(BF16)


def gradients(
    slab_ref, l_ref, r_ref, beyond_ref, yp_ref, yn_ref, bank_ref, far_ref, wb_ref, pick_ref, sib_ref,
    keep_ref, send_ref,
    e_ref, ve_ref, ga_ref, rows_ref, wide_ref,
):
    ends = assemble(slab_ref, l_ref, r_ref, beyond_ref, yp_ref, yn_ref, e_ref, ve_ref)
    lane = lax.broadcasted_iota(jnp.int32, (1, 128), 1)
    low, high = lane == 0, lane == 127
    eye = (
        lax.broadcasted_iota(jnp.int32, (48, 128), 0) == lax.broadcasted_iota(jnp.int32, (48, 128), 1)
    ).astype(F32).astype(BF16)
    left = dot_nt(eye, ends[0][:, 640:768])
    right = dot_nt(eye, ends[1][:, 640:768])
    shifted = []
    for xe in range(6):
        v = ve_ref[xe].astype(F32)
        shifted.append(
            (
                jnp.where(low, left[:, xe : xe + 1], roll(v, 1)).astype(BF16),
                ve_ref[xe],
                jnp.where(high, right[:, xe : xe + 1], roll(v, -1)).astype(BF16),
            )
        )
    rest = jnp.zeros((80, 128), BF16)
    patches = jnp.concatenate(
        [
            jnp.concatenate([shifted[x + a][c] for a in range(3) for c in range(3)] + [rest], axis=0)
            for x in range(4)
        ],
        axis=1,
    )
    pre = dot(wb_ref[...], patches)
    sig = 1.0 / (1.0 + jnp.exp(-pre))
    act = (pre * sig).astype(BF16)
    slope = sig * (1.0 + pre * (1.0 - sig))
    halos = []
    for end in ends:
        m = end[:, 0:640].astype(F32)
        halos.append(
            jnp.concatenate(
                [
                    jnp.concatenate([m[a : a + 4, 128 * k : 128 * k + 256] for a in range(3)], axis=1)
                    for k in range(4)
                ],
                axis=0,
            ).astype(BF16)
        )
    none = jnp.zeros((32, 64), BF16)
    weights = turned(yp_ref, yn_ref, bank_ref, far_ref, rows_ref)
    blocks = []
    for c in range(3):
        for yl in range(2):
            cells = []
            for a in range(3):
                for yp in range(4):
                    b = yp - yl
                    if 0 <= b <= 2:
                        tap = (2 - a) * 9 + (2 - b) * 3 + (2 - c)
                        cells.append(weights[tap * 32 : tap * 32 + 32])
                    else:
                        cells.append(none)
            blocks.append(jnp.concatenate(cells, axis=1))
    bank = jnp.concatenate(blocks, axis=0)
    from_left = dot_nt(bank[0:64], halos[0])
    from_right = dot_nt(bank[128:192], halos[1])
    for k in range(4):
        for xp in range(2):
            cells = jnp.concatenate(
                [
                    jnp.concatenate(
                        [e_ref[2 * xp + j + a, 128 * k : 128 * k + 256, :] for j in range(2)], axis=1
                    )
                    for a in range(3)
                ],
                axis=0,
            )
            v = dot(bank, cells)
            for j in range(2):
                x = 2 * xp + j
                at = slice(128 * j, 128 * j + 128)
                col = 4 * k + x
                ga_ref[64 * k : 64 * k + 64, 128 * x : 128 * x + 128] = (
                    v[64:128, at]
                    + jnp.where(low, from_left[:, col : col + 1], roll(v[0:64, at], 1))
                    + jnp.where(high, from_right[:, col : col + 1], roll(v[128:192, at], -1))
                )
    grad_pre = (ga_ref[...] * slope).astype(BF16)
    product = dot_nt(grad_pre, patches)
    total = product[0:32]
    for y in range(1, 8):
        total = total + roll(product[32 * y : 32 * y + 32], -4 * y)
    split, rest = [], total
    for _ in range(3):
        split.append(rest.astype(BF16))
        rest = rest - split[-1].astype(F32)
    picked = dot(jnp.concatenate(split, axis=0), pick_ref[...])
    narrow = picked[0:32] + (picked[32:64] + picked[64:96])
    act32 = act.astype(F32)
    before, after = [], []
    for x in range(4):
        part = act32[:, 128 * x : 128 * x + 128]
        before.append(jnp.where(low, 0.0, roll(part, 1)).astype(BF16))
        after.append(jnp.where(high, 0.0, roll(part, -1)).astype(BF16))
    before = jnp.concatenate(before, axis=1)
    after = jnp.concatenate(after, axis=1)
    empty = jnp.zeros((32, 512), BF16)
    rows = []
    for k in range(4):
        parts = []
        for yl in range(2):
            at = slice(64 * k + 32 * yl, 64 * k + 32 * yl + 32)
            parts += [before[at], act[at], after[at], empty]
        rows.append(jnp.concatenate(parts, axis=0))
    acts = jnp.concatenate(rows, axis=1)
    cots = jnp.concatenate(
        [
            jnp.concatenate(
                [e_ref[x + a, 128 * k : 128 * k + 256, :] for k in range(4) for x in range(4)], axis=1
            )
            for a in range(3)
        ],
        axis=0,
    )
    wide = dot_nt(cots, acts)
    row = lax.broadcasted_iota(jnp.int32, (16, 512), 0)
    lanes = lax.broadcasted_iota(jnp.int32, (16, 512), 1)
    pick = ((row < 4) & (lanes == row * 128)) | ((row >= 4) & (row < 8) & (lanes == (row - 4) * 128 + 127))
    edges = dot_nt(pick.astype(F32).astype(BF16), act)
    gap = jnp.zeros((4, 64), F32)
    one = jnp.zeros((4, 32), F32)
    table = []
    for k in range(4):
        e0 = edges[0:4, 64 * k : 64 * k + 32]
        e1 = edges[0:4, 64 * k + 32 : 64 * k + 64]
        table.append(jnp.concatenate([gap, e0, one, gap, e1, one], axis=1))
    for k in range(4):
        e0 = edges[4:8, 64 * k : 64 * k + 32]
        e1 = edges[4:8, 64 * k + 32 : 64 * k + 64]
        table.append(jnp.concatenate([e0, one, gap, e1, one, gap], axis=1))
    table = jnp.concatenate(table, axis=0).astype(BF16)
    wide = wide + dot_tn(jnp.concatenate(halos, axis=0), table)
    taps = []
    for a in range(3):
        for b in range(3):
            at = (2 - a) * 256 + (2 - b) * 64
            taps.append((wide[at : at + 64, 0:128] + wide[at + 64 : at + 128, 128:256])[:, 0:96])
    wide = jnp.concatenate(taps + [jnp.zeros((64, 32), F32)], axis=1)
    flat = flatten(narrow)
    for j in range(7):
        wide_ref[64 * j : 64 * j + 64, :] = wide[:, 128 * j : 128 * j + 128]
    core = lax.axis_index("core")
    gap = jnp.zeros((4, 128), F32)
    for p in range(8):
        zl, zh = p // 4, p % 4
        halves = []
        for yh in range(2):
            rows = [
                wide_ref[pl.ds(64 * j + 32 * zl + 2 * zh + yh, 4, stride=8), :] for j in range(7)
            ]
            under = [rows[6]] + [flat[16 * yh + 4 * j : 16 * yh + 4 * j + 4] for j in range(4)] + [gap]
            halves.append(
                jnp.concatenate([jnp.concatenate(rows[0:6], axis=1), jnp.concatenate(under, axis=1)], axis=0)
            )
        keep_ref[p] = jnp.where(core == 0, halves[0], halves[1])
        send_ref[p] = jnp.where(core == 0, halves[1], halves[0])


def first_stage(a_ref, b_ref, out_ref):
    out_ref[...] = a_ref[...] + b_ref[...]


def second_stage(in_ref, out_ref):
    total = in_ref[0]
    for p in range(1, 8):
        total = total + in_ref[p]
    narrow = [total[4:8, 128 * j : 128 * j + 128] for j in range(1, 5)]
    for x in range(4):
        block = [total[x : x + 1, 128 * j : 128 * j + 128] for j in range(6)]
        block += [total[4 + x : 5 + x, 0:128], jnp.zeros((1, 128), F32)]
        rows = jnp.concatenate(block + narrow, axis=0)
        for y in range(4):
            out_ref[4 * x + y] = rows


def third_stage(in_ref, own_ref, sib_ref, out_ref):
    total = in_ref[0]
    for p in range(1, 16):
        total = total + in_ref[p]
    out_ref[0:24, :] = total
    even = lax.axis_index("y") % 2 == 0
    own, sib = own_ref[...], sib_ref[...]
    out_ref[24:32, :] = jnp.where(even, own, sib)
    out_ref[32:40, :] = jnp.where(even, sib, own)


def moments(master, first, second, grad):
    first_new = 0.9 * first + 0.1 * grad
    second_new = 0.999 * second + 0.001 * grad * grad
    direction = (
        first_new / (1.0 - 0.9**10) / (jnp.sqrt(second_new / (1.0 - 0.999**10)) + 1e-06)
        + 0.01 * master
    )
    return (first_new, second_new, direction)


def runs():
    row = lax.broadcasted_iota(jnp.int32, (27, 128), 0)
    lane = lax.broadcasted_iota(jnp.int32, (27, 128), 1)
    start = (row * 128) // 108
    run = (row * 128 + lane) // 108
    return [(run == start + p, lane == start + p) for p in range(3)]


def run_sums(value):
    total = jnp.zeros((27, 128), F32)
    for inside, column in runs():
        part = jnp.sum(jnp.where(inside, value, 0.0), axis=1, keepdims=True)
        total = total + jnp.where(column, part, 0.0)
    return jnp.sum(total, axis=0, keepdims=True)


def run_spread(value):
    total = jnp.zeros((27, 128), F32)
    for inside, column in runs():
        part = jnp.sum(jnp.where(column, value, 0.0), axis=1, keepdims=True)
        total = total + jnp.where(inside, part, 0.0)
    return total


def update(in_ref, other_ref, own_ref, m_ref, f_ref, s_ref, w2_ref, f2_ref, s2_ref, w1_ref, f1_ref, s1_ref):
    y, core = lax.axis_index("y"), lax.axis_index("core")
    quarter = y % 2 * 2 + core
    mine, other = in_ref[...], other_ref[...]
    low, high = jnp.where(core == 0, mine, other), jnp.where(core == 0, other, mine)
    grad = jnp.where(y // 2 == 0, low[0:8], high[0:8])
    inside = (
        lax.broadcasted_iota(jnp.int32, (8, 128), 0) * 128 + lax.broadcasted_iota(jnp.int32, (8, 128), 1)
    ) < 864
    block = []
    for j in range(3):
        parts = [half[at + 2 * j : at + 2 * j + 2] for at in (24, 32) for half in (low, high)]
        block.append(sum(place(part, q) for q, part in enumerate(parts)))
    _, _, direction = moments(block[0], block[1], block[2], grad)
    direction = jnp.where(inside, direction, 0.0)
    ratio = jnp.sqrt(jnp.sum(block[0] * block[0], keepdims=True)) / (
        jnp.sqrt(jnp.sum(direction * direction, keepdims=True)) + 1e-06
    )
    mine = take(grad, 0)
    for q in range(1, 4):
        mine = jnp.where(quarter == q, take(grad, q), mine)
    master, first, second = (own_ref[2 * j : 2 * j + 2] for j in range(3))
    first_new, second_new, direction = moments(master, first, second, mine)
    for ref, value in (
        (w2_ref, master - 0.01 * (ratio * direction)),
        (f2_ref, first_new),
        (s2_ref, second_new),
    ):
        ref[...] = jnp.concatenate([value[0:1], value[1:2, 0:88]], axis=1)
    grad = jnp.concatenate([low[8:24], high[8:24]], axis=0)[0:27]
    master = m_ref[...]
    first_new, second_new, direction = moments(master, f_ref[...], s_ref[...], grad)
    ratio = jnp.sqrt(run_sums(master * master)) / (jnp.sqrt(run_sums(direction * direction)) + 1e-06)
    w1_ref[...] = master - 0.01 * (run_spread(ratio) * direction)
    f1_ref[...] = first_new
    s1_ref[...] = second_new


def exchange(up, down, axes):
    size = lax.axis_size(axes)
    pairs = [(i, i + 1) for i in range(size - 1)]
    before = lax.ppermute(up, axes, pairs)
    after = lax.ppermute(down, axes, [(j, i) for i, j in pairs])
    return before, after


def turn(value, by):
    return lax.ppermute(value, GY, [(i, (i + by) % 4) for i in range(4)])


def swap(value):
    return lax.ppermute(value, "core", [(0, 1), (1, 0)])


def local(volume, cotangent, w1_master, w1_first, w1_second, w2_master, w2_first, w2_second):
    wide = [w.reshape(1, 216) for w in (w2_master, w2_first, w2_second)]
    narrow = [w.reshape(27, 128) for w in (w1_master, w1_first, w1_second)]
    narrow_band, pick = call(narrow_rows, (shape((256, 512), BF16), shape((512, 128), BF16)), narrow[0])
    face, along_y = shape((544, 128), BF16), shape((560, 128), BF16)
    slabs, up, down, message, own = call(
        pack,
        (shape((4, 544, 128), BF16), face, face, shape((64, 24, 128), BF16), shape((8, 128), F32)),
        cotangent.reshape(2048, 128),
        volume.reshape(128, 128),
        *wide,
        scratch=(
            pltpu.VMEM((2048, 128), BF16),
            pltpu.VMEM((128, 128), BF16),
            pltpu.VMEM((1, 216), F32),
            pltpu.VMEM((1, 216), F32),
            pltpu.VMEM((1, 216), F32),
            pltpu.VMEM((2048, 128), F32),
            pltpu.VMEM((128, 128), F32),
            pltpu.SemaphoreType.DMA((5,)),
        ),
        space=pl.BlockSpec(memory_space=pltpu.HBM),
        params=pltpu.CompilerParams(vmem_limit_bytes=60 * 1024 * 1024),
    )
    before_x, after_x = exchange(up, down, GX)
    sibling = lax.ppermute(own, "y", [(0, 1), (1, 0), (2, 3), (3, 2)])
    message = lax.all_to_all(message, GX + GZ, 0, 0, tiled=True)
    bank = call(bank_rows, shape((128, 128), BF16), message)
    far = turn(bank, 2)
    up, down, beyond = call(
        y_messages, (along_y, along_y, shape((16, 640), F32)), slabs, before_x, after_x, message, bank
    )
    before_y, after_y = turn(up, 1), turn(down, 3)
    keep, send = call(
        gradients,
        (shape((8, 8, 768), F32), shape((8, 8, 768), F32)),
        slabs,
        before_x,
        after_x,
        beyond,
        before_y,
        after_y,
        bank,
        far,
        narrow_band,
        pick,
        sibling,
        scratch=(
            pltpu.VMEM((6, 640, 128), BF16),
            pltpu.VMEM((6, 48, 128), BF16),
            pltpu.VMEM((256, 512), F32),
            pltpu.VMEM((512, 128), F32),
            pltpu.VMEM((448, 128), F32),
        ),
    )
    sums = call(first_stage, shape((8, 8, 768), F32), keep, swap(send))
    sums = lax.all_to_all(sums, ("zl", "zh"), 0, 0, tiled=True)
    sums = call(second_stage, shape((16, 24, 128), F32), sums)
    sums = lax.all_to_all(sums, ("x", "y"), 0, 0, tiled=True)
    half = call(third_stage, shape((40, 128), F32), sums, own, sibling)
    one, rows = shape((1, 216), F32), shape((27, 128), F32)
    new = call(update, (one, one, one, rows, rows, rows), half, swap(half), own, *narrow)
    return tuple(w.reshape(-1) for w in new[3:] + new[:3])


def solution(mesh):
    parts = Mesh(mesh.devices.reshape(2, 4, 4, 4, 2), GX + GY + GZ)
    field = P(None, GX, GY, GZ)
    owned = P(GX + GY + GZ)
    return jax.shard_map(
        local,
        mesh=parts,
        in_specs=(field, field, P(), P(), P(), owned, owned, owned),
        out_specs=(P(), P(), P(), owned, owned, owned),
        check_vma=False,
    )
```

```python
import jax
import jax.numpy as jnp
from jax import lax
from jax.experimental import pallas as pl
from jax.experimental.pallas import tpu as pltpu
from jax.sharding import Mesh, PartitionSpec as P

CI = 4
C1 = 32
C2 = 64
F32 = jnp.float32
BF16 = jnp.bfloat16
GX = ("zl", "x")
GY = ("zh",)
GZ = ("y", "core")
VMEM = pl.BlockSpec(memory_space=pltpu.VMEM)
PARAMS = pltpu.CompilerParams(vmem_limit_bytes=32 * 1024 * 1024)


def dot(a, b):
    return lax.dot_general(a, b, (((1,), (0,)), ((), ())), preferred_element_type=F32)


def dot_nt(a, b):
    return lax.dot_general(a, b, (((1,), (1,)), ((), ())), preferred_element_type=F32)


def dot_tn(a, b):
    return lax.dot_general(a, b, (((0,), (0,)), ((), ())), preferred_element_type=F32)


def call(kernel, out_shapes, *args, scratch=(), space=VMEM, params=PARAMS):
    return pl.pallas_call(
        kernel,
        out_shape=out_shapes,
        in_specs=[space] * len(args),
        out_specs=jax.tree.map(lambda _: VMEM, out_shapes),
        scratch_shapes=scratch,
        compiler_params=params,
    )(*args)


def shape(dims, dtype):
    return jax.ShapeDtypeStruct(dims, dtype)


def roll(v, by):
    return pltpu.roll(v, by % v.shape[1], 1)


def lanes():
    return lax.broadcasted_iota(jnp.int32, (1, 128), 1)


def within(v, low, high):
    return jnp.where((lanes() >= low) & (lanes() < high), v, 0.0)


def two_rows(v):
    return [v[:, 0:128], jnp.concatenate([v[:, 128:216], jnp.zeros((1, 40), F32)], axis=1)]


def place(two, q):
    lane = lax.broadcasted_iota(jnp.int32, (1, 128), 1)
    row, at = divmod(216 * q, 128)
    one, last = roll(two[0:1], at), roll(jnp.where(lane < 88, two[1:2], 0.0), at)
    gap = jnp.zeros((1, 128), F32)
    pieces = [gap] * row + [
        jnp.where(lane >= at, one, 0.0),
        jnp.where(lane < at, one, 0.0) + jnp.where(lane >= at, last, 0.0),
        jnp.where(lane < at, last, 0.0),
    ]
    return jnp.concatenate((pieces + [gap] * 8)[:8], axis=0)


def take(block, q):
    lane = lax.broadcasted_iota(jnp.int32, (1, 128), 1)
    row, at = divmod(216 * q, 128)
    moved = [roll(block[r : r + 1], -at) for r in range(row, min(row + 3, 8))]
    one = jnp.where(lane < 128 - at, moved[0], moved[1])
    two = jnp.where(lane < 128 - at, moved[1], moved[2]) if len(moved) > 2 else moved[1]
    return jnp.concatenate([one, two], axis=0)


def along_gz():
    return lax.axis_index("y") * 2 + lax.axis_index("core")


def pack(
    cot_hbm, vol_hbm, w2_hbm, f2_hbm, s2_hbm, slab_ref, up_ref, dn_ref, out_ref, own_ref,
    cot_ref, vol_ref, w2_ref, f2_ref, s2_ref, cot32, vol32, sems,
):
    copies = [
        pltpu.make_async_copy(source, target, sems.at[i])
        for i, (source, target) in enumerate(
            ((cot_hbm, cot_ref), (vol_hbm, vol_ref), (w2_hbm, w2_ref), (f2_hbm, f2_ref), (s2_hbm, s2_ref))
        )
    ]
    for copy in copies:
        copy.start()
    for copy in copies:
        copy.wait()
    cot32[...] = cot_ref[...].astype(F32)
    vol32[...] = vol_ref[...].astype(F32)
    for x in range(4):
        for y in range(8):
            slab_ref[x, 64 * y : 64 * y + 64, :] = cot32[pl.ds(8 * x + y, 64, stride=32), :].astype(BF16)
        slab_ref[x, 512:544, :] = jnp.concatenate(
            [vol32[pl.ds(8 * x + y, 4, stride=32), :] for y in range(8)], axis=0
        ).astype(BF16)
    up_ref[...] = slab_ref[3]
    dn_ref[...] = slab_ref[0]
    row = lax.broadcasted_iota(jnp.int32, (16, 512), 0)
    lane = lax.broadcasted_iota(jnp.int32, (16, 512), 1)
    pick = ((row < 4) & (lane == row * 128)) | ((row >= 4) & (row < 8) & (lane == row * 128 - 385))
    cells = jnp.concatenate([slab_ref[x] for x in range(4)], axis=1)
    cells = jnp.concatenate([cells, jnp.zeros((96, 512), BF16)], axis=0)
    edge = dot_nt(pick.astype(F32).astype(BF16), cells)
    own = [row for ref in (w2_ref, f2_ref, s2_ref) for row in two_rows(ref[...])]
    own_ref[...] = jnp.concatenate(own + [jnp.zeros((2, 128), F32)], axis=0)
    ends = []
    for side in range(2):
        at = slice(4 * side, 4 * side + 4)
        tail = edge[at, 512:640]
        tail = [sum(roll(tail[x : x + 1], 32 * x) for x in range(4))] + own[0:2] + [jnp.zeros((5, 128), F32)]
        ends.append(jnp.concatenate([edge[at, 128 * j : 128 * j + 128] for j in range(4)] + tail, axis=0))
    me = along_gz()
    for p in range(8):
        message = jnp.where(me < p, ends[1], ends[0]).astype(BF16)
        for x in range(8):
            out_ref[8 * x + p] = message


def bank_rows(in_ref, out_ref):
    rows = [in_ref[p, 16:24, :].astype(F32)[1:3] for p in range(64)]
    out_ref[...] = jnp.concatenate(rows, axis=0).astype(BF16)


def y_messages(slab_ref, l_ref, r_ref, in_ref, pb_ref, nb_ref, up_ref, dn_ref, beyond_ref):
    slabs = [l_ref] + [slab_ref.at[x] for x in range(4)] + [r_ref]
    first, last = [], []
    for xe, slab in enumerate(slabs):
        up_ref[xe * 64 : xe * 64 + 64, :] = slab[448:512, :]
        dn_ref[xe * 64 : xe * 64 + 64, :] = slab[0:64, :]
        vol = slab[512:544, :].astype(F32)
        first.append(vol[0:4])
        last.append(vol[28:32])
    fill = [jnp.zeros((8, 128), F32)]
    four = [jnp.zeros((4, 128), F32)]
    across, along = lax.axis_index("zl") * 4 + lax.axis_index("x"), along_gz()
    rows_up, rows_dn = [], []
    for side in range(2):
        other = along + 2 * side - 1
        inside = (other >= 0) & (other <= 7)
        other = jnp.clip(other, 0, 7)
        mid = jnp.where(inside, in_ref[8 * across + other].astype(F32), 0.0)
        before = in_ref[8 * jnp.maximum(across - 1, 0) + other].astype(F32)
        before = jnp.where(inside & (across > 0), before, 0.0)
        after = in_ref[8 * jnp.minimum(across + 1, 7) + other].astype(F32)
        after = jnp.where(inside & (across < 7), after, 0.0)
        parts = [
            jnp.concatenate(
                [before[4 * j + 3 : 4 * j + 4], mid[4 * j : 4 * j + 4], after[4 * j : 4 * j + 1]], axis=0
            )
            for j in range(4)
        ]
        tail = [before[16:17]] + [mid[16:17]] * 4 + [after[16:17]]
        tail = [roll(row, -32 * x) for row, x in zip(tail, (3, 0, 1, 2, 3, 0), strict=True)]
        parts.append(within(jnp.concatenate(tail, axis=0), 0, 32))
        for j in range(5):
            beyond_ref[8 * side : 8 * side + 8, 128 * j : 128 * j + 128] = jnp.concatenate(
                [parts[j], jnp.zeros((2, 128), F32)], axis=0
            )
        rows_up.append(within(roll(parts[3], -64), 0, 64) + within(roll(parts[4], 36), 64, 68))
        rows_dn.append(within(parts[0], 0, 64) + within(roll(parts[4], 64), 64, 68))
    up_ref[384:432, :] = jnp.concatenate(last + fill + rows_up + four, axis=0).astype(BF16)
    dn_ref[384:432, :] = jnp.concatenate(first + fill + rows_dn + four, axis=0).astype(BF16)
    up_ref[432:496, :] = pb_ref[0:64, :]
    dn_ref[432:496, :] = nb_ref[64:128, :]


def assemble(slab_ref, l_ref, r_ref, beyond_ref, yp_ref, yn_ref, e_ref, ve_ref):
    slabs = [l_ref] + [slab_ref.at[x] for x in range(4)] + [r_ref]
    along_y = lax.axis_index("zh")
    some, more = along_y > 0, along_y < 3
    before = jnp.where(some, yp_ref[384:432, :].astype(F32), 0.0)
    after = jnp.where(more, yn_ref[384:432, :].astype(F32), 0.0)
    for xe, slab in enumerate(slabs):
        at = slice(128 * xe, 128 * xe + 128)
        e_ref[0:64, at] = jnp.where(some, yp_ref[xe * 64 : xe * 64 + 64, :].astype(F32), 0.0).astype(BF16)
        e_ref[64:576, at] = slab[0:512, :]
        e_ref[576:640, at] = jnp.where(more, yn_ref[xe * 64 : xe * 64 + 64, :].astype(F32), 0.0).astype(BF16)
        vol = slab[512:544, :].astype(F32)
        ve_ref[xe] = jnp.concatenate(
            [before[xe * 4 : xe * 4 + 4], vol, after[xe * 4 : xe * 4 + 4], jnp.zeros((8, 128), F32)], axis=0
        ).astype(BF16)
    ends = []
    for side in range(2):
        parts = [roll(beyond_ref[8 * side : 8 * side + 6, 128 * j : 128 * j + 128], 64) for j in range(5)]
        prev = before[32 + 6 * side : 38 + 6 * side]
        nxt = after[32 + 6 * side : 38 + 6 * side]
        tiles = [within(prev, 0, 64) + within(parts[0], 64, 128)]
        for k in range(1, 4):
            tiles.append(jnp.where(lanes() < 64, parts[k - 1], parts[k]))
        tiles.append(within(parts[3], 0, 64) + within(roll(nxt, 64), 64, 128))
        tiles.append(
            within(roll(prev, -64), 0, 4) + within(roll(parts[4], -60), 4, 36) + within(roll(nxt, -28), 36, 40)
        )
        ends.append(
            jnp.concatenate([jnp.concatenate(tiles, axis=1), jnp.zeros((10, 768), F32)], axis=0).astype(BF16)
        )
    return ends


def flatten(narrow):
    lane = lax.broadcasted_iota(jnp.int32, (1, 128), 1)
    rows = [jnp.zeros((1, 128), F32) for _ in range(33)]
    for c in range(32):
        row, at = divmod(108 * c, 128)
        moved = roll(jnp.where(lane < 108, narrow[c : c + 1], 0.0), at)
        if at + 108 <= 128:
            rows[row] = rows[row] + moved
        else:
            rows[row] = rows[row] + jnp.where(lane >= at, moved, 0.0)
            rows[row + 1] = rows[row + 1] + jnp.where(lane < at, moved, 0.0)
    return jnp.concatenate(rows[:32], axis=0)


def turned(yp_ref, yn_ref, own_ref, pb_ref, nb_ref, rows_ref):
    me = lax.axis_index("zh")
    for by in range(4):
        zh = (me + by) % 4
        for across in range(8):
            at = pl.multiple_of(64 * across + 16 * zh, 16)
            if by == 2:
                ref, row = (yp_ref if across < 4 else yn_ref), 432 + 16 * (across % 4)
            else:
                ref, row = (own_ref, nb_ref, None, pb_ref)[by], 16 * across
            rows_ref[pl.ds(at, 16), :] = ref[row : row + 16, :].astype(F32)
    parts = []
    for q in range(4):
        parts.append(rows_ref[pl.ds(2 * q, 64, stride=8), :].T)
        parts.append(rows_ref[pl.ds(2 * q + 1, 64, stride=8), :].T[0:88])
    return jnp.concatenate(parts, axis=0).astype(BF16)


def narrow_lanes():
    row = lax.broadcasted_iota(jnp.int32, (512, 128), 0)
    col = lax.broadcasted_iota(jnp.int32, (512, 128), 1)
    group, inner = row // 48, row % 48
    a, c = group // 3, group % 3
    b, i = inner // 4, inner % 4
    return ((b < 3) & (group < 9) & (col == (9 * a + 3 * b + c) * 4 + i)).astype(F32)


def narrow_rows(w1_ref, out_ref, pick_ref):
    lane = lax.broadcasted_iota(jnp.int32, (1, 128), 1)
    rows = []
    for c in range(32):
        row, at = divmod(108 * c, 128)
        piece = roll(w1_ref[row : row + 1, :], -at)
        if at > 20:
            piece = jnp.where(lane < 128 - at, piece, roll(w1_ref[row + 1 : row + 2, :], -at))
        rows.append(jnp.where(lane < 108, piece, 0.0))
    bank = jnp.concatenate(rows, axis=0).astype(BF16)
    pick = narrow_lanes().astype(BF16)
    pick_ref[...] = pick
    first = dot_nt(bank, pick)
    for y in range(8):
        out_ref[32 * y : 32 * y + 32, :] = roll(first, 4 * y).astype(BF16)


def gradients(
    slab_ref, l_ref, r_ref, beyond_ref, yp_ref, yn_ref, bank_ref, pb_ref, nb_ref, wb_ref, pick_ref, sib_ref,
    keep_ref, send_ref,
    e_ref, ve_ref, ga_ref, rows_ref, wide_ref,
):
    ends = assemble(slab_ref, l_ref, r_ref, beyond_ref, yp_ref, yn_ref, e_ref, ve_ref)
    lane = lax.broadcasted_iota(jnp.int32, (1, 128), 1)
    low, high = lane == 0, lane == 127
    eye = (
        lax.broadcasted_iota(jnp.int32, (48, 128), 0) == lax.broadcasted_iota(jnp.int32, (48, 128), 1)
    ).astype(F32).astype(BF16)
    left = dot_nt(eye, ends[0][:, 640:768])
    right = dot_nt(eye, ends[1][:, 640:768])
    shifted = []
    for xe in range(6):
        v = ve_ref[xe].astype(F32)
        shifted.append(
            (
                jnp.where(low, left[:, xe : xe + 1], roll(v, 1)).astype(BF16),
                ve_ref[xe],
                jnp.where(high, right[:, xe : xe + 1], roll(v, -1)).astype(BF16),
            )
        )
    rest = jnp.zeros((80, 128), BF16)
    patches = jnp.concatenate(
        [
            jnp.concatenate([shifted[x + a][c] for a in range(3) for c in range(3)] + [rest], axis=0)
            for x in range(4)
        ],
        axis=1,
    )
    pre = dot(wb_ref[...], patches)
    sig = 1.0 / (1.0 + jnp.exp(-pre))
    act = (pre * sig).astype(BF16)
    slope = sig * (1.0 + pre * (1.0 - sig))
    halos = []
    for end in ends:
        m = end[:, 0:640].astype(F32)
        halos.append(
            jnp.concatenate(
                [
                    jnp.concatenate([m[a : a + 4, 128 * k : 128 * k + 256] for a in range(3)], axis=1)
                    for k in range(4)
                ],
                axis=0,
            ).astype(BF16)
        )
    none = jnp.zeros((32, 64), BF16)
    weights = turned(yp_ref, yn_ref, bank_ref, pb_ref, nb_ref, rows_ref)
    blocks = []
    for c in range(3):
        for yl in range(2):
            cells = []
            for a in range(3):
                for yp in range(4):
                    b = yp - yl
                    if 0 <= b <= 2:
                        tap = (2 - a) * 9 + (2 - b) * 3 + (2 - c)
                        cells.append(weights[tap * 32 : tap * 32 + 32])
                    else:
                        cells.append(none)
            blocks.append(jnp.concatenate(cells, axis=1))
    bank = jnp.concatenate(blocks, axis=0)
    from_left = dot_nt(bank[0:64], halos[0])
    from_right = dot_nt(bank[128:192], halos[1])
    for k in range(4):
        for xp in range(2):
            v = sum(
                dot(
                    bank[:, 256 * a : 256 * a + 256],
                    e_ref[128 * k : 128 * k + 256, 128 * (2 * xp + a) : 128 * (2 * xp + a) + 256],
                )
                for a in range(3)
            )
            for j in range(2):
                x = 2 * xp + j
                at = slice(128 * j, 128 * j + 128)
                col = 4 * k + x
                ga_ref[64 * k : 64 * k + 64, 128 * x : 128 * x + 128] = (
                    v[64:128, at]
                    + jnp.where(low, from_left[:, col : col + 1], roll(v[0:64, at], 1))
                    + jnp.where(high, from_right[:, col : col + 1], roll(v[128:192, at], -1))
                )
    grad_pre = (ga_ref[...] * slope).astype(BF16)
    product = dot_nt(grad_pre, patches)
    total = product[0:32]
    for y in range(1, 8):
        total = total + roll(product[32 * y : 32 * y + 32], -4 * y)
    split, rest = [], total
    for _ in range(3):
        split.append(rest.astype(BF16))
        rest = rest - split[-1].astype(F32)
    picked = dot(jnp.concatenate(split, axis=0), pick_ref[...])
    narrow = picked[0:32] + (picked[32:64] + picked[64:96])
    act32 = act.astype(F32)
    before, after = [], []
    for x in range(4):
        part = act32[:, 128 * x : 128 * x + 128]
        before.append(jnp.where(low, 0.0, roll(part, 1)).astype(BF16))
        after.append(jnp.where(high, 0.0, roll(part, -1)).astype(BF16))
    before = jnp.concatenate(before, axis=1)
    after = jnp.concatenate(after, axis=1)
    empty = jnp.zeros((32, 512), BF16)
    rows = []
    for k in range(4):
        parts = []
        for yl in range(2):
            at = slice(64 * k + 32 * yl, 64 * k + 32 * yl + 32)
            parts += [before[at], act[at], after[at], empty]
        rows.append(jnp.concatenate(parts, axis=0))
    wide = jnp.concatenate(
        [
            sum(
                dot_nt(e_ref[128 * k : 128 * k + 256, 128 * a : 128 * a + 512], rows[k])
                for k in range(4)
            )
            for a in range(3)
        ],
        axis=0,
    )
    row = lax.broadcasted_iota(jnp.int32, (16, 512), 0)
    lanes = lax.broadcasted_iota(jnp.int32, (16, 512), 1)
    pick = ((row < 4) & (lanes == row * 128)) | ((row >= 4) & (row < 8) & (lanes == (row - 4) * 128 + 127))
    edges = dot_nt(pick.astype(F32).astype(BF16), act)
    gap = jnp.zeros((4, 64), F32)
    one = jnp.zeros((4, 32), F32)
    table = []
    for k in range(4):
        e0 = edges[0:4, 64 * k : 64 * k + 32]
        e1 = edges[0:4, 64 * k + 32 : 64 * k + 64]
        table.append(jnp.concatenate([gap, e0, one, gap, e1, one], axis=1))
    for k in range(4):
        e0 = edges[4:8, 64 * k : 64 * k + 32]
        e1 = edges[4:8, 64 * k + 32 : 64 * k + 64]
        table.append(jnp.concatenate([e0, one, gap, e1, one, gap], axis=1))
    table = jnp.concatenate(table, axis=0).astype(BF16)
    wide = wide + dot_tn(jnp.concatenate(halos, axis=0), table)
    taps = []
    for a in range(3):
        for b in range(3):
            at = (2 - a) * 256 + (2 - b) * 64
            taps.append((wide[at : at + 64, 0:128] + wide[at + 64 : at + 128, 128:256])[:, 0:96])
    wide = jnp.concatenate(taps + [jnp.zeros((64, 32), F32)], axis=1)
    flat = flatten(narrow)
    for j in range(7):
        wide_ref[64 * j : 64 * j + 64, :] = wide[:, 128 * j : 128 * j + 128]
    core = lax.axis_index("core")
    gap = jnp.zeros((4, 128), F32)
    for p in range(8):
        zl, zh = p // 4, p % 4
        halves = []
        for yh in range(2):
            rows = [
                wide_ref[pl.ds(64 * j + 32 * zl + 2 * zh + yh, 4, stride=8), :] for j in range(7)
            ]
            under = [rows[6]] + [flat[16 * yh + 4 * j : 16 * yh + 4 * j + 4] for j in range(4)] + [gap]
            halves.append(
                jnp.concatenate([jnp.concatenate(rows[0:6], axis=1), jnp.concatenate(under, axis=1)], axis=0)
            )
        keep_ref[p] = jnp.where(core == 0, halves[0], halves[1])
        send_ref[p] = jnp.where(core == 0, halves[1], halves[0])


def first_stage(a_ref, b_ref, out_ref):
    out_ref[...] = a_ref[...] + b_ref[...]


def second_stage(in_ref, out_ref):
    total = in_ref[0]
    for p in range(1, 8):
        total = total + in_ref[p]
    narrow = [total[4:8, 128 * j : 128 * j + 128] for j in range(1, 5)]
    for x in range(4):
        block = [total[x : x + 1, 128 * j : 128 * j + 128] for j in range(6)]
        block += [total[4 + x : 5 + x, 0:128], jnp.zeros((1, 128), F32)]
        rows = jnp.concatenate(block + narrow, axis=0)
        for y in range(4):
            out_ref[4 * x + y] = rows


def third_stage(in_ref, own_ref, sib_ref, out_ref):
    total = in_ref[0]
    for p in range(1, 16):
        total = total + in_ref[p]
    out_ref[0:24, :] = total
    even = lax.axis_index("y") % 2 == 0
    own, sib = own_ref[...], sib_ref[...]
    out_ref[24:32, :] = jnp.where(even, own, sib)
    out_ref[32:40, :] = jnp.where(even, sib, own)


def moments(master, first, second, grad):
    first_new = 0.9 * first + 0.1 * grad
    second_new = 0.999 * second + 0.001 * grad * grad
    direction = (
        first_new / (1.0 - 0.9**10) / (jnp.sqrt(second_new / (1.0 - 0.999**10)) + 1e-06)
        + 0.01 * master
    )
    return (first_new, second_new, direction)


def runs():
    row = lax.broadcasted_iota(jnp.int32, (27, 128), 0)
    lane = lax.broadcasted_iota(jnp.int32, (27, 128), 1)
    start = (row * 128) // 108
    run = (row * 128 + lane) // 108
    return [(run == start + p, lane == start + p) for p in range(3)]


def run_sums(value):
    total = jnp.zeros((27, 128), F32)
    for inside, column in runs():
        part = jnp.sum(jnp.where(inside, value, 0.0), axis=1, keepdims=True)
        total = total + jnp.where(column, part, 0.0)
    return jnp.sum(total, axis=0, keepdims=True)


def run_spread(value):
    total = jnp.zeros((27, 128), F32)
    for inside, column in runs():
        part = jnp.sum(jnp.where(column, value, 0.0), axis=1, keepdims=True)
        total = total + jnp.where(inside, part, 0.0)
    return total


def update(in_ref, other_ref, own_ref, m_ref, f_ref, s_ref, w2_ref, f2_ref, s2_ref, w1_ref, f1_ref, s1_ref):
    y, core = lax.axis_index("y"), lax.axis_index("core")
    quarter = y % 2 * 2 + core
    mine, other = in_ref[...], other_ref[...]
    low, high = jnp.where(core == 0, mine, other), jnp.where(core == 0, other, mine)
    grad = jnp.where(y // 2 == 0, low[0:8], high[0:8])
    inside = (
        lax.broadcasted_iota(jnp.int32, (8, 128), 0) * 128 + lax.broadcasted_iota(jnp.int32, (8, 128), 1)
    ) < 864
    block = []
    for j in range(3):
        parts = [half[at + 2 * j : at + 2 * j + 2] for at in (24, 32) for half in (low, high)]
        block.append(sum(place(part, q) for q, part in enumerate(parts)))
    _, _, direction = moments(block[0], block[1], block[2], grad)
    direction = jnp.where(inside, direction, 0.0)
    ratio = jnp.sqrt(jnp.sum(block[0] * block[0], keepdims=True)) / (
        jnp.sqrt(jnp.sum(direction * direction, keepdims=True)) + 1e-06
    )
    mine = take(grad, 0)
    for q in range(1, 4):
        mine = jnp.where(quarter == q, take(grad, q), mine)
    master, first, second = (own_ref[2 * j : 2 * j + 2] for j in range(3))
    first_new, second_new, direction = moments(master, first, second, mine)
    for ref, value in (
        (w2_ref, master - 0.01 * (ratio * direction)),
        (f2_ref, first_new),
        (s2_ref, second_new),
    ):
        ref[...] = jnp.concatenate([value[0:1], value[1:2, 0:88]], axis=1)
    grad = jnp.concatenate([low[8:24], high[8:24]], axis=0)[0:27]
    master = m_ref[...]
    first_new, second_new, direction = moments(master, f_ref[...], s_ref[...], grad)
    ratio = jnp.sqrt(run_sums(master * master)) / (jnp.sqrt(run_sums(direction * direction)) + 1e-06)
    w1_ref[...] = master - 0.01 * (run_spread(ratio) * direction)
    f1_ref[...] = first_new
    s1_ref[...] = second_new


def exchange(up, down, axes):
    size = lax.axis_size(axes)
    pairs = [(i, i + 1) for i in range(size - 1)]
    before = lax.ppermute(up, axes, pairs)
    after = lax.ppermute(down, axes, [(j, i) for i, j in pairs])
    return before, after


def turn(value, by):
    return lax.ppermute(value, GY, [(i, (i + by) % 4) for i in range(4)])


def swap(value):
    return lax.ppermute(value, "core", [(0, 1), (1, 0)])


def local(volume, cotangent, w1_master, w1_first, w1_second, w2_master, w2_first, w2_second):
    wide = [w.reshape(1, 216) for w in (w2_master, w2_first, w2_second)]
    narrow = [w.reshape(27, 128) for w in (w1_master, w1_first, w1_second)]
    narrow_band, pick = call(narrow_rows, (shape((256, 512), BF16), shape((512, 128), BF16)), narrow[0])
    face, along_y = shape((544, 128), BF16), shape((496, 128), BF16)
    slabs, up, down, message, own = call(
        pack,
        (shape((4, 544, 128), BF16), face, face, shape((64, 24, 128), BF16), shape((8, 128), F32)),
        cotangent.reshape(2048, 128),
        volume.reshape(128, 128),
        *wide,
        scratch=(
            pltpu.VMEM((2048, 128), BF16),
            pltpu.VMEM((128, 128), BF16),
            pltpu.VMEM((1, 216), F32),
            pltpu.VMEM((1, 216), F32),
            pltpu.VMEM((1, 216), F32),
            pltpu.VMEM((2048, 128), F32),
            pltpu.VMEM((128, 128), F32),
            pltpu.SemaphoreType.DMA((5,)),
        ),
        space=pl.BlockSpec(memory_space=pltpu.HBM),
        params=pltpu.CompilerParams(vmem_limit_bytes=60 * 1024 * 1024),
    )
    before_x, after_x = exchange(up, down, GX)
    sibling = lax.ppermute(own, "y", [(0, 1), (1, 0), (2, 3), (3, 2)])
    message = lax.all_to_all(message, GX + GZ, 0, 0, tiled=True)
    bank = call(bank_rows, shape((128, 128), BF16), message)
    near_banks = turn(bank, 1), turn(bank, 3)
    up, down, beyond = call(
        y_messages, (along_y, along_y, shape((16, 640), F32)), slabs, before_x, after_x, message, *near_banks
    )
    before_y, after_y = turn(up, 1), turn(down, 3)
    keep, send = call(
        gradients,
        (shape((8, 8, 768), F32), shape((8, 8, 768), F32)),
        slabs,
        before_x,
        after_x,
        beyond,
        before_y,
        after_y,
        bank,
        *near_banks,
        narrow_band,
        pick,
        sibling,
        scratch=(
            pltpu.VMEM((640, 768), BF16),
            pltpu.VMEM((6, 48, 128), BF16),
            pltpu.VMEM((256, 512), F32),
            pltpu.VMEM((512, 128), F32),
            pltpu.VMEM((448, 128), F32),
        ),
    )
    sums = call(first_stage, shape((8, 8, 768), F32), keep, swap(send))
    sums = lax.all_to_all(sums, ("zl", "zh"), 0, 0, tiled=True)
    sums = call(second_stage, shape((16, 24, 128), F32), sums)
    sums = lax.all_to_all(sums, ("x", "y"), 0, 0, tiled=True)
    half = call(third_stage, shape((40, 128), F32), sums, own, sibling)
    one, rows = shape((1, 216), F32), shape((27, 128), F32)
    new = call(update, (one, one, one, rows, rows, rows), half, swap(half), own, *narrow)
    return tuple(w.reshape(-1) for w in new[3:] + new[:3])


def solution(mesh):
    parts = Mesh(mesh.devices.reshape(2, 4, 4, 4, 2), GX + GY + GZ)
    field = P(None, GX, GY, GZ)
    owned = P(GX + GY + GZ)
    return jax.shard_map(
        local,
        mesh=parts,
        in_specs=(field, field, P(), P(), P(), owned, owned, owned),
        out_specs=(P(), P(), P(), owned, owned, owned),
        check_vma=False,
    )
```

```python
import jax
import jax.numpy as jnp
from jax import lax
from jax.experimental import pallas as pl
from jax.experimental.pallas import tpu as pltpu
from jax.sharding import Mesh, PartitionSpec as P

CI = 4
C1 = 32
C2 = 64
F32 = jnp.float32
BF16 = jnp.bfloat16
GX = ("zl", "x")
GY = ("zh",)
GZ = ("y", "core")
PAST = ((3, 0), (2, 2))
VMEM = pl.BlockSpec(memory_space=pltpu.VMEM)
PARAMS = pltpu.CompilerParams(vmem_limit_bytes=32 * 1024 * 1024)


def dot(a, b):
    return lax.dot_general(a, b, (((1,), (0,)), ((), ())), preferred_element_type=F32)


def dot_nt(a, b):
    return lax.dot_general(a, b, (((1,), (1,)), ((), ())), preferred_element_type=F32)


def dot_tn(a, b):
    return lax.dot_general(a, b, (((0,), (0,)), ((), ())), preferred_element_type=F32)


def call(kernel, out_shapes, *args, scratch=(), space=VMEM, params=PARAMS):
    return pl.pallas_call(
        kernel,
        out_shape=out_shapes,
        in_specs=[space] * len(args),
        out_specs=jax.tree.map(lambda _: VMEM, out_shapes),
        scratch_shapes=scratch,
        compiler_params=params,
    )(*args)


def shape(dims, dtype):
    return jax.ShapeDtypeStruct(dims, dtype)


def roll(v, by):
    return pltpu.roll(v, by % v.shape[1], 1)


def lanes():
    return lax.broadcasted_iota(jnp.int32, (1, 128), 1)


def within(v, low, high):
    return jnp.where((lanes() >= low) & (lanes() < high), v, 0.0)


def two_rows(v):
    return [v[:, 0:128], jnp.concatenate([v[:, 128:216], jnp.zeros((1, 40), F32)], axis=1)]


def place(two, q):
    lane = lax.broadcasted_iota(jnp.int32, (1, 128), 1)
    row, at = divmod(216 * q, 128)
    one, last = roll(two[0:1], at), roll(jnp.where(lane < 88, two[1:2], 0.0), at)
    gap = jnp.zeros((1, 128), F32)
    pieces = [gap] * row + [
        jnp.where(lane >= at, one, 0.0),
        jnp.where(lane < at, one, 0.0) + jnp.where(lane >= at, last, 0.0),
        jnp.where(lane < at, last, 0.0),
    ]
    return jnp.concatenate((pieces + [gap] * 8)[:8], axis=0)


def take(block, q):
    lane = lax.broadcasted_iota(jnp.int32, (1, 128), 1)
    row, at = divmod(216 * q, 128)
    moved = [roll(block[r : r + 1], -at) for r in range(row, min(row + 3, 8))]
    one = jnp.where(lane < 128 - at, moved[0], moved[1])
    two = jnp.where(lane < 128 - at, moved[1], moved[2]) if len(moved) > 2 else moved[1]
    return jnp.concatenate([one, two], axis=0)


def along_gz():
    return lax.axis_index("y") * 2 + lax.axis_index("core")


def pack(
    cot_hbm, vol_hbm, w2_hbm, f2_hbm, s2_hbm, slab_ref, ahead_ref, out_ref, own_ref,
    cot_ref, vol_ref, w2_ref, f2_ref, s2_ref, cot32, vol32, sems,
):
    copies = [
        pltpu.make_async_copy(source, target, sems.at[i])
        for i, (source, target) in enumerate(
            ((cot_hbm, cot_ref), (vol_hbm, vol_ref), (w2_hbm, w2_ref), (f2_hbm, f2_ref), (s2_hbm, s2_ref))
        )
    ]
    for copy in copies:
        copy.start()
    for copy in copies:
        copy.wait()
    cot32[...] = cot_ref[...].astype(F32)
    vol32[...] = vol_ref[...].astype(F32)
    for x in range(4):
        for y in range(8):
            slab_ref[x, 64 * y : 64 * y + 64, :] = cot32[pl.ds(8 * x + y, 64, stride=32), :].astype(BF16)
        slab_ref[x, 512:544, :] = jnp.concatenate(
            [vol32[pl.ds(8 * x + y, 4, stride=32), :] for y in range(8)], axis=0
        ).astype(BF16)
    ahead_ref[...] = slab_ref[0:2]
    row = lax.broadcasted_iota(jnp.int32, (16, 512), 0)
    lane = lax.broadcasted_iota(jnp.int32, (16, 512), 1)
    pick = ((row < 4) & (lane == row * 128)) | ((row >= 4) & (row < 8) & (lane == row * 128 - 385))
    cells = jnp.concatenate([slab_ref[x] for x in range(4)], axis=1)
    cells = jnp.concatenate([cells, jnp.zeros((96, 512), BF16)], axis=0)
    edge = dot_nt(pick.astype(F32).astype(BF16), cells)
    own = [row for ref in (w2_ref, f2_ref, s2_ref) for row in two_rows(ref[...])]
    own_ref[...] = jnp.concatenate(own + [jnp.zeros((2, 128), F32)], axis=0)
    ends = []
    for side in range(2):
        at = slice(4 * side, 4 * side + 4)
        tail = edge[at, 512:640]
        tail = [sum(roll(tail[x : x + 1], 32 * x) for x in range(4))] + own[0:2] + [jnp.zeros((1, 128), F32)]
        ends.append(jnp.concatenate([edge[at, 128 * j : 128 * j + 128] for j in range(4)] + tail, axis=0))
    me = along_gz()
    for p in range(8):
        message = jnp.where(me < p, ends[1], ends[0]).astype(BF16)
        for x in range(8):
            for j in range(5):
                out_ref[8 * x + p, j] = message[4 * j : 4 * j + 4]


def bank_rows(in_ref, out_ref):
    rows = [in_ref[p, 4].astype(F32)[1:3] for p in range(64)]
    out_ref[...] = jnp.concatenate(rows, axis=0).astype(BF16)


def y_messages(slab_ref, next_ref, in_ref, nb_ref, pb_ref, up_ref, dn_ref, beyond_ref):
    slabs = [slab_ref.at[x] for x in range(4)] + [next_ref.at[x] for x in range(2)]
    first, last = [], []
    for xe, slab in enumerate(slabs):
        up_ref[xe * 64 : xe * 64 + 64, :] = slab[448:512, :]
        dn_ref[xe * 64 : xe * 64 + 64, :] = slab[0:64, :]
        vol = slab[512:544, :].astype(F32)
        first.append(vol[0:4])
        last.append(vol[28:32])
    fill = [jnp.zeros((8, 128), F32)]
    four = [jnp.zeros((4, 128), F32)]
    across, along = lax.axis_index("zl") * 4 + lax.axis_index("x"), along_gz()
    rows_up, rows_dn = [], []
    for side in range(2):
        other = along + 2 * side - 1
        inside = (other >= 0) & (other <= 7)
        other = jnp.clip(other, 0, 7)
        mid = jnp.where(inside, in_ref[8 * across + other].astype(F32), 0.0)
        after = jnp.where(inside, in_ref[8 * ((across + 1) % 8) + other].astype(F32), 0.0)
        parts = [jnp.concatenate([mid[j], after[j, 0:2]], axis=0) for j in range(4)]
        tail = [mid[4, 0:1]] * 4 + [after[4, 0:1]] * 2
        tail = [roll(row, -32 * x) for row, x in zip(tail, (0, 1, 2, 3, 0, 1), strict=True)]
        parts.append(within(jnp.concatenate(tail, axis=0), 0, 32))
        for j in range(5):
            beyond_ref[8 * side : 8 * side + 8, 128 * j : 128 * j + 128] = jnp.concatenate(
                [parts[j], jnp.zeros((2, 128), F32)], axis=0
            )
        rows_up.append(within(roll(parts[3], -64), 0, 64) + within(roll(parts[4], 36), 64, 68))
        rows_dn.append(within(parts[0], 0, 64) + within(roll(parts[4], 64), 64, 68))
    up_ref[384:432, :] = jnp.concatenate(last + fill + rows_up + four, axis=0).astype(BF16)
    dn_ref[384:432, :] = jnp.concatenate(first + fill + rows_dn + four, axis=0).astype(BF16)
    up_ref[432:496, :] = pb_ref[0:64, :]
    dn_ref[432:496, :] = nb_ref[64:128, :]


def assemble(slab_ref, next_ref, beyond_ref, yp_ref, yn_ref, e_ref, ve_ref, keep):
    slabs = [slab_ref.at[x] for x in range(4)] + [next_ref.at[x] for x in range(2)]
    along_y = lax.axis_index("zh")
    some, more = along_y > 0, along_y < 3
    before = jnp.where(some, yp_ref[384:432, :].astype(F32), 0.0)
    after = jnp.where(more, yn_ref[384:432, :].astype(F32), 0.0)
    for xe, slab in enumerate(slabs):
        rows = jnp.concatenate(
            [
                jnp.where(some, yp_ref[xe * 64 : xe * 64 + 64, :].astype(F32), 0.0).astype(BF16),
                slab[0:512, :],
                jnp.where(more, yn_ref[xe * 64 : xe * 64 + 64, :].astype(F32), 0.0).astype(BF16),
            ],
            axis=0,
        )
        for a in range(3):
            x = xe - a
            if 0 <= x < 4:
                value = (rows.astype(F32) * keep).astype(BF16) if (x, a) in PAST else rows
                e_ref[:, 512 * a + 128 * x : 512 * a + 128 * x + 128] = value
        vol = slab[512:544, :].astype(F32)
        ve_ref[xe] = jnp.concatenate(
            [before[xe * 4 : xe * 4 + 4], vol, after[xe * 4 : xe * 4 + 4], jnp.zeros((8, 128), F32)], axis=0
        ).astype(BF16)
    ends = []
    for side in range(2):
        parts = [roll(beyond_ref[8 * side : 8 * side + 6, 128 * j : 128 * j + 128], 64) for j in range(5)]
        prev = before[32 + 6 * side : 38 + 6 * side]
        nxt = after[32 + 6 * side : 38 + 6 * side]
        tiles = [within(prev, 0, 64) + within(parts[0], 64, 128)]
        for k in range(1, 4):
            tiles.append(jnp.where(lanes() < 64, parts[k - 1], parts[k]))
        tiles.append(within(parts[3], 0, 64) + within(roll(nxt, 64), 64, 128))
        tiles.append(
            within(roll(prev, -64), 0, 4) + within(roll(parts[4], -60), 4, 36) + within(roll(nxt, -28), 36, 40)
        )
        ends.append(
            jnp.concatenate([jnp.concatenate(tiles, axis=1), jnp.zeros((10, 768), F32)], axis=0).astype(BF16)
        )
    return ends


def flatten(narrow):
    lane = lax.broadcasted_iota(jnp.int32, (1, 128), 1)
    rows = [jnp.zeros((1, 128), F32) for _ in range(33)]
    for c in range(32):
        row, at = divmod(108 * c, 128)
        moved = roll(jnp.where(lane < 108, narrow[c : c + 1], 0.0), at)
        if at + 108 <= 128:
            rows[row] = rows[row] + moved
        else:
            rows[row] = rows[row] + jnp.where(lane >= at, moved, 0.0)
            rows[row + 1] = rows[row + 1] + jnp.where(lane < at, moved, 0.0)
    return jnp.concatenate(rows[:32], axis=0)


def turned(yp_ref, yn_ref, own_ref, pb_ref, nb_ref, rows_ref):
    me = lax.axis_index("zh")
    for by in range(4):
        zh = (me + by) % 4
        for across in range(8):
            at = pl.multiple_of(64 * across + 16 * zh, 16)
            if by == 2:
                ref, row = (yp_ref if across < 4 else yn_ref), 432 + 16 * (across % 4)
            else:
                ref, row = (own_ref, nb_ref, None, pb_ref)[by], 16 * across
            rows_ref[pl.ds(at, 16), :] = ref[row : row + 16, :].astype(F32)
    parts = []
    for q in range(4):
        parts.append(rows_ref[pl.ds(2 * q, 64, stride=8), :].T)
        parts.append(rows_ref[pl.ds(2 * q + 1, 64, stride=8), :].T[0:88])
    return jnp.concatenate(parts, axis=0).astype(BF16)


def narrow_lanes():
    row = lax.broadcasted_iota(jnp.int32, (512, 128), 0)
    col = lax.broadcasted_iota(jnp.int32, (512, 128), 1)
    group, inner = row // 48, row % 48
    a, c = group // 3, group % 3
    b, i = inner // 4, inner % 4
    return ((b < 3) & (group < 9) & (col == (9 * a + 3 * b + c) * 4 + i)).astype(F32)


def narrow_rows(w1_ref, out_ref, pick_ref):
    lane = lax.broadcasted_iota(jnp.int32, (1, 128), 1)
    rows = []
    for c in range(32):
        row, at = divmod(108 * c, 128)
        piece = roll(w1_ref[row : row + 1, :], -at)
        if at > 20:
            piece = jnp.where(lane < 128 - at, piece, roll(w1_ref[row + 1 : row + 2, :], -at))
        rows.append(jnp.where(lane < 108, piece, 0.0))
    bank = jnp.concatenate(rows, axis=0).astype(BF16)
    pick = narrow_lanes().astype(BF16)
    pick_ref[...] = pick
    first = dot_nt(bank, pick)
    for y in range(8):
        out_ref[32 * y : 32 * y + 32, :] = roll(first, 4 * y).astype(BF16)


def gradients(
    slab_ref, next_ref, beyond_ref, yp_ref, yn_ref, bank_ref, pb_ref, nb_ref, wb_ref, pick_ref, sib_ref,
    keep_ref, send_ref,
    e_ref, ve_ref, ga_ref, rows_ref, wide_ref,
):
    final = (lax.axis_index("zl") == 1) & (lax.axis_index("x") == 3)
    keep = jnp.where(final, 0.0, 1.0)
    ends = assemble(slab_ref, next_ref, beyond_ref, yp_ref, yn_ref, e_ref, ve_ref, keep)
    lane = lax.broadcasted_iota(jnp.int32, (1, 128), 1)
    low, high = lane == 0, lane == 127
    eye = (
        lax.broadcasted_iota(jnp.int32, (48, 128), 0) == lax.broadcasted_iota(jnp.int32, (48, 128), 1)
    ).astype(F32).astype(BF16)
    left = dot_nt(eye, ends[0][:, 640:768])
    right = dot_nt(eye, ends[1][:, 640:768])
    shifted = []
    for xe in range(6):
        v = ve_ref[xe].astype(F32)
        shifted.append(
            (
                jnp.where(low, left[:, xe : xe + 1], roll(v, 1)).astype(BF16),
                ve_ref[xe],
                jnp.where(high, right[:, xe : xe + 1], roll(v, -1)).astype(BF16),
            )
        )
    rest = jnp.zeros((80, 128), BF16)
    patches = jnp.concatenate(
        [
            jnp.concatenate(
                [
                    (shifted[x + a][c].astype(F32) * keep).astype(BF16) if (x, a) in PAST else shifted[x + a][c]
                    for a in range(3)
                    for c in range(3)
                ]
                + [rest],
                axis=0,
            )
            for x in range(4)
        ],
        axis=1,
    )
    pre = dot(wb_ref[...], patches)
    sig = 1.0 / (1.0 + jnp.exp(-pre))
    act = (pre * sig).astype(BF16)
    slope = sig * (1.0 + pre * (1.0 - sig))
    halos = []
    for end in ends:
        m = end[:, 0:640].astype(F32)
        by_a = []
        for a in range(3):
            rows = m[a : a + 4]
            if a != 1:
                row = lax.broadcasted_iota(jnp.int32, (4, 1), 0)
                rows = rows * jnp.where(row == (3 if a == 0 else 2), keep, 1.0)
            by_a.append(rows)
        halos.append(
            jnp.concatenate(
                [
                    jnp.concatenate([rows[:, 128 * k : 128 * k + 256] for rows in by_a], axis=1)
                    for k in range(4)
                ],
                axis=0,
            ).astype(BF16)
        )
    none = jnp.zeros((32, 64), BF16)
    weights = turned(yp_ref, yn_ref, bank_ref, pb_ref, nb_ref, rows_ref)
    blocks = []
    for c in range(3):
        for yl in range(2):
            cells = []
            for a in range(3):
                for yp in range(4):
                    b = yp - yl
                    if 0 <= b <= 2:
                        tap = (2 - a) * 9 + (2 - b) * 3 + (2 - c)
                        cells.append(weights[tap * 32 : tap * 32 + 32])
                    else:
                        cells.append(none)
            blocks.append(jnp.concatenate(cells, axis=1))
    bank = jnp.concatenate(blocks, axis=0)
    from_left = dot_nt(bank[0:64], halos[0])
    from_right = dot_nt(bank[128:192], halos[1])
    for k in range(4):
        for xp in range(2):
            v = sum(
                dot(
                    bank[:, 256 * a : 256 * a + 256],
                    e_ref[128 * k : 128 * k + 256, 512 * a + 256 * xp : 512 * a + 256 * xp + 256],
                )
                for a in range(3)
            )
            for j in range(2):
                x = 2 * xp + j
                at = slice(128 * j, 128 * j + 128)
                col = 4 * k + x
                ga_ref[64 * k : 64 * k + 64, 128 * x : 128 * x + 128] = (
                    v[64:128, at]
                    + jnp.where(low, from_left[:, col : col + 1], roll(v[0:64, at], 1))
                    + jnp.where(high, from_right[:, col : col + 1], roll(v[128:192, at], -1))
                )
    grad_pre = (ga_ref[...] * slope).astype(BF16)
    product = dot_nt(grad_pre, patches)
    total = product[0:32]
    for y in range(1, 8):
        total = total + roll(product[32 * y : 32 * y + 32], -4 * y)
    split, rest = [], total
    for _ in range(3):
        split.append(rest.astype(BF16))
        rest = rest - split[-1].astype(F32)
    picked = dot(jnp.concatenate(split, axis=0), pick_ref[...])
    narrow = picked[0:32] + (picked[32:64] + picked[64:96])
    act32 = act.astype(F32)
    before, after = [], []
    for x in range(4):
        part = act32[:, 128 * x : 128 * x + 128]
        before.append(jnp.where(low, 0.0, roll(part, 1)).astype(BF16))
        after.append(jnp.where(high, 0.0, roll(part, -1)).astype(BF16))
    before = jnp.concatenate(before, axis=1)
    after = jnp.concatenate(after, axis=1)
    empty = jnp.zeros((32, 512), BF16)
    rows = []
    for k in range(4):
        parts = []
        for yl in range(2):
            at = slice(64 * k + 32 * yl, 64 * k + 32 * yl + 32)
            parts += [before[at], act[at], after[at], empty]
        rows.append(jnp.concatenate(parts, axis=0))
    wide = jnp.concatenate(
        [
            sum(
                dot_nt(e_ref[128 * k : 128 * k + 256, 512 * a : 512 * a + 512], rows[k])
                for k in range(4)
            )
            for a in range(3)
        ],
        axis=0,
    )
    row = lax.broadcasted_iota(jnp.int32, (16, 512), 0)
    lanes = lax.broadcasted_iota(jnp.int32, (16, 512), 1)
    pick = ((row < 4) & (lanes == row * 128)) | ((row >= 4) & (row < 8) & (lanes == (row - 4) * 128 + 127))
    edges = dot_nt(pick.astype(F32).astype(BF16), act)
    gap = jnp.zeros((4, 64), F32)
    one = jnp.zeros((4, 32), F32)
    table = []
    for k in range(4):
        e0 = edges[0:4, 64 * k : 64 * k + 32]
        e1 = edges[0:4, 64 * k + 32 : 64 * k + 64]
        table.append(jnp.concatenate([gap, e0, one, gap, e1, one], axis=1))
    for k in range(4):
        e0 = edges[4:8, 64 * k : 64 * k + 32]
        e1 = edges[4:8, 64 * k + 32 : 64 * k + 64]
        table.append(jnp.concatenate([e0, one, gap, e1, one, gap], axis=1))
    table = jnp.concatenate(table, axis=0).astype(BF16)
    wide = wide + dot_tn(jnp.concatenate(halos, axis=0), table)
    taps = []
    for a in range(3):
        for b in range(3):
            at = (2 - a) * 256 + (2 - b) * 64
            taps.append((wide[at : at + 64, 0:128] + wide[at + 64 : at + 128, 128:256])[:, 0:96])
    wide = jnp.concatenate(taps + [jnp.zeros((64, 32), F32)], axis=1)
    flat = flatten(narrow)
    for j in range(7):
        wide_ref[64 * j : 64 * j + 64, :] = wide[:, 128 * j : 128 * j + 128]
    core = lax.axis_index("core")
    for p in range(8):
        zl, zh = p // 4, p % 4
        halves = []
        for yh in range(2):
            rows = [wide_ref[pl.ds(64 * j + 32 * zl + 2 * zh + yh, 4, stride=8), :] for j in range(7)]
            halves.append(jnp.concatenate(rows + [flat[14 * yh : 14 * yh + 14]], axis=0))
        keep_ref[p] = jnp.where(core == 0, halves[0], halves[1])
        send_ref[p] = jnp.where(core == 0, halves[1], halves[0])


def first_stage(a_ref, b_ref, out_ref):
    out_ref[...] = a_ref[...] + b_ref[...]


def second_stage(in_ref, out_ref):
    total = in_ref[0]
    for p in range(1, 8):
        total = total + in_ref[p]
    for x in range(4):
        block = [total[4 * j + x : 4 * j + x + 1] for j in range(7)]
        rows = jnp.concatenate(block + [total[28:42]], axis=0)
        for y in range(4):
            out_ref[4 * x + y] = rows


def third_stage(in_ref, own_ref, sib_ref, out_ref):
    total = in_ref[0]
    for p in range(1, 16):
        total = total + in_ref[p]
    gap = [jnp.zeros((1, 128), F32)]
    out_ref[0:24, :] = jnp.concatenate([total[0:7]] + gap + [total[7:21]] + gap + gap, axis=0)
    even = lax.axis_index("y") % 2 == 0
    own, sib = own_ref[...], sib_ref[...]
    out_ref[24:32, :] = jnp.where(even, own, sib)
    out_ref[32:40, :] = jnp.where(even, sib, own)


def moments(master, first, second, grad):
    first_new = 0.9 * first + 0.1 * grad
    second_new = 0.999 * second + 0.001 * grad * grad
    direction = (
        first_new / (1.0 - 0.9**10) / (jnp.sqrt(second_new / (1.0 - 0.999**10)) + 1e-06)
        + 0.01 * master
    )
    return (first_new, second_new, direction)


def runs():
    row = lax.broadcasted_iota(jnp.int32, (27, 128), 0)
    lane = lax.broadcasted_iota(jnp.int32, (27, 128), 1)
    start = (row * 128) // 108
    run = (row * 128 + lane) // 108
    return [(run == start + p, lane == start + p) for p in range(3)]


def run_sums(value):
    total = jnp.zeros((27, 128), F32)
    for inside, column in runs():
        part = jnp.sum(jnp.where(inside, value, 0.0), axis=1, keepdims=True)
        total = total + jnp.where(column, part, 0.0)
    return jnp.sum(total, axis=0, keepdims=True)


def run_spread(value):
    total = jnp.zeros((27, 128), F32)
    for inside, column in runs():
        part = jnp.sum(jnp.where(column, value, 0.0), axis=1, keepdims=True)
        total = total + jnp.where(inside, part, 0.0)
    return total


def update(in_ref, other_ref, own_ref, m_ref, f_ref, s_ref, w2_ref, f2_ref, s2_ref, w1_ref, f1_ref, s1_ref):
    y, core = lax.axis_index("y"), lax.axis_index("core")
    quarter = y % 2 * 2 + core
    mine, other = in_ref[...], other_ref[...]
    low, high = jnp.where(core == 0, mine, other), jnp.where(core == 0, other, mine)
    grad = jnp.where(y // 2 == 0, low[0:8], high[0:8])
    inside = (
        lax.broadcasted_iota(jnp.int32, (8, 128), 0) * 128 + lax.broadcasted_iota(jnp.int32, (8, 128), 1)
    ) < 864
    block = []
    for j in range(3):
        parts = [half[at + 2 * j : at + 2 * j + 2] for at in (24, 32) for half in (low, high)]
        block.append(sum(place(part, q) for q, part in enumerate(parts)))
    _, _, direction = moments(block[0], block[1], block[2], grad)
    direction = jnp.where(inside, direction, 0.0)
    ratio = jnp.sqrt(jnp.sum(block[0] * block[0], keepdims=True)) / (
        jnp.sqrt(jnp.sum(direction * direction, keepdims=True)) + 1e-06
    )
    mine = take(grad, 0)
    for q in range(1, 4):
        mine = jnp.where(quarter == q, take(grad, q), mine)
    master, first, second = (own_ref[2 * j : 2 * j + 2] for j in range(3))
    first_new, second_new, direction = moments(master, first, second, mine)
    for ref, value in (
        (w2_ref, master - 0.01 * (ratio * direction)),
        (f2_ref, first_new),
        (s2_ref, second_new),
    ):
        ref[...] = jnp.concatenate([value[0:1], value[1:2, 0:88]], axis=1)
    grad = jnp.concatenate([low[8:22], high[8:22]], axis=0)[0:27]
    master = m_ref[...]
    first_new, second_new, direction = moments(master, f_ref[...], s_ref[...], grad)
    ratio = jnp.sqrt(run_sums(master * master)) / (jnp.sqrt(run_sums(direction * direction)) + 1e-06)
    w1_ref[...] = master - 0.01 * (run_spread(ratio) * direction)
    f1_ref[...] = first_new
    s1_ref[...] = second_new


def turn(value, by):
    return lax.ppermute(value, GY, [(i, (i + by) % 4) for i in range(4)])


def swap(value):
    return lax.ppermute(value, "core", [(0, 1), (1, 0)])


def local(volume, cotangent, w1_master, w1_first, w1_second, w2_master, w2_first, w2_second):
    wide = [w.reshape(1, 216) for w in (w2_master, w2_first, w2_second)]
    narrow = [w.reshape(27, 128) for w in (w1_master, w1_first, w1_second)]
    narrow_band, pick = call(narrow_rows, (shape((256, 512), BF16), shape((512, 128), BF16)), narrow[0])
    along_y = shape((496, 128), BF16)
    slabs, ahead, message, own = call(
        pack,
        (shape((4, 544, 128), BF16), shape((2, 544, 128), BF16), shape((64, 5, 4, 128), BF16), shape((8, 128), F32)),
        cotangent.reshape(2048, 128),
        volume.reshape(128, 128),
        *wide,
        scratch=(
            pltpu.VMEM((2048, 128), BF16),
            pltpu.VMEM((128, 128), BF16),
            pltpu.VMEM((1, 216), F32),
            pltpu.VMEM((1, 216), F32),
            pltpu.VMEM((1, 216), F32),
            pltpu.VMEM((2048, 128), F32),
            pltpu.VMEM((128, 128), F32),
            pltpu.SemaphoreType.DMA((5,)),
        ),
        space=pl.BlockSpec(memory_space=pltpu.HBM),
        params=pltpu.CompilerParams(vmem_limit_bytes=60 * 1024 * 1024),
    )
    next_x = lax.ppermute(ahead, GX, [(i, (i + 7) % 8) for i in range(8)])
    sibling = lax.ppermute(own, "y", [(0, 1), (1, 0), (2, 3), (3, 2)])
    message = lax.all_to_all(message, GX + GZ, 0, 0, tiled=True)
    bank = call(bank_rows, shape((128, 128), BF16), message)
    near_banks = turn(bank, 1), turn(bank, 3)
    up, down, beyond = call(
        y_messages, (along_y, along_y, shape((16, 640), F32)), slabs, next_x, message, *near_banks[::-1]
    )
    before_y, after_y = turn(up, 1), turn(down, 3)
    keep, send = call(
        gradients,
        (shape((8, 42, 128), F32), shape((8, 42, 128), F32)),
        slabs,
        next_x,
        beyond,
        before_y,
        after_y,
        bank,
        *near_banks,
        narrow_band,
        pick,
        sibling,
        scratch=(
            pltpu.VMEM((640, 1536), BF16),
            pltpu.VMEM((6, 48, 128), BF16),
            pltpu.VMEM((256, 512), F32),
            pltpu.VMEM((512, 128), F32),
            pltpu.VMEM((448, 128), F32),
        ),
    )
    sums = call(first_stage, shape((8, 42, 128), F32), keep, swap(send))
    sums = lax.all_to_all(sums, ("zl", "zh"), 0, 0, tiled=True)
    sums = call(second_stage, shape((16, 21, 128), F32), sums)
    sums = lax.all_to_all(sums, ("x", "y"), 0, 0, tiled=True)
    half = call(third_stage, shape((40, 128), F32), sums, own, sibling)
    one, rows = shape((1, 216), F32), shape((27, 128), F32)
    new = call(update, (one, one, one, rows, rows, rows), half, swap(half), own, *narrow)
    return tuple(w.reshape(-1) for w in new[3:] + new[:3])


def solution(mesh):
    parts = Mesh(mesh.devices.reshape(2, 4, 4, 4, 2), GX + GY + GZ)
    field = P(None, GX, GY, GZ)
    owned = P(GX + GY + GZ)
    return jax.shard_map(
        local,
        mesh=parts,
        in_specs=(field, field, P(), P(), P(), owned, owned, owned),
        out_specs=(P(), P(), P(), owned, owned, owned),
        check_vma=False,
    )
```

```python
import jax
import jax.numpy as jnp
from jax import lax
from jax.experimental import pallas as pl
from jax.experimental.pallas import tpu as pltpu
from jax.sharding import Mesh, PartitionSpec as P

CI = 4
C1 = 32
C2 = 64
F32 = jnp.float32
BF16 = jnp.bfloat16
GX = ("zl", "x")
GY = ("zh",)
GZ = ("y", "core")
PAST = ((3, 0), (2, 2))
VMEM = pl.BlockSpec(memory_space=pltpu.VMEM)
PARAMS = pltpu.CompilerParams(vmem_limit_bytes=32 * 1024 * 1024)


def dot(a, b):
    return lax.dot_general(a, b, (((1,), (0,)), ((), ())), preferred_element_type=F32)


def dot_nt(a, b):
    return lax.dot_general(a, b, (((1,), (1,)), ((), ())), preferred_element_type=F32)


def dot_tn(a, b):
    return lax.dot_general(a, b, (((0,), (0,)), ((), ())), preferred_element_type=F32)


def call(kernel, out_shapes, *args, scratch=(), space=VMEM, params=PARAMS):
    return pl.pallas_call(
        kernel,
        out_shape=out_shapes,
        in_specs=[space] * len(args),
        out_specs=jax.tree.map(lambda _: VMEM, out_shapes),
        scratch_shapes=scratch,
        compiler_params=params,
    )(*args)


def shape(dims, dtype):
    return jax.ShapeDtypeStruct(dims, dtype)


def roll(v, by):
    return pltpu.roll(v, by % v.shape[1], 1)


def lanes():
    return lax.broadcasted_iota(jnp.int32, (1, 128), 1)


def within(v, low, high):
    return jnp.where((lanes() >= low) & (lanes() < high), v, 0.0)


def two_rows(v):
    return [v[:, 0:128], jnp.concatenate([v[:, 128:216], jnp.zeros((1, 40), F32)], axis=1)]


def place(two, q):
    lane = lax.broadcasted_iota(jnp.int32, (1, 128), 1)
    row, at = divmod(216 * q, 128)
    one, last = roll(two[0:1], at), roll(jnp.where(lane < 88, two[1:2], 0.0), at)
    gap = jnp.zeros((1, 128), F32)
    pieces = [gap] * row + [
        jnp.where(lane >= at, one, 0.0),
        jnp.where(lane < at, one, 0.0) + jnp.where(lane >= at, last, 0.0),
        jnp.where(lane < at, last, 0.0),
    ]
    return jnp.concatenate((pieces + [gap] * 8)[:8], axis=0)


def take(block, q):
    lane = lax.broadcasted_iota(jnp.int32, (1, 128), 1)
    row, at = divmod(216 * q, 128)
    moved = [roll(block[r : r + 1], -at) for r in range(row, min(row + 3, 8))]
    one = jnp.where(lane < 128 - at, moved[0], moved[1])
    two = jnp.where(lane < 128 - at, moved[1], moved[2]) if len(moved) > 2 else moved[1]
    return jnp.concatenate([one, two], axis=0)


def along_gz():
    return lax.axis_index("y") * 2 + lax.axis_index("core")


def pack(
    cot_hbm, vol_hbm, w2_hbm, f2_hbm, s2_hbm, slab_ref, ahead_ref, out_ref, own_ref,
    cot_ref, vol_ref, w2_ref, f2_ref, s2_ref, cot32, vol32, sems,
):
    copies = [
        pltpu.make_async_copy(source, target, sems.at[i])
        for i, (source, target) in enumerate(
            ((cot_hbm, cot_ref), (vol_hbm, vol_ref), (w2_hbm, w2_ref), (f2_hbm, f2_ref), (s2_hbm, s2_ref))
        )
    ]
    for copy in copies:
        copy.start()
    for copy in copies:
        copy.wait()
    cot32[...] = cot_ref[...].astype(F32)
    vol32[...] = vol_ref[...].astype(F32)
    for x in range(4):
        for y in range(8):
            slab_ref[x, 64 * y : 64 * y + 64, :] = cot32[pl.ds(8 * x + y, 64, stride=32), :].astype(BF16)
        slab_ref[x, 512:544, :] = jnp.concatenate(
            [vol32[pl.ds(8 * x + y, 4, stride=32), :] for y in range(8)], axis=0
        ).astype(BF16)
    ahead_ref[...] = slab_ref[0:2]
    row = lax.broadcasted_iota(jnp.int32, (16, 512), 0)
    lane = lax.broadcasted_iota(jnp.int32, (16, 512), 1)
    pick = ((row < 4) & (lane == row * 128)) | ((row >= 4) & (row < 8) & (lane == row * 128 - 385))
    cells = jnp.concatenate([slab_ref[x] for x in range(4)], axis=1)
    cells = jnp.concatenate([cells, jnp.zeros((96, 512), BF16)], axis=0)
    edge = dot_nt(pick.astype(F32).astype(BF16), cells)
    own = [row for ref in (w2_ref, f2_ref, s2_ref) for row in two_rows(ref[...])]
    own_ref[...] = jnp.concatenate(own + [jnp.zeros((2, 128), F32)], axis=0)
    ends = []
    for side in range(2):
        at = slice(4 * side, 4 * side + 4)
        tail = edge[at, 512:640]
        tail = [sum(roll(tail[x : x + 1], 32 * x) for x in range(4))] + own[0:2] + [jnp.zeros((1, 128), F32)]
        ends.append(jnp.concatenate([edge[at, 128 * j : 128 * j + 128] for j in range(4)] + tail, axis=0))
    me = along_gz()
    for p in range(8):
        message = jnp.where(me < p, ends[1], ends[0]).astype(BF16)
        for x in range(8):
            for j in range(5):
                out_ref[8 * x + p, j] = message[4 * j : 4 * j + 4]


def bank_rows(in_ref, out_ref):
    rows = [in_ref[p, 4].astype(F32)[1:3] for p in range(64)]
    out_ref[...] = jnp.concatenate(rows, axis=0).astype(BF16)


def y_messages(slab_ref, next_ref, in_ref, pb_ref, nb_ref, up_ref, dn_ref, beyond_ref):
    slabs = [slab_ref.at[x] for x in range(4)] + [next_ref.at[x] for x in range(2)]
    first, last = [], []
    for xe, slab in enumerate(slabs):
        up_ref[xe * 64 : xe * 64 + 64, :] = slab[448:512, :]
        dn_ref[xe * 64 : xe * 64 + 64, :] = slab[0:64, :]
        vol = slab[512:544, :].astype(F32)
        first.append(vol[0:4])
        last.append(vol[28:32])
    fill = [jnp.zeros((8, 128), F32)]
    four = [jnp.zeros((4, 128), F32)]
    across, along = lax.axis_index("zl") * 4 + lax.axis_index("x"), along_gz()
    rows_up, rows_dn = [], []
    for side in range(2):
        other = along + 2 * side - 1
        inside = (other >= 0) & (other <= 7)
        other = jnp.clip(other, 0, 7)
        mid = jnp.where(inside, in_ref[8 * across + other].astype(F32), 0.0)
        after = jnp.where(inside, in_ref[8 * ((across + 1) % 8) + other].astype(F32), 0.0)
        parts = [jnp.concatenate([mid[j], after[j, 0:2]], axis=0) for j in range(4)]
        tail = [mid[4, 0:1]] * 4 + [after[4, 0:1]] * 2
        tail = [roll(row, -32 * x) for row, x in zip(tail, (0, 1, 2, 3, 0, 1), strict=True)]
        parts.append(within(jnp.concatenate(tail, axis=0), 0, 32))
        for j in range(5):
            beyond_ref[8 * side : 8 * side + 8, 128 * j : 128 * j + 128] = jnp.concatenate(
                [parts[j], jnp.zeros((2, 128), F32)], axis=0
            )
        rows_up.append(within(roll(parts[3], -64), 0, 64) + within(roll(parts[4], 36), 64, 68))
        rows_dn.append(within(parts[0], 0, 64) + within(roll(parts[4], 64), 64, 68))
    up_ref[384:432, :] = jnp.concatenate(last + fill + rows_up + four, axis=0).astype(BF16)
    dn_ref[384:432, :] = jnp.concatenate(first + fill + rows_dn + four, axis=0).astype(BF16)
    up_ref[432:496, :] = pb_ref[0:64, :]
    dn_ref[432:496, :] = nb_ref[64:128, :]


def assemble(slab_ref, next_ref, beyond_ref, yp_ref, yn_ref, e_ref, ve_ref, keep):
    slabs = [slab_ref.at[x] for x in range(4)] + [next_ref.at[x] for x in range(2)]
    along_y = lax.axis_index("zh")
    some, more = along_y > 0, along_y < 3
    before = jnp.where(some, yp_ref[384:432, :].astype(F32), 0.0)
    after = jnp.where(more, yn_ref[384:432, :].astype(F32), 0.0)
    for xe, slab in enumerate(slabs):
        rows = jnp.concatenate(
            [
                jnp.where(some, yp_ref[xe * 64 : xe * 64 + 64, :].astype(F32), 0.0).astype(BF16),
                slab[0:512, :],
                jnp.where(more, yn_ref[xe * 64 : xe * 64 + 64, :].astype(F32), 0.0).astype(BF16),
            ],
            axis=0,
        )
        for a in range(3):
            x = xe - a
            if 0 <= x < 4:
                value = (rows.astype(F32) * keep).astype(BF16) if (x, a) in PAST else rows
                e_ref[:, 512 * a + 128 * x : 512 * a + 128 * x + 128] = value
        vol = slab[512:544, :].astype(F32)
        ve_ref[xe] = jnp.concatenate(
            [before[xe * 4 : xe * 4 + 4], vol, after[xe * 4 : xe * 4 + 4], jnp.zeros((8, 128), F32)], axis=0
        ).astype(BF16)
    ends = []
    for side in range(2):
        parts = [roll(beyond_ref[8 * side : 8 * side + 6, 128 * j : 128 * j + 128], 64) for j in range(5)]
        prev = before[32 + 6 * side : 38 + 6 * side]
        nxt = after[32 + 6 * side : 38 + 6 * side]
        tiles = [within(prev, 0, 64) + within(parts[0], 64, 128)]
        for k in range(1, 4):
            tiles.append(jnp.where(lanes() < 64, parts[k - 1], parts[k]))
        tiles.append(within(parts[3], 0, 64) + within(roll(nxt, 64), 64, 128))
        tiles.append(
            within(roll(prev, -64), 0, 4) + within(roll(parts[4], -60), 4, 36) + within(roll(nxt, -28), 36, 40)
        )
        ends.append(
            jnp.concatenate([jnp.concatenate(tiles, axis=1), jnp.zeros((10, 768), F32)], axis=0).astype(BF16)
        )
    return ends


def flatten(narrow):
    lane = lax.broadcasted_iota(jnp.int32, (1, 128), 1)
    rows = [jnp.zeros((1, 128), F32) for _ in range(33)]
    for c in range(32):
        row, at = divmod(108 * c, 128)
        moved = roll(jnp.where(lane < 108, narrow[c : c + 1], 0.0), at)
        if at + 108 <= 128:
            rows[row] = rows[row] + moved
        else:
            rows[row] = rows[row] + jnp.where(lane >= at, moved, 0.0)
            rows[row + 1] = rows[row + 1] + jnp.where(lane < at, moved, 0.0)
    return jnp.concatenate(rows[:32], axis=0)


def turned(yp_ref, yn_ref, own_ref, pb_ref, nb_ref, rows_ref):
    me = lax.axis_index("zh")
    for by in range(4):
        zh = (me + by) % 4
        for across in range(8):
            at = pl.multiple_of(64 * across + 16 * zh, 16)
            if by == 2:
                ref, row = (yp_ref if across < 4 else yn_ref), 432 + 16 * (across % 4)
            else:
                ref, row = (own_ref, nb_ref, None, pb_ref)[by], 16 * across
            rows_ref[pl.ds(at, 16), :] = ref[row : row + 16, :].astype(F32)
    parts = []
    for q in range(4):
        parts.append(rows_ref[pl.ds(2 * q, 64, stride=8), :].T)
        parts.append(rows_ref[pl.ds(2 * q + 1, 64, stride=8), :].T[0:88])
    return jnp.concatenate(parts, axis=0).astype(BF16)


def narrow_lanes():
    row = lax.broadcasted_iota(jnp.int32, (512, 128), 0)
    col = lax.broadcasted_iota(jnp.int32, (512, 128), 1)
    group, inner = row // 48, row % 48
    a, c = group // 3, group % 3
    b, i = inner // 4, inner % 4
    return ((b < 3) & (group < 9) & (col == (9 * a + 3 * b + c) * 4 + i)).astype(F32)


def narrow_rows(w1_ref, out_ref, pick_ref):
    lane = lax.broadcasted_iota(jnp.int32, (1, 128), 1)
    rows = []
    for c in range(32):
        row, at = divmod(108 * c, 128)
        piece = roll(w1_ref[row : row + 1, :], -at)
        if at > 20:
            piece = jnp.where(lane < 128 - at, piece, roll(w1_ref[row + 1 : row + 2, :], -at))
        rows.append(jnp.where(lane < 108, piece, 0.0))
    bank = jnp.concatenate(rows, axis=0).astype(BF16)
    pick = narrow_lanes().astype(BF16)
    pick_ref[...] = pick
    first = dot_nt(bank, pick)
    for y in range(8):
        out_ref[32 * y : 32 * y + 32, :] = roll(first, 4 * y).astype(BF16)


def gradients(
    slab_ref, next_ref, beyond_ref, yn_ref, yp_ref, bank_ref, pb_ref, nb_ref, wb_ref, pick_ref, sib_ref,
    keep_ref, send_ref,
    e_ref, ve_ref, ga_ref, rows_ref, wide_ref,
):
    final = (lax.axis_index("zl") == 1) & (lax.axis_index("x") == 3)
    keep = jnp.where(final, 0.0, 1.0)
    ends = assemble(slab_ref, next_ref, beyond_ref, yp_ref, yn_ref, e_ref, ve_ref, keep)
    lane = lax.broadcasted_iota(jnp.int32, (1, 128), 1)
    low, high = lane == 0, lane == 127
    eye = (
        lax.broadcasted_iota(jnp.int32, (48, 128), 0) == lax.broadcasted_iota(jnp.int32, (48, 128), 1)
    ).astype(F32).astype(BF16)
    left = dot_nt(eye, ends[0][:, 640:768])
    right = dot_nt(eye, ends[1][:, 640:768])
    shifted = []
    for xe in range(6):
        v = ve_ref[xe].astype(F32)
        shifted.append(
            (
                jnp.where(low, left[:, xe : xe + 1], roll(v, 1)).astype(BF16),
                ve_ref[xe],
                jnp.where(high, right[:, xe : xe + 1], roll(v, -1)).astype(BF16),
            )
        )
    rest = jnp.zeros((80, 128), BF16)
    patches = jnp.concatenate(
        [
            jnp.concatenate(
                [
                    (shifted[x + a][c].astype(F32) * keep).astype(BF16) if (x, a) in PAST else shifted[x + a][c]
                    for a in range(3)
                    for c in range(3)
                ]
                + [rest],
                axis=0,
            )
            for x in range(4)
        ],
        axis=1,
    )
    pre = dot(wb_ref[...], patches)
    sig = 1.0 / (1.0 + jnp.exp(-pre))
    act = (pre * sig).astype(BF16)
    slope = sig * (1.0 + pre * (1.0 - sig))
    halos = []
    for end in ends:
        m = end[:, 0:640].astype(F32)
        by_a = []
        for a in range(3):
            rows = m[a : a + 4]
            if a != 1:
                row = lax.broadcasted_iota(jnp.int32, (4, 1), 0)
                rows = rows * jnp.where(row == (3 if a == 0 else 2), keep, 1.0)
            by_a.append(rows)
        halos.append(
            jnp.concatenate(
                [
                    jnp.concatenate([rows[:, 128 * k : 128 * k + 256] for rows in by_a], axis=1)
                    for k in range(4)
                ],
                axis=0,
            ).astype(BF16)
        )
    none = jnp.zeros((32, 64), BF16)
    weights = turned(yp_ref, yn_ref, bank_ref, pb_ref, nb_ref, rows_ref)
    blocks = []
    for c in range(3):
        for yl in range(2):
            cells = []
            for a in range(3):
                for yp in range(4):
                    b = yp - yl
                    if 0 <= b <= 2:
                        tap = (2 - a) * 9 + (2 - b) * 3 + (2 - c)
                        cells.append(weights[tap * 32 : tap * 32 + 32])
                    else:
                        cells.append(none)
            blocks.append(jnp.concatenate(cells, axis=1))
    bank = jnp.concatenate(blocks, axis=0)
    from_left = dot_nt(bank[0:64], halos[0])
    from_right = dot_nt(bank[128:192], halos[1])
    for k in range(4):
        for xp in range(2):
            v = sum(
                dot(
                    bank[:, 256 * a : 256 * a + 256],
                    e_ref[128 * k : 128 * k + 256, 512 * a + 256 * xp : 512 * a + 256 * xp + 256],
                )
                for a in range(3)
            )
            for j in range(2):
                x = 2 * xp + j
                at = slice(128 * j, 128 * j + 128)
                col = 4 * k + x
                ga_ref[64 * k : 64 * k + 64, 128 * x : 128 * x + 128] = (
                    v[64:128, at]
                    + jnp.where(low, from_left[:, col : col + 1], roll(v[0:64, at], 1))
                    + jnp.where(high, from_right[:, col : col + 1], roll(v[128:192, at], -1))
                )
    grad_pre = (ga_ref[...] * slope).astype(BF16)
    product = dot_nt(grad_pre, patches)
    total = product[0:32]
    for y in range(1, 8):
        total = total + roll(product[32 * y : 32 * y + 32], -4 * y)
    split, rest = [], total
    for _ in range(3):
        split.append(rest.astype(BF16))
        rest = rest - split[-1].astype(F32)
    picked = dot(jnp.concatenate(split, axis=0), pick_ref[...])
    narrow = picked[0:32] + (picked[32:64] + picked[64:96])
    act32 = act.astype(F32)
    before, after = [], []
    for x in range(4):
        part = act32[:, 128 * x : 128 * x + 128]
        before.append(jnp.where(low, 0.0, roll(part, 1)).astype(BF16))
        after.append(jnp.where(high, 0.0, roll(part, -1)).astype(BF16))
    before = jnp.concatenate(before, axis=1)
    after = jnp.concatenate(after, axis=1)
    empty = jnp.zeros((32, 512), BF16)
    rows = []
    for k in range(4):
        parts = []
        for yl in range(2):
            at = slice(64 * k + 32 * yl, 64 * k + 32 * yl + 32)
            parts += [before[at], act[at], after[at], empty]
        rows.append(jnp.concatenate(parts, axis=0))
    wide = jnp.concatenate(
        [
            sum(
                dot_nt(e_ref[128 * k : 128 * k + 256, 512 * a : 512 * a + 512], rows[k])
                for k in range(4)
            )
            for a in range(3)
        ],
        axis=0,
    )
    row = lax.broadcasted_iota(jnp.int32, (16, 512), 0)
    lanes = lax.broadcasted_iota(jnp.int32, (16, 512), 1)
    pick = ((row < 4) & (lanes == row * 128)) | ((row >= 4) & (row < 8) & (lanes == (row - 4) * 128 + 127))
    edges = dot_nt(pick.astype(F32).astype(BF16), act)
    gap = jnp.zeros((4, 64), F32)
    one = jnp.zeros((4, 32), F32)
    table = []
    for k in range(4):
        e0 = edges[0:4, 64 * k : 64 * k + 32]
        e1 = edges[0:4, 64 * k + 32 : 64 * k + 64]
        table.append(jnp.concatenate([gap, e0, one, gap, e1, one], axis=1))
    for k in range(4):
        e0 = edges[4:8, 64 * k : 64 * k + 32]
        e1 = edges[4:8, 64 * k + 32 : 64 * k + 64]
        table.append(jnp.concatenate([e0, one, gap, e1, one, gap], axis=1))
    table = jnp.concatenate(table, axis=0).astype(BF16)
    wide = wide + dot_tn(jnp.concatenate(halos, axis=0), table)
    taps = []
    for a in range(3):
        for b in range(3):
            at = (2 - a) * 256 + (2 - b) * 64
            taps.append((wide[at : at + 64, 0:128] + wide[at + 64 : at + 128, 128:256])[:, 0:96])
    wide = jnp.concatenate(taps + [jnp.zeros((64, 32), F32)], axis=1)
    flat = flatten(narrow)
    for j in range(7):
        wide_ref[64 * j : 64 * j + 64, :] = wide[:, 128 * j : 128 * j + 128]
    core = lax.axis_index("core")
    for p in range(8):
        zl, zh = p // 4, p % 4
        halves = []
        for yh in range(2):
            rows = [wide_ref[pl.ds(64 * j + 32 * zl + 2 * zh + yh, 4, stride=8), :] for j in range(7)]
            halves.append(jnp.concatenate(rows + [flat[14 * yh : 14 * yh + 14]], axis=0))
        keep_ref[p] = jnp.where(core == 0, halves[0], halves[1])
        send_ref[p] = jnp.where(core == 0, halves[1], halves[0])


def first_stage(a_ref, b_ref, out_ref):
    out_ref[...] = a_ref[...] + b_ref[...]


def second_stage(in_ref, out_ref):
    total = in_ref[0]
    for p in range(1, 8):
        total = total + in_ref[p]
    for x in range(4):
        block = [total[4 * j + x : 4 * j + x + 1] for j in range(7)]
        rows = jnp.concatenate(block + [total[28:42]], axis=0)
        for y in range(4):
            out_ref[4 * x + y] = rows


def third_stage(in_ref, own_ref, sib_ref, out_ref):
    total = in_ref[0]
    for p in range(1, 16):
        total = total + in_ref[p]
    gap = [jnp.zeros((1, 128), F32)]
    out_ref[0:24, :] = jnp.concatenate([total[0:7]] + gap + [total[7:21]] + gap + gap, axis=0)
    even = lax.axis_index("y") % 2 == 0
    own, sib = own_ref[...], sib_ref[...]
    out_ref[24:32, :] = jnp.where(even, own, sib)
    out_ref[32:40, :] = jnp.where(even, sib, own)


def moments(master, first, second, grad):
    first_new = 0.9 * first + 0.1 * grad
    second_new = 0.999 * second + 0.001 * grad * grad
    direction = (
        first_new / (1.0 - 0.9**10) / (jnp.sqrt(second_new / (1.0 - 0.999**10)) + 1e-06)
        + 0.01 * master
    )
    return (first_new, second_new, direction)


def runs():
    row = lax.broadcasted_iota(jnp.int32, (27, 128), 0)
    lane = lax.broadcasted_iota(jnp.int32, (27, 128), 1)
    start = (row * 128) // 108
    run = (row * 128 + lane) // 108
    return [(run == start + p, lane == start + p) for p in range(3)]


def run_sums(value):
    total = jnp.zeros((27, 128), F32)
    for inside, column in runs():
        part = jnp.sum(jnp.where(inside, value, 0.0), axis=1, keepdims=True)
        total = total + jnp.where(column, part, 0.0)
    return jnp.sum(total, axis=0, keepdims=True)


def run_spread(value):
    total = jnp.zeros((27, 128), F32)
    for inside, column in runs():
        part = jnp.sum(jnp.where(column, value, 0.0), axis=1, keepdims=True)
        total = total + jnp.where(inside, part, 0.0)
    return total


def update(in_ref, other_ref, own_ref, m_ref, f_ref, s_ref, w2_ref, f2_ref, s2_ref, w1_ref, f1_ref, s1_ref):
    y, core = lax.axis_index("y"), lax.axis_index("core")
    quarter = y % 2 * 2 + core
    mine, other = in_ref[...], other_ref[...]
    low, high = jnp.where(core == 0, mine, other), jnp.where(core == 0, other, mine)
    grad = jnp.where(y // 2 == 0, low[0:8], high[0:8])
    inside = (
        lax.broadcasted_iota(jnp.int32, (8, 128), 0) * 128 + lax.broadcasted_iota(jnp.int32, (8, 128), 1)
    ) < 864
    block = []
    for j in range(3):
        parts = [half[at + 2 * j : at + 2 * j + 2] for at in (24, 32) for half in (low, high)]
        block.append(sum(place(part, q) for q, part in enumerate(parts)))
    _, _, direction = moments(block[0], block[1], block[2], grad)
    direction = jnp.where(inside, direction, 0.0)
    ratio = jnp.sqrt(jnp.sum(block[0] * block[0], keepdims=True)) / (
        jnp.sqrt(jnp.sum(direction * direction, keepdims=True)) + 1e-06
    )
    mine = take(grad, 0)
    for q in range(1, 4):
        mine = jnp.where(quarter == q, take(grad, q), mine)
    master, first, second = (own_ref[2 * j : 2 * j + 2] for j in range(3))
    first_new, second_new, direction = moments(master, first, second, mine)
    for ref, value in (
        (w2_ref, master - 0.01 * (ratio * direction)),
        (f2_ref, first_new),
        (s2_ref, second_new),
    ):
        ref[...] = jnp.concatenate([value[0:1], value[1:2, 0:88]], axis=1)
    grad = jnp.concatenate([low[8:22], high[8:22]], axis=0)[0:27]
    master = m_ref[...]
    first_new, second_new, direction = moments(master, f_ref[...], s_ref[...], grad)
    ratio = jnp.sqrt(run_sums(master * master)) / (jnp.sqrt(run_sums(direction * direction)) + 1e-06)
    w1_ref[...] = master - 0.01 * (run_spread(ratio) * direction)
    f1_ref[...] = first_new
    s1_ref[...] = second_new


def turn(value, by):
    return lax.ppermute(value, GY, [(i, (i + by) % 4) for i in range(4)])


def swap(value):
    return lax.ppermute(value, "core", [(0, 1), (1, 0)])


def local(volume, cotangent, w1_master, w1_first, w1_second, w2_master, w2_first, w2_second):
    wide = [w.reshape(1, 216) for w in (w2_master, w2_first, w2_second)]
    narrow = [w.reshape(27, 128) for w in (w1_master, w1_first, w1_second)]
    narrow_band, pick = call(narrow_rows, (shape((256, 512), BF16), shape((512, 128), BF16)), narrow[0])
    along_y = shape((496, 128), BF16)
    slabs, ahead, message, own = call(
        pack,
        (shape((4, 544, 128), BF16), shape((2, 544, 128), BF16), shape((64, 5, 4, 128), BF16), shape((8, 128), F32)),
        cotangent.reshape(2048, 128),
        volume.reshape(128, 128),
        *wide,
        scratch=(
            pltpu.VMEM((2048, 128), BF16),
            pltpu.VMEM((128, 128), BF16),
            pltpu.VMEM((1, 216), F32),
            pltpu.VMEM((1, 216), F32),
            pltpu.VMEM((1, 216), F32),
            pltpu.VMEM((2048, 128), F32),
            pltpu.VMEM((128, 128), F32),
            pltpu.SemaphoreType.DMA((5,)),
        ),
        space=pl.BlockSpec(memory_space=pltpu.HBM),
        params=pltpu.CompilerParams(vmem_limit_bytes=60 * 1024 * 1024),
    )
    next_x = lax.ppermute(ahead, GX, [(i, (i + 7) % 8) for i in range(8)])
    sibling = lax.ppermute(own, "y", [(0, 1), (1, 0), (2, 3), (3, 2)])
    message = lax.all_to_all(message, GX + GZ, 0, 0, tiled=True)
    bank = call(bank_rows, shape((128, 128), BF16), message)
    near_banks = turn(bank, 1), turn(bank, 3)
    up, down, beyond = call(
        y_messages, (along_y, along_y, shape((16, 640), F32)), slabs, next_x, message, *near_banks
    )
    before_y, after_y = turn(up, 1), turn(down, 3)
    keep, send = call(
        gradients,
        (shape((8, 42, 128), F32), shape((8, 42, 128), F32)),
        slabs,
        next_x,
        beyond,
        after_y,
        before_y,
        bank,
        *near_banks,
        narrow_band,
        pick,
        sibling,
        scratch=(
            pltpu.VMEM((640, 1536), BF16),
            pltpu.VMEM((6, 48, 128), BF16),
            pltpu.VMEM((256, 512), F32),
            pltpu.VMEM((512, 128), F32),
            pltpu.VMEM((448, 128), F32),
        ),
    )
    sums = call(first_stage, shape((8, 42, 128), F32), keep, swap(send))
    sums = lax.all_to_all(sums, ("zl", "zh"), 0, 0, tiled=True)
    sums = call(second_stage, shape((16, 21, 128), F32), sums)
    sums = lax.all_to_all(sums, ("x", "y"), 0, 0, tiled=True)
    half = call(third_stage, shape((40, 128), F32), sums, own, sibling)
    one, rows = shape((1, 216), F32), shape((27, 128), F32)
    new = call(update, (one, one, one, rows, rows, rows), half, swap(half), own, *narrow)
    return tuple(w.reshape(-1) for w in new[3:] + new[:3])


def solution(mesh):
    parts = Mesh(mesh.devices.reshape(2, 4, 4, 4, 2), GX + GY + GZ)
    field = P(None, GX, GY, GZ)
    owned = P(GX + GY + GZ)
    return jax.shard_map(
        local,
        mesh=parts,
        in_specs=(field, field, P(), P(), P(), owned, owned, owned),
        out_specs=(P(), P(), P(), owned, owned, owned),
        check_vma=False,
    )
```

```python
import jax
import jax.numpy as jnp
from jax import lax
from jax.experimental import pallas as pl
from jax.experimental.pallas import tpu as pltpu
from jax.sharding import Mesh, PartitionSpec as P

CI = 4
C1 = 32
C2 = 64
F32 = jnp.float32
BF16 = jnp.bfloat16
GX = ("zl", "x")
GY = ("zh",)
GZ = ("y", "core")
PAST = ((3, 0), (2, 2))
VMEM = pl.BlockSpec(memory_space=pltpu.VMEM)
PARAMS = pltpu.CompilerParams(vmem_limit_bytes=32 * 1024 * 1024)


def dot(a, b):
    return lax.dot_general(a, b, (((1,), (0,)), ((), ())), preferred_element_type=F32)


def dot_nt(a, b):
    return lax.dot_general(a, b, (((1,), (1,)), ((), ())), preferred_element_type=F32)


def dot_tn(a, b):
    return lax.dot_general(a, b, (((0,), (0,)), ((), ())), preferred_element_type=F32)


def call(kernel, out_shapes, *args, scratch=(), space=VMEM, params=PARAMS):
    return pl.pallas_call(
        kernel,
        out_shape=out_shapes,
        in_specs=[space] * len(args),
        out_specs=jax.tree.map(lambda _: VMEM, out_shapes),
        scratch_shapes=scratch,
        compiler_params=params,
    )(*args)


def shape(dims, dtype):
    return jax.ShapeDtypeStruct(dims, dtype)


def roll(v, by):
    return pltpu.roll(v, by % v.shape[1], 1)


def lanes():
    return lax.broadcasted_iota(jnp.int32, (1, 128), 1)


def within(v, low, high):
    return jnp.where((lanes() >= low) & (lanes() < high), v, 0.0)


def two_rows(v):
    return [v[:, 0:128], jnp.concatenate([v[:, 128:216], jnp.zeros((1, 40), F32)], axis=1)]


def place(two, q):
    lane = lax.broadcasted_iota(jnp.int32, (1, 128), 1)
    row, at = divmod(216 * q, 128)
    one, last = roll(two[0:1], at), roll(jnp.where(lane < 88, two[1:2], 0.0), at)
    gap = jnp.zeros((1, 128), F32)
    pieces = [gap] * row + [
        jnp.where(lane >= at, one, 0.0),
        jnp.where(lane < at, one, 0.0) + jnp.where(lane >= at, last, 0.0),
        jnp.where(lane < at, last, 0.0),
    ]
    return jnp.concatenate((pieces + [gap] * 8)[:8], axis=0)


def take(block, q):
    lane = lax.broadcasted_iota(jnp.int32, (1, 128), 1)
    row, at = divmod(216 * q, 128)
    moved = [roll(block[r : r + 1], -at) for r in range(row, min(row + 3, 8))]
    one = jnp.where(lane < 128 - at, moved[0], moved[1])
    two = jnp.where(lane < 128 - at, moved[1], moved[2]) if len(moved) > 2 else moved[1]
    return jnp.concatenate([one, two], axis=0)


def along_gz():
    return lax.axis_index("y") * 2 + lax.axis_index("core")


def pack(
    cot_hbm, vol_hbm, w2_hbm, f2_hbm, s2_hbm, slab_ref, ahead_ref, out_ref, own_ref,
    cot_ref, vol_ref, w2_ref, f2_ref, s2_ref, cot32, vol32, sems,
):
    copies = [
        pltpu.make_async_copy(source, target, sems.at[i])
        for i, (source, target) in enumerate(
            ((cot_hbm, cot_ref), (vol_hbm, vol_ref), (w2_hbm, w2_ref), (f2_hbm, f2_ref), (s2_hbm, s2_ref))
        )
    ]
    for copy in copies:
        copy.start()
    for copy in copies:
        copy.wait()
    cot32[...] = cot_ref[...].astype(F32)
    vol32[...] = vol_ref[...].astype(F32)
    for x in range(4):
        for y in range(8):
            slab_ref[x, 64 * y : 64 * y + 64, :] = cot32[pl.ds(8 * x + y, 64, stride=32), :].astype(BF16)
        slab_ref[x, 512:544, :] = jnp.concatenate(
            [vol32[pl.ds(8 * x + y, 4, stride=32), :] for y in range(8)], axis=0
        ).astype(BF16)
    ahead_ref[...] = slab_ref[0:2]
    row = lax.broadcasted_iota(jnp.int32, (16, 512), 0)
    lane = lax.broadcasted_iota(jnp.int32, (16, 512), 1)
    pick = ((row < 4) & (lane == row * 128)) | ((row >= 4) & (row < 8) & (lane == row * 128 - 385))
    cells = jnp.concatenate([slab_ref[x] for x in range(4)], axis=1)
    cells = jnp.concatenate([cells, jnp.zeros((96, 512), BF16)], axis=0)
    edge = dot_nt(pick.astype(F32).astype(BF16), cells)
    own = [row for ref in (w2_ref, f2_ref, s2_ref) for row in two_rows(ref[...])]
    own_ref[...] = jnp.concatenate(own + [jnp.zeros((2, 128), F32)], axis=0)
    ends = []
    for side in range(2):
        at = slice(4 * side, 4 * side + 4)
        tail = edge[at, 512:640]
        tail = [sum(roll(tail[x : x + 1], 32 * x) for x in range(4))] + own[0:2] + [jnp.zeros((1, 128), F32)]
        ends.append(jnp.concatenate([edge[at, 128 * j : 128 * j + 128] for j in range(4)] + tail, axis=0))
    me = along_gz()
    for p in range(8):
        message = jnp.where(me < p, ends[1], ends[0]).astype(BF16)
        for x in range(8):
            for j in range(5):
                out_ref[8 * x + p, j] = message[4 * j : 4 * j + 4]


def bank_rows(in_ref, out_ref):
    rows = [in_ref[p, 4].astype(F32)[1:3] for p in range(64)]
    out_ref[...] = jnp.concatenate(rows, axis=0).astype(BF16)


def y_messages(slab_ref, next_ref, in_ref, pb_ref, nb_ref, up_ref, dn_ref, beyond_ref):
    slabs = [slab_ref.at[x] for x in range(4)] + [next_ref.at[x] for x in range(2)]
    first, last = [], []
    for xe, slab in enumerate(slabs):
        up_ref[xe * 64 : xe * 64 + 64, :] = slab[448:512, :]
        dn_ref[xe * 64 : xe * 64 + 64, :] = slab[0:64, :]
        vol = slab[512:544, :].astype(F32)
        first.append(vol[0:4])
        last.append(vol[28:32])
    fill = [jnp.zeros((8, 128), F32)]
    four = [jnp.zeros((4, 128), F32)]
    across, along = lax.axis_index("zl") * 4 + lax.axis_index("x"), along_gz()
    rows_up, rows_dn = [], []
    for side in range(2):
        other = along + 2 * side - 1
        inside = (other >= 0) & (other <= 7)
        other = jnp.clip(other, 0, 7)
        mid = jnp.where(inside, in_ref[8 * across + other].astype(F32), 0.0)
        after = jnp.where(inside, in_ref[8 * ((across + 1) % 8) + other].astype(F32), 0.0)
        parts = [jnp.concatenate([mid[j], after[j, 0:2]], axis=0) for j in range(4)]
        tail = [mid[4, 0:1]] * 4 + [after[4, 0:1]] * 2
        tail = [roll(row, -32 * x) for row, x in zip(tail, (0, 1, 2, 3, 0, 1), strict=True)]
        parts.append(within(jnp.concatenate(tail, axis=0), 0, 32))
        for j in range(5):
            beyond_ref[8 * side : 8 * side + 8, 128 * j : 128 * j + 128] = jnp.concatenate(
                [parts[j], jnp.zeros((2, 128), F32)], axis=0
            )
        rows_up.append(within(roll(parts[3], -64), 0, 64) + within(roll(parts[4], 36), 64, 68))
        rows_dn.append(within(parts[0], 0, 64) + within(roll(parts[4], 64), 64, 68))
    up_ref[384:432, :] = jnp.concatenate(last + fill + rows_up + four, axis=0).astype(BF16)
    dn_ref[384:432, :] = jnp.concatenate(first + fill + rows_dn + four, axis=0).astype(BF16)
    up_ref[432:496, :] = pb_ref[0:64, :]
    dn_ref[432:496, :] = nb_ref[64:128, :]


def assemble(slab_ref, next_ref, beyond_ref, yp_ref, yn_ref, e_ref, ve_ref, keep):
    slabs = [slab_ref.at[x] for x in range(4)] + [next_ref.at[x] for x in range(2)]
    along_y = lax.axis_index("zh")
    some, more = along_y > 0, along_y < 3
    before = jnp.where(some, yp_ref[384:432, :].astype(F32), 0.0)
    after = jnp.where(more, yn_ref[384:432, :].astype(F32), 0.0)
    for xe, slab in enumerate(slabs):
        rows = jnp.concatenate(
            [
                jnp.where(some, yp_ref[xe * 64 : xe * 64 + 64, :].astype(F32), 0.0).astype(BF16),
                slab[0:512, :],
                jnp.where(more, yn_ref[xe * 64 : xe * 64 + 64, :].astype(F32), 0.0).astype(BF16),
            ],
            axis=0,
        )
        for a in range(3):
            x = xe - a
            if 0 <= x < 4:
                value = (rows.astype(F32) * keep).astype(BF16) if (x, a) in PAST else rows
                e_ref[:, 512 * a + 128 * x : 512 * a + 128 * x + 128] = value
        vol = slab[512:544, :].astype(F32)
        ve_ref[xe] = jnp.concatenate(
            [before[xe * 4 : xe * 4 + 4], vol, after[xe * 4 : xe * 4 + 4], jnp.zeros((8, 128), F32)], axis=0
        ).astype(BF16)
    ends = []
    for side in range(2):
        parts = [roll(beyond_ref[8 * side : 8 * side + 6, 128 * j : 128 * j + 128], 64) for j in range(5)]
        prev = before[32 + 6 * side : 38 + 6 * side]
        nxt = after[32 + 6 * side : 38 + 6 * side]
        tiles = [within(prev, 0, 64) + within(parts[0], 64, 128)]
        for k in range(1, 4):
            tiles.append(jnp.where(lanes() < 64, parts[k - 1], parts[k]))
        tiles.append(within(parts[3], 0, 64) + within(roll(nxt, 64), 64, 128))
        tiles.append(
            within(roll(prev, -64), 0, 4) + within(roll(parts[4], -60), 4, 36) + within(roll(nxt, -28), 36, 40)
        )
        ends.append(
            jnp.concatenate([jnp.concatenate(tiles, axis=1), jnp.zeros((10, 768), F32)], axis=0).astype(BF16)
        )
    return ends


def flatten(narrow):
    lane = lax.broadcasted_iota(jnp.int32, (1, 128), 1)
    rows = [jnp.zeros((1, 128), F32) for _ in range(33)]
    for c in range(32):
        row, at = divmod(108 * c, 128)
        moved = roll(jnp.where(lane < 108, narrow[c : c + 1], 0.0), at)
        if at + 108 <= 128:
            rows[row] = rows[row] + moved
        else:
            rows[row] = rows[row] + jnp.where(lane >= at, moved, 0.0)
            rows[row + 1] = rows[row + 1] + jnp.where(lane < at, moved, 0.0)
    return jnp.concatenate(rows[:32], axis=0)


def turned(yp_ref, yn_ref, own_ref, pb_ref, nb_ref, rows_ref):
    me = lax.axis_index("zh")
    for by in range(4):
        zh = (me + by) % 4
        for across in range(8):
            at = pl.multiple_of(64 * across + 16 * zh, 16)
            if by == 2:
                ref, row = (yp_ref if across < 4 else yn_ref), 432 + 16 * (across % 4)
            else:
                ref, row = (own_ref, nb_ref, None, pb_ref)[by], 16 * across
            rows_ref[pl.ds(at, 16), :] = ref[row : row + 16, :].astype(F32)
    parts = []
    for q in range(4):
        parts.append(rows_ref[pl.ds(2 * q, 64, stride=8), :].T)
        parts.append(rows_ref[pl.ds(2 * q + 1, 64, stride=8), :].T[0:88])
    return jnp.concatenate(parts, axis=0).astype(BF16)


def narrow_lanes():
    row = lax.broadcasted_iota(jnp.int32, (512, 128), 0)
    col = lax.broadcasted_iota(jnp.int32, (512, 128), 1)
    group, inner = row // 48, row % 48
    a, c = group // 3, group % 3
    b, i = inner // 4, inner % 4
    return ((b < 3) & (group < 9) & (col == (9 * a + 3 * b + c) * 4 + i)).astype(F32)


def narrow_rows(w1_ref, out_ref, pick_ref):
    lane = lax.broadcasted_iota(jnp.int32, (1, 128), 1)
    rows = []
    for c in range(32):
        row, at = divmod(108 * c, 128)
        piece = roll(w1_ref[row : row + 1, :], -at)
        if at > 20:
            piece = jnp.where(lane < 128 - at, piece, roll(w1_ref[row + 1 : row + 2, :], -at))
        rows.append(jnp.where(lane < 108, piece, 0.0))
    bank = jnp.concatenate(rows, axis=0).astype(BF16)
    pick = narrow_lanes().astype(BF16)
    pick_ref[...] = pick
    first = dot_nt(bank, pick)
    for y in range(8):
        out_ref[32 * y : 32 * y + 32, :] = roll(first, 4 * y).astype(BF16)


def gradients(
    slab_ref, next_ref, beyond_ref, yn_ref, yp_ref, bank_ref, pb_ref, nb_ref, wb_ref, pick_ref, sib_ref,
    keep_ref, send_ref,
    e_ref, ve_ref, ga_ref, rows_ref, wide_ref,
):
    final = (lax.axis_index("zl") == 1) & (lax.axis_index("x") == 3)
    keep = jnp.where(final, 0.0, 1.0)
    ends = assemble(slab_ref, next_ref, beyond_ref, yp_ref, yn_ref, e_ref, ve_ref, keep)
    lane = lax.broadcasted_iota(jnp.int32, (1, 128), 1)
    low, high = lane == 0, lane == 127
    eye = (
        lax.broadcasted_iota(jnp.int32, (48, 128), 0) == lax.broadcasted_iota(jnp.int32, (48, 128), 1)
    ).astype(F32).astype(BF16)
    left = dot_nt(eye, ends[0][:, 640:768])
    right = dot_nt(eye, ends[1][:, 640:768])
    shifted = []
    for xe in range(6):
        v = ve_ref[xe].astype(F32)
        shifted.append(
            (
                jnp.where(low, left[:, xe : xe + 1], roll(v, 1)).astype(BF16),
                ve_ref[xe],
                jnp.where(high, right[:, xe : xe + 1], roll(v, -1)).astype(BF16),
            )
        )
    rest = jnp.zeros((80, 128), BF16)
    patches = jnp.concatenate(
        [
            jnp.concatenate(
                [
                    (shifted[x + a][c].astype(F32) * keep).astype(BF16) if (x, a) in PAST else shifted[x + a][c]
                    for a in range(3)
                    for c in range(3)
                ]
                + [rest],
                axis=0,
            )
            for x in range(4)
        ],
        axis=1,
    )
    pre = dot(wb_ref[...], patches)
    sig = 1.0 / (1.0 + jnp.exp(-pre))
    act = (pre * sig).astype(BF16)
    slope = sig * (1.0 + pre * (1.0 - sig))
    halos = []
    for end in ends:
        m = end[:, 0:640].astype(F32)
        by_a = []
        for a in range(3):
            rows = m[a : a + 4]
            if a != 1:
                row = lax.broadcasted_iota(jnp.int32, (4, 1), 0)
                rows = rows * jnp.where(row == (3 if a == 0 else 2), keep, 1.0)
            by_a.append(rows)
        halos.append(
            jnp.concatenate(
                [
                    jnp.concatenate([rows[:, 128 * k : 128 * k + 256] for rows in by_a], axis=1)
                    for k in range(4)
                ],
                axis=0,
            ).astype(BF16)
        )
    none = jnp.zeros((32, 64), BF16)
    weights = turned(yp_ref, yn_ref, bank_ref, pb_ref, nb_ref, rows_ref)
    blocks = []
    for c in range(3):
        for yl in range(2):
            cells = []
            for a in range(3):
                for yp in range(4):
                    b = yp - yl
                    if 0 <= b <= 2:
                        tap = (2 - a) * 9 + (2 - b) * 3 + (2 - c)
                        cells.append(weights[tap * 32 : tap * 32 + 32])
                    else:
                        cells.append(none)
            blocks.append(jnp.concatenate(cells, axis=1))
    bank = jnp.concatenate(blocks, axis=0)
    from_left = dot_nt(bank[0:64], halos[0])
    from_right = dot_nt(bank[128:192], halos[1])
    for k in range(4):
        for xp in range(2):
            v = sum(
                dot(
                    bank[:, 256 * a : 256 * a + 256],
                    e_ref[128 * k : 128 * k + 256, 512 * a + 256 * xp : 512 * a + 256 * xp + 256],
                )
                for a in range(3)
            )
            for j in range(2):
                x = 2 * xp + j
                at = slice(128 * j, 128 * j + 128)
                col = 4 * k + x
                ga_ref[64 * k : 64 * k + 64, 128 * x : 128 * x + 128] = (
                    v[64:128, at]
                    + jnp.where(low, from_left[:, col : col + 1], roll(v[0:64, at], 1))
                    + jnp.where(high, from_right[:, col : col + 1], roll(v[128:192, at], -1))
                )
    grad_pre = (ga_ref[...] * slope).astype(BF16)
    product = dot_nt(grad_pre, patches)
    total = product[0:32]
    for y in range(1, 8):
        total = total + roll(product[32 * y : 32 * y + 32], -4 * y)
    split, rest = [], total
    for _ in range(3):
        split.append(rest.astype(BF16))
        rest = rest - split[-1].astype(F32)
    picked = dot(jnp.concatenate(split, axis=0), pick_ref[...])
    narrow = picked[0:32] + (picked[32:64] + picked[64:96])
    act32 = act.astype(F32)
    before, after = [], []
    for x in range(4):
        part = act32[:, 128 * x : 128 * x + 128]
        before.append(jnp.where(low, 0.0, roll(part, 1)).astype(BF16))
        after.append(jnp.where(high, 0.0, roll(part, -1)).astype(BF16))
    before = jnp.concatenate(before, axis=1)
    after = jnp.concatenate(after, axis=1)
    empty = jnp.zeros((32, 512), BF16)
    rows = []
    for k in range(4):
        parts = []
        for yl in range(2):
            at = slice(64 * k + 32 * yl, 64 * k + 32 * yl + 32)
            parts += [before[at], act[at], after[at], empty]
        rows.append(jnp.concatenate(parts, axis=0))
    wide = jnp.concatenate(
        [
            sum(
                dot_nt(e_ref[128 * k : 128 * k + 256, 512 * a : 512 * a + 512], rows[k])
                for k in range(4)
            )
            for a in range(3)
        ],
        axis=0,
    )
    row = lax.broadcasted_iota(jnp.int32, (16, 512), 0)
    lanes = lax.broadcasted_iota(jnp.int32, (16, 512), 1)
    pick = ((row < 4) & (lanes == row * 128)) | ((row >= 4) & (row < 8) & (lanes == (row - 4) * 128 + 127))
    edges = dot_nt(pick.astype(F32).astype(BF16), act)
    gap = jnp.zeros((4, 64), F32)
    one = jnp.zeros((4, 32), F32)
    table = []
    for k in range(4):
        e0 = edges[0:4, 64 * k : 64 * k + 32]
        e1 = edges[0:4, 64 * k + 32 : 64 * k + 64]
        table.append(jnp.concatenate([gap, e0, one, gap, e1, one], axis=1))
    for k in range(4):
        e0 = edges[4:8, 64 * k : 64 * k + 32]
        e1 = edges[4:8, 64 * k + 32 : 64 * k + 64]
        table.append(jnp.concatenate([e0, one, gap, e1, one, gap], axis=1))
    table = jnp.concatenate(table, axis=0).astype(BF16)
    wide = wide + dot_tn(jnp.concatenate(halos, axis=0), table)
    taps = []
    for a in range(3):
        for b in range(3):
            at = (2 - a) * 256 + (2 - b) * 64
            taps.append((wide[at : at + 64, 0:128] + wide[at + 64 : at + 128, 128:256])[:, 0:96])
    wide = jnp.concatenate(taps + [jnp.zeros((64, 32), F32)], axis=1)
    flat = flatten(narrow)
    for j in range(7):
        wide_ref[64 * j : 64 * j + 64, :] = wide[:, 128 * j : 128 * j + 128]
    core = lax.axis_index("core")
    parts = [flat[0:14], flat[14:28]]
    mine = jnp.where(core == 0, parts[0], parts[1])
    others = jnp.where(core == 0, parts[1], parts[0])
    for p in range(8):
        zl, zh = p // 4, p % 4
        for ref, yh, part in ((keep_ref, core, mine), (send_ref, 1 - core, others)):
            for j in range(7):
                ref[p, 4 * j : 4 * j + 4, :] = wide_ref[pl.ds(64 * j + 32 * zl + 2 * zh + yh, 4, stride=8), :]
            ref[p, 28:42, :] = part


def first_stage(a_ref, b_ref, out_ref):
    out_ref[...] = a_ref[...] + b_ref[...]


def second_stage(in_ref, out_ref):
    total = in_ref[0]
    for p in range(1, 8):
        total = total + in_ref[p]
    for x in range(4):
        block = [total[4 * j + x : 4 * j + x + 1] for j in range(7)]
        rows = jnp.concatenate(block + [total[28:42]], axis=0)
        for y in range(4):
            out_ref[4 * y + x] = rows


def third_stage(in_ref, own_ref, sib_ref, out_ref):
    total = in_ref[0]
    for p in range(1, 16):
        total = total + in_ref[p]
    gap = [jnp.zeros((1, 128), F32)]
    out_ref[0:24, :] = jnp.concatenate([total[0:7]] + gap + [total[7:21]] + gap + gap, axis=0)
    even = lax.axis_index("y") % 2 == 0
    own, sib = own_ref[...], sib_ref[...]
    out_ref[24:32, :] = jnp.where(even, own, sib)
    out_ref[32:40, :] = jnp.where(even, sib, own)


def moments(master, first, second, grad):
    first_new = 0.9 * first + 0.1 * grad
    second_new = 0.999 * second + 0.001 * grad * grad
    direction = (
        first_new / (1.0 - 0.9**10) / (jnp.sqrt(second_new / (1.0 - 0.999**10)) + 1e-06)
        + 0.01 * master
    )
    return (first_new, second_new, direction)


def runs():
    row = lax.broadcasted_iota(jnp.int32, (27, 128), 0)
    lane = lax.broadcasted_iota(jnp.int32, (27, 128), 1)
    start = (row * 128) // 108
    run = (row * 128 + lane) // 108
    return [(run == start + p, lane == start + p) for p in range(3)]


def run_sums(value):
    total = jnp.zeros((27, 128), F32)
    for inside, column in runs():
        part = jnp.sum(jnp.where(inside, value, 0.0), axis=1, keepdims=True)
        total = total + jnp.where(column, part, 0.0)
    return jnp.sum(total, axis=0, keepdims=True)


def run_spread(value):
    total = jnp.zeros((27, 128), F32)
    for inside, column in runs():
        part = jnp.sum(jnp.where(column, value, 0.0), axis=1, keepdims=True)
        total = total + jnp.where(inside, part, 0.0)
    return total


def update(in_ref, other_ref, own_ref, m_ref, f_ref, s_ref, w2_ref, f2_ref, s2_ref, w1_ref, f1_ref, s1_ref):
    y, core = lax.axis_index("y"), lax.axis_index("core")
    quarter = y % 2 * 2 + core
    mine, other = in_ref[...], other_ref[...]
    low, high = jnp.where(core == 0, mine, other), jnp.where(core == 0, other, mine)
    grad = jnp.where(y // 2 == 0, low[0:8], high[0:8])
    inside = (
        lax.broadcasted_iota(jnp.int32, (8, 128), 0) * 128 + lax.broadcasted_iota(jnp.int32, (8, 128), 1)
    ) < 864
    block = []
    for j in range(3):
        parts = [half[at + 2 * j : at + 2 * j + 2] for at in (24, 32) for half in (low, high)]
        block.append(sum(place(part, q) for q, part in enumerate(parts)))
    _, _, direction = moments(block[0], block[1], block[2], grad)
    direction = jnp.where(inside, direction, 0.0)
    ratio = jnp.sqrt(jnp.sum(block[0] * block[0], keepdims=True)) / (
        jnp.sqrt(jnp.sum(direction * direction, keepdims=True)) + 1e-06
    )
    mine = take(grad, 0)
    for q in range(1, 4):
        mine = jnp.where(quarter == q, take(grad, q), mine)
    master, first, second = (own_ref[2 * j : 2 * j + 2] for j in range(3))
    first_new, second_new, direction = moments(master, first, second, mine)
    for ref, value in (
        (w2_ref, master - 0.01 * (ratio * direction)),
        (f2_ref, first_new),
        (s2_ref, second_new),
    ):
        ref[...] = jnp.concatenate([value[0:1], value[1:2, 0:88]], axis=1)
    grad = jnp.concatenate([low[8:22], high[8:22]], axis=0)[0:27]
    master = m_ref[...]
    first_new, second_new, direction = moments(master, f_ref[...], s_ref[...], grad)
    ratio = jnp.sqrt(run_sums(master * master)) / (jnp.sqrt(run_sums(direction * direction)) + 1e-06)
    w1_ref[...] = master - 0.01 * (run_spread(ratio) * direction)
    f1_ref[...] = first_new
    s1_ref[...] = second_new


def turn(value, by):
    return lax.ppermute(value, GY, [(i, (i + by) % 4) for i in range(4)])


def swap(value):
    return lax.ppermute(value, "core", [(0, 1), (1, 0)])


def local(volume, cotangent, w1_master, w1_first, w1_second, w2_master, w2_first, w2_second):
    wide = [w.reshape(1, 216) for w in (w2_master, w2_first, w2_second)]
    narrow = [w.reshape(27, 128) for w in (w1_master, w1_first, w1_second)]
    narrow_band, pick = call(narrow_rows, (shape((256, 512), BF16), shape((512, 128), BF16)), narrow[0])
    along_y = shape((496, 128), BF16)
    slabs, ahead, message, own = call(
        pack,
        (shape((4, 544, 128), BF16), shape((2, 544, 128), BF16), shape((64, 5, 4, 128), BF16), shape((8, 128), F32)),
        cotangent.reshape(2048, 128),
        volume.reshape(128, 128),
        *wide,
        scratch=(
            pltpu.VMEM((2048, 128), BF16),
            pltpu.VMEM((128, 128), BF16),
            pltpu.VMEM((1, 216), F32),
            pltpu.VMEM((1, 216), F32),
            pltpu.VMEM((1, 216), F32),
            pltpu.VMEM((2048, 128), F32),
            pltpu.VMEM((128, 128), F32),
            pltpu.SemaphoreType.DMA((5,)),
        ),
        space=pl.BlockSpec(memory_space=pltpu.HBM),
        params=pltpu.CompilerParams(vmem_limit_bytes=60 * 1024 * 1024),
    )
    next_x = lax.ppermute(ahead, GX, [(i, (i + 7) % 8) for i in range(8)])
    sibling = lax.ppermute(own, "y", [(0, 1), (1, 0), (2, 3), (3, 2)])
    message = lax.all_to_all(message, GX + GZ, 0, 0, tiled=True)
    bank = call(bank_rows, shape((128, 128), BF16), message)
    near_banks = turn(bank, 1), turn(bank, 3)
    up, down, beyond = call(
        y_messages, (along_y, along_y, shape((16, 640), F32)), slabs, next_x, message, *near_banks
    )
    before_y, after_y = turn(up, 1), turn(down, 3)
    keep, send = call(
        gradients,
        (shape((8, 42, 128), F32), shape((8, 42, 128), F32)),
        slabs,
        next_x,
        beyond,
        after_y,
        before_y,
        bank,
        *near_banks,
        narrow_band,
        pick,
        sibling,
        scratch=(
            pltpu.VMEM((640, 1536), BF16),
            pltpu.VMEM((6, 48, 128), BF16),
            pltpu.VMEM((256, 512), F32),
            pltpu.VMEM((512, 128), F32),
            pltpu.VMEM((448, 128), F32),
        ),
    )
    sums = call(first_stage, shape((8, 42, 128), F32), keep, swap(send))
    sums = lax.all_to_all(sums, ("zl", "zh"), 0, 0, tiled=True)
    sums = call(second_stage, shape((16, 21, 128), F32), sums)
    sums = lax.all_to_all(sums, ("y", "x"), 0, 0, tiled=True)
    half = call(third_stage, shape((40, 128), F32), sums, own, sibling)
    one, rows = shape((1, 216), F32), shape((27, 128), F32)
    new = call(update, (one, one, one, rows, rows, rows), half, swap(half), own, *narrow)
    return tuple(w.reshape(-1) for w in new[3:] + new[:3])


def solution(mesh):
    parts = Mesh(mesh.devices.reshape(2, 4, 4, 4, 2), GX + GY + GZ)
    field = P(None, GX, GY, GZ)
    owned = P(GX + GY + GZ)
    return jax.shard_map(
        local,
        mesh=parts,
        in_specs=(field, field, P(), P(), P(), owned, owned, owned),
        out_specs=(P(), P(), P(), owned, owned, owned),
        check_vma=False,
    )
```

```python
import jax
import jax.numpy as jnp
from jax import lax
from jax.experimental import pallas as pl
from jax.experimental.pallas import tpu as pltpu
from jax.sharding import Mesh, PartitionSpec as P

CI = 4
C1 = 32
C2 = 64
F32 = jnp.float32
BF16 = jnp.bfloat16
GX = ("zl", "x")
GY = ("zh",)
GZ = ("y", "core")
PAST = ((3, 0), (2, 2))
VMEM = pl.BlockSpec(memory_space=pltpu.VMEM)
PARAMS = pltpu.CompilerParams(vmem_limit_bytes=32 * 1024 * 1024)


def dot(a, b):
    return lax.dot_general(a, b, (((1,), (0,)), ((), ())), preferred_element_type=F32)


def dot_nt(a, b):
    return lax.dot_general(a, b, (((1,), (1,)), ((), ())), preferred_element_type=F32)


def dot_tn(a, b):
    return lax.dot_general(a, b, (((0,), (0,)), ((), ())), preferred_element_type=F32)


def call(kernel, out_shapes, *args, scratch=(), space=VMEM, params=PARAMS):
    return pl.pallas_call(
        kernel,
        out_shape=out_shapes,
        in_specs=[space] * len(args),
        out_specs=jax.tree.map(lambda _: VMEM, out_shapes),
        scratch_shapes=scratch,
        compiler_params=params,
    )(*args)


def shape(dims, dtype):
    return jax.ShapeDtypeStruct(dims, dtype)


def roll(v, by):
    return pltpu.roll(v, by % v.shape[1], 1)


def lanes():
    return lax.broadcasted_iota(jnp.int32, (1, 128), 1)


def within(v, low, high):
    return jnp.where((lanes() >= low) & (lanes() < high), v, 0.0)


def two_rows(v):
    return [v[:, 0:128], jnp.concatenate([v[:, 128:216], jnp.zeros((1, 40), F32)], axis=1)]


def place(two, q):
    lane = lax.broadcasted_iota(jnp.int32, (1, 128), 1)
    row, at = divmod(216 * q, 128)
    one, last = roll(two[0:1], at), roll(jnp.where(lane < 88, two[1:2], 0.0), at)
    gap = jnp.zeros((1, 128), F32)
    pieces = [gap] * row + [
        jnp.where(lane >= at, one, 0.0),
        jnp.where(lane < at, one, 0.0) + jnp.where(lane >= at, last, 0.0),
        jnp.where(lane < at, last, 0.0),
    ]
    return jnp.concatenate((pieces + [gap] * 8)[:8], axis=0)


def take(block, q):
    lane = lax.broadcasted_iota(jnp.int32, (1, 128), 1)
    row, at = divmod(216 * q, 128)
    moved = [roll(block[r : r + 1], -at) for r in range(row, min(row + 3, 8))]
    one = jnp.where(lane < 128 - at, moved[0], moved[1])
    two = jnp.where(lane < 128 - at, moved[1], moved[2]) if len(moved) > 2 else moved[1]
    return jnp.concatenate([one, two], axis=0)


def along_gz():
    return lax.axis_index("y") * 2 + lax.axis_index("core")


def pack(
    cot_hbm, vol_hbm, w2_hbm, f2_hbm, s2_hbm, slab_ref, ahead_ref, out_ref, own_ref,
    cot_ref, vol_ref, w2_ref, f2_ref, s2_ref, cot32, vol32, sems,
):
    copies = [
        pltpu.make_async_copy(source, target, sems.at[i])
        for i, (source, target) in enumerate(
            ((cot_hbm, cot_ref), (vol_hbm, vol_ref), (w2_hbm, w2_ref), (f2_hbm, f2_ref), (s2_hbm, s2_ref))
        )
    ]
    for copy in copies:
        copy.start()
    for copy in copies:
        copy.wait()
    cot32[...] = cot_ref[...].astype(F32)
    vol32[...] = vol_ref[...].astype(F32)
    for x in range(4):
        for y in range(8):
            slab_ref[x, 64 * y : 64 * y + 64, :] = cot32[pl.ds(8 * x + y, 64, stride=32), :].astype(BF16)
        slab_ref[x, 512:544, :] = jnp.concatenate(
            [vol32[pl.ds(8 * x + y, 4, stride=32), :] for y in range(8)], axis=0
        ).astype(BF16)
    ahead_ref[...] = slab_ref[0:2]
    row = lax.broadcasted_iota(jnp.int32, (16, 512), 0)
    lane = lax.broadcasted_iota(jnp.int32, (16, 512), 1)
    pick = ((row < 4) & (lane == row * 128)) | ((row >= 4) & (row < 8) & (lane == row * 128 - 385))
    cells = jnp.concatenate([slab_ref[x] for x in range(4)], axis=1)
    cells = jnp.concatenate([cells, jnp.zeros((96, 512), BF16)], axis=0)
    edge = dot_nt(pick.astype(F32).astype(BF16), cells)
    own = [row for ref in (w2_ref, f2_ref, s2_ref) for row in two_rows(ref[...])]
    own_ref[...] = jnp.concatenate(own + [jnp.zeros((2, 128), F32)], axis=0)
    ends = []
    for side in range(2):
        at = slice(4 * side, 4 * side + 4)
        tail = edge[at, 512:640]
        tail = [sum(roll(tail[x : x + 1], 32 * x) for x in range(4))] + own[0:2] + [jnp.zeros((1, 128), F32)]
        ends.append(jnp.concatenate([edge[at, 128 * j : 128 * j + 128] for j in range(4)] + tail, axis=0))
    me = along_gz()
    for p in range(8):
        message = jnp.where(me < p, ends[1], ends[0]).astype(BF16)
        for x in range(8):
            for j in range(5):
                out_ref[8 * x + p, j] = message[4 * j : 4 * j + 4]


def bank_rows(in_ref, out_ref):
    rows = [in_ref[p, 4].astype(F32)[1:3] for p in range(64)]
    out_ref[...] = jnp.concatenate(rows, axis=0).astype(BF16)


def y_messages(slab_ref, next_ref, in_ref, pb_ref, nb_ref, up_ref, dn_ref, beyond_ref):
    slabs = [slab_ref.at[x] for x in range(4)] + [next_ref.at[x] for x in range(2)]
    first, last = [], []
    for xe, slab in enumerate(slabs):
        up_ref[xe * 64 : xe * 64 + 64, :] = slab[448:512, :]
        dn_ref[xe * 64 : xe * 64 + 64, :] = slab[0:64, :]
        vol = slab[512:544, :].astype(F32)
        first.append(vol[0:4])
        last.append(vol[28:32])
    fill = [jnp.zeros((8, 128), F32)]
    four = [jnp.zeros((4, 128), F32)]
    across, along = lax.axis_index("zl") * 4 + lax.axis_index("x"), along_gz()
    rows_up, rows_dn = [], []
    for side in range(2):
        other = along + 2 * side - 1
        inside = (other >= 0) & (other <= 7)
        other = jnp.clip(other, 0, 7)
        mid = jnp.where(inside, in_ref[8 * across + other].astype(F32), 0.0)
        after = jnp.where(inside, in_ref[8 * ((across + 1) % 8) + other].astype(F32), 0.0)
        parts = [jnp.concatenate([mid[j], after[j, 0:2]], axis=0) for j in range(4)]
        tail = [mid[4, 0:1]] * 4 + [after[4, 0:1]] * 2
        tail = [roll(row, -32 * x) for row, x in zip(tail, (0, 1, 2, 3, 0, 1), strict=True)]
        parts.append(within(jnp.concatenate(tail, axis=0), 0, 32))
        for j in range(5):
            beyond_ref[8 * side : 8 * side + 8, 128 * j : 128 * j + 128] = jnp.concatenate(
                [parts[j], jnp.zeros((2, 128), F32)], axis=0
            )
        rows_up.append(within(roll(parts[3], -64), 0, 64) + within(roll(parts[4], 36), 64, 68))
        rows_dn.append(within(parts[0], 0, 64) + within(roll(parts[4], 64), 64, 68))
    up_ref[384:432, :] = jnp.concatenate(last + fill + rows_up + four, axis=0).astype(BF16)
    dn_ref[384:432, :] = jnp.concatenate(first + fill + rows_dn + four, axis=0).astype(BF16)
    up_ref[432:496, :] = pb_ref[0:64, :]
    dn_ref[432:496, :] = nb_ref[64:128, :]


def assemble(slab_ref, next_ref, beyond_ref, yp_ref, yn_ref, e_ref, ve_ref, keep):
    slabs = [slab_ref.at[x] for x in range(4)] + [next_ref.at[x] for x in range(2)]
    along_y = lax.axis_index("zh")
    some, more = along_y > 0, along_y < 3
    before = jnp.where(some, yp_ref[384:432, :].astype(F32), 0.0)
    after = jnp.where(more, yn_ref[384:432, :].astype(F32), 0.0)
    for xe, slab in enumerate(slabs):
        rows = jnp.concatenate(
            [
                jnp.where(some, yp_ref[xe * 64 : xe * 64 + 64, :].astype(F32), 0.0).astype(BF16),
                slab[0:512, :],
                jnp.where(more, yn_ref[xe * 64 : xe * 64 + 64, :].astype(F32), 0.0).astype(BF16),
            ],
            axis=0,
        )
        for a in range(3):
            x = xe - a
            if 0 <= x < 4:
                value = (rows.astype(F32) * keep).astype(BF16) if (x, a) in PAST else rows
                e_ref[:, 512 * a + 128 * x : 512 * a + 128 * x + 128] = value
        vol = slab[512:544, :].astype(F32)
        ve_ref[xe] = jnp.concatenate(
            [before[xe * 4 : xe * 4 + 4], vol, after[xe * 4 : xe * 4 + 4], jnp.zeros((8, 128), F32)], axis=0
        ).astype(BF16)
    ends = []
    for side in range(2):
        parts = [roll(beyond_ref[8 * side : 8 * side + 6, 128 * j : 128 * j + 128], 64) for j in range(5)]
        prev = before[32 + 6 * side : 38 + 6 * side]
        nxt = after[32 + 6 * side : 38 + 6 * side]
        tiles = [within(prev, 0, 64) + within(parts[0], 64, 128)]
        for k in range(1, 4):
            tiles.append(jnp.where(lanes() < 64, parts[k - 1], parts[k]))
        tiles.append(within(parts[3], 0, 64) + within(roll(nxt, 64), 64, 128))
        tiles.append(
            within(roll(prev, -64), 0, 4) + within(roll(parts[4], -60), 4, 36) + within(roll(nxt, -28), 36, 40)
        )
        ends.append(
            jnp.concatenate([jnp.concatenate(tiles, axis=1), jnp.zeros((10, 768), F32)], axis=0).astype(BF16)
        )
    return ends


def flatten(narrow):
    lane = lax.broadcasted_iota(jnp.int32, (1, 128), 1)
    rows = [jnp.zeros((1, 128), F32) for _ in range(33)]
    for c in range(32):
        row, at = divmod(108 * c, 128)
        moved = roll(jnp.where(lane < 108, narrow[c : c + 1], 0.0), at)
        if at + 108 <= 128:
            rows[row] = rows[row] + moved
        else:
            rows[row] = rows[row] + jnp.where(lane >= at, moved, 0.0)
            rows[row + 1] = rows[row + 1] + jnp.where(lane < at, moved, 0.0)
    return jnp.concatenate(rows[:32], axis=0)


def turned(yp_ref, yn_ref, own_ref, pb_ref, nb_ref, rows_ref):
    me = lax.axis_index("zh")
    for by in range(4):
        zh = (me + by) % 4
        for across in range(8):
            at = pl.multiple_of(64 * across + 16 * zh, 16)
            if by == 2:
                ref, row = (yp_ref if across < 4 else yn_ref), 432 + 16 * (across % 4)
            else:
                ref, row = (own_ref, nb_ref, None, pb_ref)[by], 16 * across
            rows_ref[pl.ds(at, 16), :] = ref[row : row + 16, :].astype(F32)
    parts = []
    for q in range(4):
        parts.append(rows_ref[pl.ds(2 * q, 64, stride=8), :].T)
        parts.append(rows_ref[pl.ds(2 * q + 1, 64, stride=8), :].T[0:88])
    return jnp.concatenate(parts, axis=0).astype(BF16)


def narrow_lanes():
    row = lax.broadcasted_iota(jnp.int32, (512, 128), 0)
    col = lax.broadcasted_iota(jnp.int32, (512, 128), 1)
    group, inner = row // 48, row % 48
    a, c = group // 3, group % 3
    b, i = inner // 4, inner % 4
    return ((b < 3) & (group < 9) & (col == (9 * a + 3 * b + c) * 4 + i)).astype(F32)


def narrow_rows(w1_ref, out_ref, pick_ref):
    lane = lax.broadcasted_iota(jnp.int32, (1, 128), 1)
    rows = []
    for c in range(32):
        row, at = divmod(108 * c, 128)
        piece = roll(w1_ref[row : row + 1, :], -at)
        if at > 20:
            piece = jnp.where(lane < 128 - at, piece, roll(w1_ref[row + 1 : row + 2, :], -at))
        rows.append(jnp.where(lane < 108, piece, 0.0))
    bank = jnp.concatenate(rows, axis=0).astype(BF16)
    pick = narrow_lanes().astype(BF16)
    pick_ref[...] = pick
    first = dot_nt(bank, pick)
    for y in range(8):
        out_ref[32 * y : 32 * y + 32, :] = roll(first, 4 * y).astype(BF16)


def gradients(
    slab_ref, next_ref, beyond_ref, yn_ref, yp_ref, bank_ref, pb_ref, nb_ref, wb_ref, pick_ref, sib_ref,
    keep_ref, send_ref,
    e_ref, ve_ref, ga_ref, rows_ref, wide_ref,
):
    final = (lax.axis_index("zl") == 1) & (lax.axis_index("x") == 3)
    keep = jnp.where(final, 0.0, 1.0)
    ends = assemble(slab_ref, next_ref, beyond_ref, yp_ref, yn_ref, e_ref, ve_ref, keep)
    lane = lax.broadcasted_iota(jnp.int32, (1, 128), 1)
    low, high = lane == 0, lane == 127
    eye = (
        lax.broadcasted_iota(jnp.int32, (48, 128), 0) == lax.broadcasted_iota(jnp.int32, (48, 128), 1)
    ).astype(F32).astype(BF16)
    left = dot_nt(eye, ends[0][:, 640:768])
    right = dot_nt(eye, ends[1][:, 640:768])
    shifted = []
    for xe in range(6):
        v = ve_ref[xe].astype(F32)
        shifted.append(
            (
                jnp.where(low, left[:, xe : xe + 1], roll(v, 1)).astype(BF16),
                ve_ref[xe],
                jnp.where(high, right[:, xe : xe + 1], roll(v, -1)).astype(BF16),
            )
        )
    rest = jnp.zeros((80, 128), BF16)
    patches = jnp.concatenate(
        [
            jnp.concatenate(
                [
                    (shifted[x + a][c].astype(F32) * keep).astype(BF16) if (x, a) in PAST else shifted[x + a][c]
                    for a in range(3)
                    for c in range(3)
                ]
                + [rest],
                axis=0,
            )
            for x in range(4)
        ],
        axis=1,
    )
    pre = dot(wb_ref[...], patches)
    sig = 1.0 / (1.0 + jnp.exp(-pre))
    act = (pre * sig).astype(BF16)
    slope = sig * (1.0 + pre * (1.0 - sig))
    halos = []
    for end in ends:
        m = end[:, 0:640].astype(F32)
        by_a = []
        for a in range(3):
            rows = m[a : a + 4]
            if a != 1:
                row = lax.broadcasted_iota(jnp.int32, (4, 1), 0)
                rows = rows * jnp.where(row == (3 if a == 0 else 2), keep, 1.0)
            by_a.append(rows)
        halos.append(
            jnp.concatenate(
                [
                    jnp.concatenate([rows[:, 128 * k : 128 * k + 256] for rows in by_a], axis=1)
                    for k in range(4)
                ],
                axis=0,
            ).astype(BF16)
        )
    none = jnp.zeros((32, 64), BF16)
    weights = turned(yp_ref, yn_ref, bank_ref, pb_ref, nb_ref, rows_ref)
    blocks = []
    for c in range(3):
        for yl in range(2):
            cells = []
            for a in range(3):
                for yp in range(4):
                    b = yp - yl
                    if 0 <= b <= 2:
                        tap = (2 - a) * 9 + (2 - b) * 3 + (2 - c)
                        cells.append(weights[tap * 32 : tap * 32 + 32])
                    else:
                        cells.append(none)
            blocks.append(jnp.concatenate(cells, axis=1))
    bank = jnp.concatenate(blocks, axis=0)
    from_left = dot_nt(bank[0:64], halos[0])
    from_right = dot_nt(bank[128:192], halos[1])
    for k in range(4):
        for xp in range(2):
            v = sum(
                dot(
                    bank[:, 256 * a : 256 * a + 256],
                    e_ref[128 * k : 128 * k + 256, 512 * a + 256 * xp : 512 * a + 256 * xp + 256],
                )
                for a in range(3)
            )
            for j in range(2):
                x = 2 * xp + j
                at = slice(128 * j, 128 * j + 128)
                col = 4 * k + x
                ga_ref[64 * k : 64 * k + 64, 128 * x : 128 * x + 128] = (
                    v[64:128, at]
                    + jnp.where(low, from_left[:, col : col + 1], roll(v[0:64, at], 1))
                    + jnp.where(high, from_right[:, col : col + 1], roll(v[128:192, at], -1))
                )
    grad_pre = (ga_ref[...] * slope).astype(BF16)
    product = dot_nt(grad_pre, patches)
    total = product[0:32]
    for y in range(1, 8):
        total = total + roll(product[32 * y : 32 * y + 32], -4 * y)
    split, rest = [], total
    for _ in range(3):
        split.append(rest.astype(BF16))
        rest = rest - split[-1].astype(F32)
    picked = dot(jnp.concatenate(split, axis=0), pick_ref[...])
    narrow = picked[0:32] + (picked[32:64] + picked[64:96])
    act32 = act.astype(F32)
    before, after = [], []
    for x in range(4):
        part = act32[:, 128 * x : 128 * x + 128]
        before.append(jnp.where(low, 0.0, roll(part, 1)).astype(BF16))
        after.append(jnp.where(high, 0.0, roll(part, -1)).astype(BF16))
    before = jnp.concatenate(before, axis=1)
    after = jnp.concatenate(after, axis=1)
    empty = jnp.zeros((32, 512), BF16)
    rows = []
    for k in range(4):
        parts = []
        for yl in range(2):
            at = slice(64 * k + 32 * yl, 64 * k + 32 * yl + 32)
            parts += [before[at], act[at], after[at], empty]
        rows.append(jnp.concatenate(parts, axis=0))
    wide = jnp.concatenate(
        [
            sum(
                dot_nt(e_ref[128 * k : 128 * k + 256, 512 * a : 512 * a + 512], rows[k])
                for k in range(4)
            )
            for a in range(3)
        ],
        axis=0,
    )
    row = lax.broadcasted_iota(jnp.int32, (16, 512), 0)
    lanes = lax.broadcasted_iota(jnp.int32, (16, 512), 1)
    pick = ((row < 4) & (lanes == row * 128)) | ((row >= 4) & (row < 8) & (lanes == (row - 4) * 128 + 127))
    edges = dot_nt(pick.astype(F32).astype(BF16), act)
    gap = jnp.zeros((4, 64), F32)
    one = jnp.zeros((4, 32), F32)
    table = []
    for k in range(4):
        e0 = edges[0:4, 64 * k : 64 * k + 32]
        e1 = edges[0:4, 64 * k + 32 : 64 * k + 64]
        table.append(jnp.concatenate([gap, e0, one, gap, e1, one], axis=1))
    for k in range(4):
        e0 = edges[4:8, 64 * k : 64 * k + 32]
        e1 = edges[4:8, 64 * k + 32 : 64 * k + 64]
        table.append(jnp.concatenate([e0, one, gap, e1, one, gap], axis=1))
    table = jnp.concatenate(table, axis=0).astype(BF16)
    wide = wide + dot_tn(jnp.concatenate(halos, axis=0), table)
    taps = []
    for a in range(3):
        for b in range(3):
            at = (2 - a) * 256 + (2 - b) * 64
            taps.append((wide[at : at + 64, 0:128] + wide[at + 64 : at + 128, 128:256])[:, 0:96])
    wide = jnp.concatenate(taps + [jnp.zeros((64, 32), F32)], axis=1)
    flat = flatten(narrow)
    for j in range(7):
        wide_ref[64 * j : 64 * j + 64, :] = wide[:, 128 * j : 128 * j + 128]
    core = lax.axis_index("core")
    parts = [flat[0:14], flat[14:28]]
    mine = jnp.where(core == 0, parts[0], parts[1])
    others = jnp.where(core == 0, parts[1], parts[0])
    for p in range(8):
        zl, zh = p // 4, p % 4
        for ref, yh, part in ((keep_ref, core, mine), (send_ref, 1 - core, others)):
            for j in range(7):
                ref[p, 4 * j : 4 * j + 4, :] = wide_ref[pl.ds(64 * j + 32 * zl + 2 * zh + yh, 4, stride=8), :]
            ref[p, 28:42, :] = part


def first_stage(a_ref, b_ref, out_ref):
    out_ref[...] = a_ref[...] + b_ref[...]


def second_stage(in_ref, out_ref):
    total = in_ref[0]
    for p in range(1, 8):
        total = total + in_ref[p]
    for x in range(4):
        block = [total[4 * j + x : 4 * j + x + 1] for j in range(7)]
        rows = jnp.concatenate(block + [total[28:42]], axis=0)
        for y in range(4):
            out_ref[4 * x + y] = rows


def third_stage(in_ref, own_ref, sib_ref, out_ref):
    total = in_ref[0]
    for p in range(1, 16):
        total = total + in_ref[p]
    gap = [jnp.zeros((1, 128), F32)]
    out_ref[0:24, :] = jnp.concatenate([total[0:7]] + gap + [total[7:21]] + gap + gap, axis=0)
    even = lax.axis_index("y") % 2 == 0
    own, sib = own_ref[...], sib_ref[...]
    out_ref[24:32, :] = jnp.where(even, own, sib)
    out_ref[32:40, :] = jnp.where(even, sib, own)


def moments(master, first, second, grad):
    first_new = 0.9 * first + 0.1 * grad
    second_new = 0.999 * second + 0.001 * grad * grad
    direction = (
        first_new / (1.0 - 0.9**10) / (jnp.sqrt(second_new / (1.0 - 0.999**10)) + 1e-06)
        + 0.01 * master
    )
    return (first_new, second_new, direction)


def runs():
    row = lax.broadcasted_iota(jnp.int32, (27, 128), 0)
    lane = lax.broadcasted_iota(jnp.int32, (27, 128), 1)
    start = (row * 128) // 108
    run = (row * 128 + lane) // 108
    return [(run == start + p, lane == start + p) for p in range(3)]


def run_sums(value):
    total = jnp.zeros((27, 128), F32)
    for inside, column in runs():
        part = jnp.sum(jnp.where(inside, value, 0.0), axis=1, keepdims=True)
        total = total + jnp.where(column, part, 0.0)
    return jnp.sum(total, axis=0, keepdims=True)


def run_spread(value):
    total = jnp.zeros((27, 128), F32)
    for inside, column in runs():
        part = jnp.sum(jnp.where(column, value, 0.0), axis=1, keepdims=True)
        total = total + jnp.where(inside, part, 0.0)
    return total


def update(in_ref, other_ref, own_ref, m_ref, f_ref, s_ref, w2_ref, f2_ref, s2_ref, w1_ref, f1_ref, s1_ref):
    y, core = lax.axis_index("y"), lax.axis_index("core")
    quarter = y % 2 * 2 + core
    mine, other = in_ref[...], other_ref[...]
    low, high = jnp.where(core == 0, mine, other), jnp.where(core == 0, other, mine)
    grad = jnp.where(y // 2 == 0, low[0:8], high[0:8])
    inside = (
        lax.broadcasted_iota(jnp.int32, (8, 128), 0) * 128 + lax.broadcasted_iota(jnp.int32, (8, 128), 1)
    ) < 864
    block = []
    for j in range(3):
        parts = [half[at + 2 * j : at + 2 * j + 2] for at in (24, 32) for half in (low, high)]
        block.append(sum(place(part, q) for q, part in enumerate(parts)))
    _, _, direction = moments(block[0], block[1], block[2], grad)
    direction = jnp.where(inside, direction, 0.0)
    ratio = jnp.sqrt(jnp.sum(block[0] * block[0], keepdims=True)) / (
        jnp.sqrt(jnp.sum(direction * direction, keepdims=True)) + 1e-06
    )
    mine = take(grad, 0)
    for q in range(1, 4):
        mine = jnp.where(quarter == q, take(grad, q), mine)
    master, first, second = (own_ref[2 * j : 2 * j + 2] for j in range(3))
    first_new, second_new, direction = moments(master, first, second, mine)
    for ref, value in (
        (w2_ref, master - 0.01 * (ratio * direction)),
        (f2_ref, first_new),
        (s2_ref, second_new),
    ):
        ref[...] = jnp.concatenate([value[0:1], value[1:2, 0:88]], axis=1)
    grad = jnp.concatenate([low[8:22], high[8:22]], axis=0)[0:27]
    master = m_ref[...]
    first_new, second_new, direction = moments(master, f_ref[...], s_ref[...], grad)
    ratio = jnp.sqrt(run_sums(master * master)) / (jnp.sqrt(run_sums(direction * direction)) + 1e-06)
    w1_ref[...] = master - 0.01 * (run_spread(ratio) * direction)
    f1_ref[...] = first_new
    s1_ref[...] = second_new


def turn(value, by):
    return lax.ppermute(value, GY, [(i, (i + by) % 4) for i in range(4)])


def swap(value):
    return lax.ppermute(value, "core", [(0, 1), (1, 0)])


def local(volume, cotangent, w1_master, w1_first, w1_second, w2_master, w2_first, w2_second):
    wide = [w.reshape(1, 216) for w in (w2_master, w2_first, w2_second)]
    narrow = [w.reshape(27, 128) for w in (w1_master, w1_first, w1_second)]
    narrow_band, pick = call(narrow_rows, (shape((256, 512), BF16), shape((512, 128), BF16)), narrow[0])
    along_y = shape((496, 128), BF16)
    slabs, ahead, message, own = call(
        pack,
        (shape((4, 544, 128), BF16), shape((2, 544, 128), BF16), shape((64, 5, 4, 128), BF16), shape((8, 128), F32)),
        cotangent.reshape(2048, 128),
        volume.reshape(128, 128),
        *wide,
        scratch=(
            pltpu.VMEM((2048, 128), BF16),
            pltpu.VMEM((128, 128), BF16),
            pltpu.VMEM((1, 216), F32),
            pltpu.VMEM((1, 216), F32),
            pltpu.VMEM((1, 216), F32),
            pltpu.VMEM((2048, 128), F32),
            pltpu.VMEM((128, 128), F32),
            pltpu.SemaphoreType.DMA((5,)),
        ),
        space=pl.BlockSpec(memory_space=pltpu.HBM),
        params=pltpu.CompilerParams(vmem_limit_bytes=60 * 1024 * 1024),
    )
    next_x = lax.ppermute(ahead, GX, [(i, (i + 7) % 8) for i in range(8)])
    sibling = lax.ppermute(own, "y", [(0, 1), (1, 0), (2, 3), (3, 2)])
    message = lax.all_to_all(message, GX + GZ, 0, 0, tiled=True)
    bank = call(bank_rows, shape((128, 128), BF16), message)
    near_banks = turn(bank, 1), turn(bank, 3)
    up, down, beyond = call(
        y_messages, (along_y, along_y, shape((16, 640), F32)), slabs, next_x, message, *near_banks
    )
    before_y, after_y = turn(up, 1), turn(down, 3)
    keep, send = call(
        gradients,
        (shape((8, 42, 128), F32), shape((8, 42, 128), F32)),
        slabs,
        next_x,
        beyond,
        after_y,
        before_y,
        bank,
        *near_banks,
        narrow_band,
        pick,
        sibling,
        scratch=(
            pltpu.VMEM((640, 1536), BF16),
            pltpu.VMEM((6, 48, 128), BF16),
            pltpu.VMEM((256, 512), F32),
            pltpu.VMEM((512, 128), F32),
            pltpu.VMEM((448, 128), F32),
        ),
    )
    sums = call(first_stage, shape((8, 42, 128), F32), keep, swap(send))
    sums = lax.all_to_all(sums, ("zl", "zh"), 0, 0, tiled=True)
    sums = call(second_stage, shape((16, 21, 128), F32), sums)
    sums = lax.all_to_all(sums, ("x", "y"), 0, 0, tiled=True)
    half = call(third_stage, shape((40, 128), F32), sums, own, sibling)
    one, rows = shape((1, 216), F32), shape((27, 128), F32)
    new = call(update, (one, one, one, rows, rows, rows), half, swap(half), own, *narrow)
    return tuple(w.reshape(-1) for w in new[3:] + new[:3])


def solution(mesh):
    parts = Mesh(mesh.devices.reshape(2, 4, 4, 4, 2), GX + GY + GZ)
    field = P(None, GX, GY, GZ)
    owned = P(GX + GY + GZ)
    return jax.shard_map(
        local,
        mesh=parts,
        in_specs=(field, field, P(), P(), P(), owned, owned, owned),
        out_specs=(P(), P(), P(), owned, owned, owned),
        check_vma=False,
    )
```
